32 devices in a mesh: slab: 16 (over z, y, x), tile: 2 (over core).
Axes of the slice: x: 2, y: 2, z: 4, core: 2. Of those that a mesh axis runs over, the one named last changes fastest.
Arguments:
- field: float32 [256, 256, 1024], P('slab', None, 'tile'), may hold values from -1 to 1
- tf_emission: float32 [3, 16], replicated, may hold values from 0 to 1
- tf_absorption: float32 [3, 16], replicated, may hold values from 0.05 to 1
Outputs:
- colour: float32 [3, 256, 1024], P(None, 'slab', 'tile')
- opacity: float32 [3, 256, 1024], P(None, 'slab', 'tile')
The draws below stay inside these ranges and needn't reach their ends.
All inputs are finite; a program needn't handle non-finite values.
Results may differ from the reference program's by a relative error of at most 0.0003.
Values sent between devices are 32-bit elements; how exact they have to be, the bound alone decides.
No kernel may reach another device: no remote copies, remote signals or barrier semaphores. Data moves between devices by JAX's collectives and lax.ppermute only.
A program may use at most 128 MiB of HBM per device.

```python
import math
import jax
import jax.numpy as jnp
from jax import lax

NY = 256
BREAKS = 16
NZ = 256
NX = 1024


def shard_levels(key, dims, pieces, smallest, high):
    loudness = 1.0
    for axis_at, parts in pieces:
        draws = jax.random.uniform(jax.random.fold_in(jax.random.fold_in(key, 6), axis_at), (parts,), jnp.float32, smallest / len(pieces), high / len(pieces))
        loudness = loudness * jnp.repeat(jnp.exp(draws), dims[axis_at] // parts).reshape((-1,) + (1,) * (len(dims) - 1 - axis_at))
    return loudness


def setup_inputs(seed: int = 0) -> dict:
    keys = jax.random.split(jax.random.key(seed), 4)
    field = jnp.clip(jax.random.uniform(keys[0], (NZ, NY, NX), jnp.float32, -1.0, 1.0) * shard_levels(keys[0], (NZ, NY, NX), ((0, 16), (2, 2)), -0.4, 0.0), -1.0, 1.0)
    tf_emission = jnp.clip(jax.random.uniform(keys[1], (3, BREAKS), jnp.float32, 0.0, 1.0), 0.0, 1.0)
    tf_absorption = jnp.clip(jnp.exp(jax.random.uniform(keys[2], (3, BREAKS), jnp.float32, math.log(0.05), math.log(1.0))), 0.05, 1.0)
    return dict(field=field, tf_emission=tf_emission, tf_absorption=tf_absorption)


LIGHT_DIR = (0.2672612, 0.5345225, 0.8017837)

def lookup_table(table, interval, fraction):
    count_breaks = table.shape[1]
    result = jnp.zeros((3,) + fraction.shape, jnp.float32)
    for k in range(count_breaks - 1):
        value = table[:, k][:, None, None] + fraction[None] * (table[:, k + 1] - table[:, k])[:, None, None]
        result = jnp.where((interval == k)[None], value, result)
    return result

def shade_plane(lower_plane, middle, upper_plane, tf_emission, tf_absorption, depth_total):
    centre = middle[:, 1:-1]
    grad_x = 0.5 * (middle[:, 2:] - middle[:, :-2])
    padded_rows = jnp.pad(centre, ((1, 1), (0, 0)))
    grad_y = 0.5 * (padded_rows[2:] - padded_rows[:-2])
    grad_z = 0.5 * (upper_plane[:, 1:-1] - lower_plane[:, 1:-1])
    squared = grad_x * grad_x + grad_y * grad_y + grad_z * grad_z
    facing = (LIGHT_DIR[0] * grad_x + LIGHT_DIR[1] * grad_y + LIGHT_DIR[2] * grad_z) * lax.rsqrt(squared + 0.25)
    shading = 0.1 + 0.9 * jnp.maximum(facing, 0.0)
    steepness = squared / (squared + 0.25)
    count_breaks = tf_emission.shape[1]
    scaled = (centre + 1.0) * (0.5 * (count_breaks - 1))
    lowest = jnp.clip(jnp.floor(scaled), 0.0, count_breaks - 2.0)
    fraction = scaled - lowest
    interval = lowest.astype(jnp.int32)
    emission = lookup_table(tf_emission, interval, fraction)
    absorption = lookup_table(tf_absorption, interval, fraction)
    opacity_step = absorption * (4.0 / depth_total) * (0.25 + 0.75 * steepness)[None]
    sample = emission * shading[None] * opacity_step
    return (sample, opacity_step)

def reference(field, tf_emission, tf_absorption):
    depth_total = field.shape[0]

    def widen(plane_data):
        return jnp.pad(plane_data, ((0, 0), (1, 1)))

    def march(plane, running):
        colour, transmit = running
        middle = lax.dynamic_index_in_dim(field, plane, 0, keepdims=False)
        lower_plane = lax.dynamic_index_in_dim(field, jnp.maximum(plane - 1, 0), 0, keepdims=False)
        lower_plane = lower_plane * (plane > 0).astype(field.dtype)
        upper_plane = lax.dynamic_index_in_dim(field, jnp.minimum(plane + 1, depth_total - 1), 0, keepdims=False)
        upper_plane = upper_plane * (plane < depth_total - 1).astype(field.dtype)
        sample, opacity_step = shade_plane(widen(lower_plane), widen(middle), widen(upper_plane), tf_emission, tf_absorption, depth_total)
        return (colour + transmit * sample, transmit * (1.0 - opacity_step))
    start = (jnp.zeros((3,) + field.shape[1:], field.dtype), jnp.ones((3,) + field.shape[1:], field.dtype))
    colour, transmit = lax.fori_loop(0, depth_total, march, start)
    return (colour, 1.0 - transmit)
```

```python
import functools

import jax
import jax.numpy as jnp
from jax import lax
from jax.experimental import pallas as pl
from jax.experimental.pallas import tpu as pltpu
from jax.sharding import PartitionSpec as P

LIGHT_DIR = (0.2672612, 0.5345225, 0.8017837)
LANES = 128
SUBLANES = 8
PAD = 8


def segment_tables(tf_emission, tf_absorption, depth_total):
    count_breaks = tf_emission.shape[1]
    scale = 0.5 * (count_breaks - 1)
    tables = jnp.concatenate([tf_emission, tf_absorption * (4.0 / depth_total)], axis=0)
    rise = tables[:, 1:] - tables[:, :-1]
    knots = jnp.arange(count_breaks - 1, dtype=jnp.float32)
    intercept = tables[:, :-1] + rise * (scale - knots)
    slope = rise * scale
    both = jnp.concatenate([intercept, slope], axis=0)
    both = jnp.concatenate([both, both[:, -1:]], axis=1)
    both = jnp.pad(both, ((0, 0), (0, LANES - count_breaks)))
    return jnp.broadcast_to(both[:, None, :], (12, SUBLANES, LANES))


def lookup(table, index):
    return jnp.take_along_axis(table, index, axis=1, mode="promise_in_bounds")


def march_kernel(
    scale, tables, field, low, high, edges, image, cells, canvas, in_sems, out_sems
):
    planes, height, width = field.shape
    tiles = width // LANES
    stride = height // SUBLANES
    body_rows = pl.ds(PAD, height)

    def columns(tile):
        return pl.ds(tile * LANES, LANES)

    def incoming(slot):
        if slot in (0, tiles + 1):
            return [
                pltpu.make_async_copy(
                    edges, cells.at[slot, pl.ds(1, planes), body_rows, :], in_sems.at[slot, 0]
                )
            ]
        here = columns(slot - 1)
        return [
            pltpu.make_async_copy(
                field.at[:, :, here],
                cells.at[slot, pl.ds(1, planes), body_rows, :],
                in_sems.at[slot, 0],
            ),
            pltpu.make_async_copy(
                low.at[:, here], cells.at[slot, 0, body_rows, :], in_sems.at[slot, 1]
            ),
            pltpu.make_async_copy(
                high.at[:, here], cells.at[slot, planes + 1, body_rows, :], in_sems.at[slot, 2]
            ),
        ]

    def outgoing(tile):
        return pltpu.make_async_copy(
            canvas.at[tile], image.at[:, :, columns(tile)], out_sems.at[tile]
        )

    for slot in range(tiles + 2):
        for copy in incoming(slot):
            copy.start()
    zeros = jnp.zeros((planes, 1, LANES), jnp.float32)
    for slot in range(1, tiles + 1):
        cells[slot, pl.ds(1, planes), pl.ds(PAD - 1, 1), :] = zeros
        cells[slot, pl.ds(1, planes), pl.ds(PAD + height, 1), :] = zeros
    lane = lax.broadcasted_iota(jnp.int32, (SUBLANES, LANES), 1)
    first_lane = lane == 0
    last_lane = lane == LANES - 1

    def strip(slot, row):
        def rows(part, plane, offset):
            return cells[part, plane, pl.ds(PAD + row + offset, SUBLANES, stride=stride), :]

        table = [tables[k] for k in range(12)]
        colour = [None] * 3
        transmit = [None] * 3
        before = rows(slot, 0, 0)
        centre = rows(slot, 1, 0)
        for plane in range(1, planes + 1):
            after = rows(slot, plane + 1, 0)
            left = pltpu.roll(jnp.where(last_lane, rows(slot - 1, plane, 0), centre), 1, 1)
            right = pltpu.roll(
                jnp.where(first_lane, rows(slot + 1, plane, 0), centre), LANES - 1, 1
            )
            diff_x = right - left
            diff_y = rows(slot, plane, 1) - rows(slot, plane, -1)
            diff_z = after - before
            inverse = lax.rsqrt(diff_x * diff_x + diff_y * diff_y + diff_z * diff_z + 1.0)
            facing = (
                (0.9 * LIGHT_DIR[0]) * diff_x
                + (0.9 * LIGHT_DIR[1]) * diff_y
                + (0.9 * LIGHT_DIR[2]) * diff_z
            ) * inverse
            shading = jnp.maximum(facing, 0.0) + 0.1
            weight = 1.0 - 0.75 * (inverse * inverse)
            interval = (centre * scale + scale).astype(jnp.int32)
            values = [
                lookup(table[k], interval) + lookup(table[k + 6], interval) * centre
                for k in range(6)
            ]
            for ch in range(3):
                step = values[3 + ch] * weight
                glow = values[ch] * shading
                if plane == 1:
                    colour[ch] = step * glow
                    transmit[ch] = 1.0 - step
                else:
                    seen = transmit[ch] * step
                    colour[ch] = colour[ch] + seen * glow
                    transmit[ch] = transmit[ch] - seen
            before, centre = centre, after
        for ch in range(3):
            target = pl.ds(row, SUBLANES, stride=stride)
            canvas[slot - 1, ch, target, :] = colour[ch]
            canvas[slot - 1, 3 + ch, target, :] = transmit[ch]

    for copy in incoming(0) + incoming(1):
        copy.wait()
    for slot in range(1, tiles + 1):
        for copy in incoming(slot + 1):
            copy.wait()

        @pl.loop(0, stride)
        def _(row):
            strip(slot, row)

        outgoing(slot - 1).start()
    for tile in range(tiles):
        outgoing(tile).wait()


def march(tables, field, low, high, edges, count_breaks):
    planes, height, width = field.shape
    tiles = width // LANES
    anywhere = pl.BlockSpec(memory_space=pl.ANY)
    return pl.pallas_call(
        functools.partial(march_kernel, 0.5 * (count_breaks - 1)),
        out_shape=jax.ShapeDtypeStruct((6, height, width), jnp.float32),
        in_specs=[pl.BlockSpec(memory_space=pltpu.VMEM)] + [anywhere] * 4,
        out_specs=anywhere,
        scratch_shapes=[
            pltpu.VMEM((tiles + 2, planes + 2, height + 2 * PAD, LANES), jnp.float32),
            pltpu.VMEM((tiles, 6, height, LANES), jnp.float32),
            pltpu.SemaphoreType.DMA((tiles + 2, 3)),
            pltpu.SemaphoreType.DMA((tiles,)),
        ],
        compiler_params=pltpu.CompilerParams(vmem_limit_bytes=40 * 1024 * 1024),
        cost_estimate=pl.CostEstimate(
            flops=planes * height * width * 80,
            bytes_accessed=planes * height * width * 5,
            transcendentals=0,
        ),
    )(tables, field, low, high, edges)


def neighbours(first, last, axis):
    count = lax.axis_size(axis)
    forward = [(i, i + 1) for i in range(count - 1)]
    backward = [(i + 1, i) for i in range(count - 1)]
    return lax.ppermute(last, axis, forward), lax.ppermute(first, axis, backward)


def over(near, far):
    return (
        [near[0] + near[1] * far[0], near[1] * far[1]]
    )


def ordered(is_far, own, other):
    near = [jnp.where(is_far, b, a) for a, b in zip(own, other)]
    far = [jnp.where(is_far, a, b) for a, b in zip(own, other)]
    return over(near, far)


def exchange(image, slab_index, shift, bits):
    size = 1 << bits
    count = lax.axis_size("slab")
    own = (slab_index >> shift) & (size - 1)
    parts = []
    for change in range(size):
        part = lax.dynamic_index_in_dim(image, own ^ change, 2, keepdims=False)
        if change:
            part = lax.ppermute(part, "slab", [(i, i ^ change << shift) for i in range(count)])
        parts.append([part[:3], part[3:]])
    for digit in range(bits):
        is_far = (own >> digit & 1) == 1
        parts = [ordered(is_far, parts[k], parts[k + 1]) for k in range(0, len(parts), 2)]
    return parts[0]


def per_device(field, tf_emission, tf_absorption):
    slab_count = lax.axis_size("slab")
    planes, height, width = field.shape
    low, high = neighbours(field[0], field[-1], "slab")
    left, right = neighbours(field[:, :, 0], field[:, :, -1], "tile")
    edge_lane = lax.broadcasted_iota(jnp.int32, (1, 1, LANES), 2) == 0
    edges = jnp.where(edge_lane, right[:, :, None], left[:, :, None])
    tables = segment_tables(tf_emission, tf_absorption, planes * slab_count)
    image = march(tables, field, low, high, edges, tf_emission.shape[1])
    levels = slab_count.bit_length() - 1
    block_rows = height // slab_count
    slab_index = lax.axis_index("slab")
    for shift in range(0, levels, 2):
        bits = min(2, levels - shift)
        outer = slab_count >> (shift + bits)
        image = image.reshape((6, outer, 1 << bits, block_rows, width))
        pair = exchange(image, slab_index, shift, bits)
        if outer > 1:
            image = jnp.concatenate(pair, axis=0)
    colour, transmit = (part.reshape((3, block_rows, width)) for part in pair)
    return colour, 1.0 - transmit


def solution(mesh):
    placed = (P("slab", None, "tile"), P(), P())
    return jax.shard_map(
        per_device,
        mesh=mesh,
        in_specs=placed,
        out_specs=(P(None, "slab", "tile"), P(None, "slab", "tile")),
        check_vma=False,
    )
```

```python
import functools

import jax
import jax.numpy as jnp
from jax import lax
from jax.experimental import pallas as pl
from jax.experimental.pallas import tpu as pltpu
from jax.sharding import PartitionSpec as P

LIGHT_DIR = (0.2672612, 0.5345225, 0.8017837)
LANES = 128
SUBLANES = 8
PAD = 8


def segment_tables(tf_emission, tf_absorption, depth_total):
    count_breaks = tf_emission.shape[1]
    scale = 0.5 * (count_breaks - 1)
    tables = jnp.concatenate([tf_emission, tf_absorption * (4.0 / depth_total)], axis=0)
    rise = tables[:, 1:] - tables[:, :-1]
    knots = jnp.arange(count_breaks - 1, dtype=jnp.float32)
    intercept = tables[:, :-1] + rise * (scale - knots)
    slope = rise * scale
    both = jnp.concatenate([intercept, slope], axis=0)
    both = jnp.concatenate([both, both[:, -1:]], axis=1)
    both = jnp.pad(both, ((0, 0), (0, LANES - count_breaks)))
    return jnp.broadcast_to(both[:, None, :], (12, SUBLANES, LANES))


def lookup(table, index):
    return jnp.take_along_axis(table, index, axis=1, mode="promise_in_bounds")


def march_kernel(
    scale, tables, field, low, high, edges, image, cells, canvas, in_sems, out_sems
):
    planes, height, width = field.shape
    tiles = width // LANES
    strips = height // SUBLANES
    body_rows = pl.ds(PAD, height)

    def columns(tile):
        return pl.ds(tile * LANES, LANES)

    def incoming(slot):
        if slot in (0, tiles + 1):
            return [
                pltpu.make_async_copy(
                    edges, cells.at[slot, pl.ds(1, planes), body_rows, :], in_sems.at[slot, 0]
                )
            ]
        here = columns(slot - 1)
        return [
            pltpu.make_async_copy(
                field.at[:, :, here],
                cells.at[slot, pl.ds(1, planes), body_rows, :],
                in_sems.at[slot, 0],
            ),
            pltpu.make_async_copy(
                low.at[:, here], cells.at[slot, 0, body_rows, :], in_sems.at[slot, 1]
            ),
            pltpu.make_async_copy(
                high.at[:, here], cells.at[slot, planes + 1, body_rows, :], in_sems.at[slot, 2]
            ),
        ]

    def outgoing(tile):
        return pltpu.make_async_copy(
            canvas.at[tile], image.at[:, :, columns(tile)], out_sems.at[tile]
        )

    for slot in range(tiles + 2):
        for copy in incoming(slot):
            copy.start()
    zeros = jnp.zeros((planes, 1, LANES), jnp.float32)
    for slot in range(1, tiles + 1):
        cells[slot, pl.ds(1, planes), pl.ds(PAD - 1, 1), :] = zeros
        cells[slot, pl.ds(1, planes), pl.ds(PAD + height, 1), :] = zeros
    lane = lax.broadcasted_iota(jnp.int32, (SUBLANES, LANES), 1)
    first_lane = lane == 0
    last_lane = lane == LANES - 1

    def strip(slot, row):
        def rows(part, plane, offset):
            return cells[part, plane, pl.ds(PAD + row * SUBLANES + offset, SUBLANES), :]

        table = [tables[k] for k in range(12)]
        colour = [None] * 3
        transmit = [None] * 3
        before = rows(slot, 0, 0)
        centre = rows(slot, 1, 0)
        for plane in range(1, planes + 1):
            after = rows(slot, plane + 1, 0)
            left = pltpu.roll(jnp.where(last_lane, rows(slot - 1, plane, 0), centre), 1, 1)
            right = pltpu.roll(
                jnp.where(first_lane, rows(slot + 1, plane, 0), centre), LANES - 1, 1
            )
            diff_x = right - left
            diff_y = rows(slot, plane, 1) - rows(slot, plane, -1)
            diff_z = after - before
            inverse = lax.rsqrt(diff_x * diff_x + diff_y * diff_y + diff_z * diff_z + 1.0)
            facing = (
                (0.9 * LIGHT_DIR[0]) * diff_x
                + (0.9 * LIGHT_DIR[1]) * diff_y
                + (0.9 * LIGHT_DIR[2]) * diff_z
            ) * inverse
            shading = jnp.maximum(facing, 0.0) + 0.1
            weight = 1.0 - 0.75 * (inverse * inverse)
            interval = (centre * scale + scale).astype(jnp.int32)
            values = [
                lookup(table[k], interval) + lookup(table[k + 6], interval) * centre
                for k in range(6)
            ]
            for ch in range(3):
                step = values[3 + ch] * weight
                glow = values[ch] * shading
                if plane == 1:
                    colour[ch] = step * glow
                    transmit[ch] = 1.0 - step
                else:
                    seen = transmit[ch] * step
                    colour[ch] = colour[ch] + seen * glow
                    transmit[ch] = transmit[ch] - seen
            before, centre = centre, after
        for ch in range(3):
            target = pl.ds(row * SUBLANES, SUBLANES)
            canvas[slot - 1, ch, target, :] = colour[ch]
            canvas[slot - 1, 3 + ch, target, :] = transmit[ch]

    for copy in incoming(0) + incoming(1):
        copy.wait()
    for slot in range(1, tiles + 1):
        for copy in incoming(slot + 1):
            copy.wait()

        @pl.loop(0, strips)
        def _(row):
            strip(slot, row)

        outgoing(slot - 1).start()
    for tile in range(tiles):
        outgoing(tile).wait()


def march(tables, field, low, high, edges, count_breaks):
    planes, height, width = field.shape
    tiles = width // LANES
    anywhere = pl.BlockSpec(memory_space=pl.ANY)
    return pl.pallas_call(
        functools.partial(march_kernel, 0.5 * (count_breaks - 1)),
        out_shape=jax.ShapeDtypeStruct((6, height, width), jnp.float32),
        in_specs=[pl.BlockSpec(memory_space=pltpu.VMEM)] + [anywhere] * 4,
        out_specs=anywhere,
        scratch_shapes=[
            pltpu.VMEM((tiles + 2, planes + 2, height + 2 * PAD, LANES), jnp.float32),
            pltpu.VMEM((tiles, 6, height, LANES), jnp.float32),
            pltpu.SemaphoreType.DMA((tiles + 2, 3)),
            pltpu.SemaphoreType.DMA((tiles,)),
        ],
        compiler_params=pltpu.CompilerParams(vmem_limit_bytes=40 * 1024 * 1024),
        cost_estimate=pl.CostEstimate(
            flops=planes * height * width * 80,
            bytes_accessed=planes * height * width * 5,
            transcendentals=0,
        ),
    )(tables, field, low, high, edges)


def neighbours(first, last, axis):
    count = lax.axis_size(axis)
    forward = [(i, i + 1) for i in range(count - 1)]
    backward = [(i + 1, i) for i in range(count - 1)]
    return lax.ppermute(last, axis, forward), lax.ppermute(first, axis, backward)


def over(near, far):
    return (
        [near[0] + near[1] * far[0], near[1] * far[1]]
    )


def ordered(is_far, own, other):
    near = [jnp.where(is_far, b, a) for a, b in zip(own, other)]
    far = [jnp.where(is_far, a, b) for a, b in zip(own, other)]
    return over(near, far)


def exchange(image, slab_index, shift, bits):
    size = 1 << bits
    count = lax.axis_size("slab")
    own = (slab_index >> shift) & (size - 1)
    parts = []
    for change in range(size):
        part = lax.dynamic_index_in_dim(image, own ^ change, 2, keepdims=False)
        if change:
            part = lax.ppermute(part, "slab", [(i, i ^ change << shift) for i in range(count)])
        parts.append([part[:3], part[3:]])
    for digit in range(bits):
        is_far = (own >> digit & 1) == 1
        parts = [ordered(is_far, parts[k], parts[k + 1]) for k in range(0, len(parts), 2)]
    return parts[0]


def per_device(field, tf_emission, tf_absorption):
    slab_count = lax.axis_size("slab")
    planes, height, width = field.shape
    low, high = neighbours(field[0], field[-1], "slab")
    left, right = neighbours(field[:, :, 0], field[:, :, -1], "tile")
    edge_lane = lax.broadcasted_iota(jnp.int32, (1, 1, LANES), 2) == 0
    edges = jnp.where(edge_lane, right[:, :, None], left[:, :, None])
    tables = segment_tables(tf_emission, tf_absorption, planes * slab_count)
    image = march(tables, field, low, high, edges, tf_emission.shape[1])
    levels = slab_count.bit_length() - 1
    block_rows = height // slab_count
    slab_index = lax.axis_index("slab")
    for shift in range(0, levels, 2):
        bits = min(2, levels - shift)
        outer = slab_count >> (shift + bits)
        image = image.reshape((6, outer, 1 << bits, block_rows, width))
        pair = exchange(image, slab_index, shift, bits)
        if outer > 1:
            image = jnp.concatenate(pair, axis=0)
    colour, transmit = (part.reshape((3, block_rows, width)) for part in pair)
    return colour, 1.0 - transmit


def solution(mesh):
    placed = (P("slab", None, "tile"), P(), P())
    return jax.shard_map(
        per_device,
        mesh=mesh,
        in_specs=placed,
        out_specs=(P(None, "slab", "tile"), P(None, "slab", "tile")),
        check_vma=False,
    )
```

```python
import functools

import jax
import jax.numpy as jnp
from jax import lax
from jax.experimental import pallas as pl
from jax.experimental.pallas import tpu as pltpu
from jax.sharding import PartitionSpec as P

LIGHT_DIR = (0.2672612, 0.5345225, 0.8017837)
LANES = 128
SUBLANES = 8
PAD = 8
WORD_SCALE = 2.0**31 - 2.0**17
HALF = 65536


def segment_words(tables):
    largest = jnp.maximum(jnp.max(tables), 1e-30)
    scaled = tables * (WORD_SCALE / largest)
    rise = jnp.round((scaled[:, 1:] - scaled[:, :-1]) * (1.0 / HALF))
    centre = 0.5 * (scaled[:, 1:] + scaled[:, :-1])
    rise = jnp.pad(rise, ((0, 0), (0, 1)))
    centre = jnp.concatenate([centre, scaled[:, -1:]], axis=1)
    upper = jnp.round((centre - rise) * (1.0 / HALF))
    return upper.astype(jnp.int32) * HALF + rise.astype(jnp.int32), largest / WORD_SCALE


def prepare_tables(tf_emission, tf_absorption, depth_total):
    emission, emission_unit = segment_words(tf_emission)
    absorption, absorption_unit = segment_words(tf_absorption)
    absorption_unit = absorption_unit * (4.0 / depth_total)
    words = jnp.concatenate([emission, absorption], axis=0)
    words = jnp.pad(words, ((0, 0), (0, LANES - words.shape[1])))
    words = jnp.broadcast_to(words[:, None, :], (6, SUBLANES, LANES))
    factors = jnp.stack(
        [(0.9 * part) * emission_unit for part in LIGHT_DIR]
        + [0.1 * emission_unit, absorption_unit, 0.75 * absorption_unit]
    )
    factors = jnp.broadcast_to(factors[:, None, None], (6, SUBLANES, LANES))
    return words, factors


def lookup(table, index):
    return jnp.take_along_axis(table, index, axis=1, mode="promise_in_bounds")


def march_kernel(mode, first_tile, tiles, scale, group, words, factors, *refs):
    refs = list(refs)
    field, side = refs.pop(0), refs.pop(0)
    low, high = (refs.pop(0), refs.pop(0)) if mode != "middle" else (None, None)
    middle = refs.pop(0) if mode == "rim" else None
    inner = refs.pop() if mode == "rim" else None
    cells, canvas, in_sems, out_sems = refs[-4:]
    outs = refs[:-4]
    planes, height, width = field.shape
    all_tiles = width // LANES
    body_rows = pl.ds(PAD, height)
    tile_index = lax.axis_index("tile")
    if mode == "full":
        blocks, marched = [(0, 1, planes)], range(planes)
    elif mode == "middle":
        blocks, marched = [(0, 1, planes)], range(1, planes - 1)
    else:
        blocks, marched = [(0, 1, 2), (planes - 2, 3, 2)], (0, planes - 1)
    place = {first + k: slot + k for first, slot, count in blocks for k in range(count)}
    place[-1] = 0
    place[planes] = max(place.values()) + 1

    def columns(tile):
        return pl.ds(tile * LANES, LANES)

    def incoming(slot):
        tile = first_tile + slot - 1
        copies = []
        for number, (first, where, count) in enumerate(blocks):
            if 0 <= tile < all_tiles:
                source = field.at[pl.ds(first, count), :, columns(tile)]
            else:
                source = side.at[pl.ds(first, count)]
            target = cells.at[slot, pl.ds(where, count), body_rows, :]
            copies.append(pltpu.make_async_copy(source, target, in_sems.at[slot, number]))
        if mode != "middle" and 1 <= slot <= tiles:
            here = columns(slot - 1)
            for number, (halo, plane) in enumerate(((low, -1), (high, planes))):
                target = cells.at[slot, place[plane], body_rows, :]
                copies.append(
                    pltpu.make_async_copy(halo.at[:, here], target, in_sems.at[slot, 2 + number])
                )
        if mode == "rim" and 1 <= slot <= tiles:
            copies.append(
                pltpu.make_async_copy(
                    middle.at[:, :, columns(slot - 1)], inner.at[slot - 1], in_sems.at[slot, 4]
                )
            )
        return copies

    def outgoing(tile):
        if len(outs) == 1:
            return [
                pltpu.make_async_copy(
                    canvas.at[tile], outs[0].at[:, :, columns(tile)], out_sems.at[tile, 0]
                )
            ]
        own = lax.axis_index("slab") & (group - 1)
        return [
            pltpu.make_async_copy(
                canvas.at[tile, :, :, own ^ change],
                outs[change].at[:, :, :, columns(tile)],
                out_sems.at[tile, change],
            )
            for change in range(group)
        ]

    for slot in range(tiles + 2):
        for copy in incoming(slot):
            copy.start()
    zeros = jnp.zeros((1, LANES), jnp.float32)
    for slot in range(1, tiles + 1):
        for plane in marched:
            cells[slot, place[plane], pl.ds(PAD - 1, 1), :] = zeros
            cells[slot, place[plane], pl.ds(PAD + height, 1), :] = zeros
    lane = lax.broadcasted_iota(jnp.int32, (SUBLANES, LANES), 1)
    first_lane = lane == 0
    last_lane = lane == LANES - 1
    has_left = (tile_index > 0).astype(jnp.float32)
    has_right = (tile_index < lax.axis_size("tile") - 1).astype(jnp.float32)

    def strip(slot, row):
        def rows(part, plane, offset=0):
            start = PAD + row * SUBLANES + offset
            return cells[part, place[plane], pl.ds(start, SUBLANES), :]

        colour = transmit = None
        for plane in marched:
            before, centre, after = (rows(slot, plane + k) for k in (-1, 0, 1))
            left_tile = rows(slot - 1, plane)
            right_tile = rows(slot + 1, plane)
            if first_tile + slot - 1 == 0:
                left_tile = left_tile * has_left
            if first_tile + slot == all_tiles:
                right_tile = right_tile * has_right
            left = pltpu.roll(jnp.where(last_lane, left_tile, centre), 1, 1)
            right = pltpu.roll(jnp.where(first_lane, right_tile, centre), LANES - 1, 1)
            diff_x = right - left
            diff_y = rows(slot, plane, 1) - rows(slot, plane, -1)
            diff_z = after - before
            inverse = lax.rsqrt(diff_x * diff_x + diff_y * diff_y + diff_z * diff_z + 1.0)
            facing = (factors[0] * diff_x + factors[1] * diff_y + factors[2] * diff_z) * inverse
            shading = jnp.maximum(facing, 0.0) + factors[3]
            weight = factors[4] - factors[5] * (inverse * inverse)
            middle_based = centre * scale + (scale - 0.5)
            interval = (middle_based + 0.5).astype(jnp.int32)
            offset = middle_based - interval.astype(jnp.float32)
            values = []
            for k in range(6):
                word = lookup(words[k], interval)
                rise = lax.shift_left(word, 16).astype(jnp.float32)
                values.append(word.astype(jnp.float32) + rise * offset)
            steps = [values[3 + ch] * weight for ch in range(3)]
            glows = [values[ch] * shading for ch in range(3)]
            if colour is None:
                colour = [step * glow for step, glow in zip(steps, glows)]
                transmit = [1.0 - step for step in steps]
            else:
                seen = [transmit[ch] * steps[ch] for ch in range(3)]
                colour = [colour[ch] + seen[ch] * glows[ch] for ch in range(3)]
                transmit = [transmit[ch] - seen[ch] for ch in range(3)]
            if mode == "rim" and plane == 0:
                here = pl.ds(row * SUBLANES, SUBLANES)
                held = [inner[slot - 1, k, here, :] for k in range(6)]
                colour = [colour[ch] + transmit[ch] * held[ch] for ch in range(3)]
                transmit = [transmit[ch] * held[3 + ch] for ch in range(3)]
        for k, value in enumerate(colour + transmit):
            if len(outs) == 1:
                canvas[slot - 1, k, pl.ds(row * SUBLANES, SUBLANES), :] = value
            else:
                block_rows = height // (canvas.shape[2] * group)
                block = (row * SUBLANES) // block_rows
                start = pl.multiple_of((row * SUBLANES) % block_rows, SUBLANES)
                canvas[
                    slot - 1, k, block // group, block % group, pl.ds(start, SUBLANES), :
                ] = value

    for copy in incoming(0) + incoming(1):
        copy.wait()
    for slot in range(1, tiles + 1):
        for copy in incoming(slot + 1):
            copy.wait()

        @pl.loop(0, height // SUBLANES)
        def _(row):
            strip(slot, row)

        for copy in outgoing(slot - 1):
            copy.start()
    for tile in range(tiles):
        for copy in outgoing(tile):
            copy.wait()


def march(mode, chunk, tables, field, side, halos, middle, count_breaks, part_shape):
    planes, height, width = field.shape
    first_tile, tiles = chunk
    extent = tiles * LANES
    held = 6 if mode == "rim" else planes + 2
    if part_shape is None:
        group = 1
        outs = [jax.ShapeDtypeStruct((6, height, extent), jnp.float32)]
        canvas = (tiles, 6, height, LANES)
    else:
        outer, group, rows = part_shape
        outs = [jax.ShapeDtypeStruct((6, outer, rows, extent), jnp.float32)] * group
        canvas = (tiles, 6, outer, group, rows, LANES)
    scratch = [
        pltpu.VMEM((tiles + 2, held, height + 2 * PAD, LANES), jnp.float32),
        pltpu.VMEM(canvas, jnp.float32),
        pltpu.SemaphoreType.DMA((tiles + 2, 5)),
        pltpu.SemaphoreType.DMA((tiles, group)),
    ]
    operands = [field, side]
    if mode != "middle":
        operands += list(halos)
    if mode == "rim":
        operands.append(middle)
        scratch.append(pltpu.VMEM((tiles, 6, height, LANES), jnp.float32))
    marched = {"full": planes, "middle": planes - 2, "rim": 2}[mode]
    anywhere = pl.BlockSpec(memory_space=pl.ANY)
    out = pl.pallas_call(
        functools.partial(
            march_kernel, mode, first_tile, tiles, 0.5 * (count_breaks - 1), group
        ),
        out_shape=outs,
        in_specs=[pl.BlockSpec(memory_space=pltpu.VMEM)] * 2 + [anywhere] * len(operands),
        out_specs=[anywhere] * len(outs),
        scratch_shapes=scratch,
        compiler_params=pltpu.CompilerParams(vmem_limit_bytes=24 * 1024 * 1024),
        cost_estimate=pl.CostEstimate(
            flops=marched * height * extent * 100,
            bytes_accessed=marched * height * extent * 6,
            transcendentals=0,
        ),
        name=f"march_{mode}_{first_tile}",
    )(*tables, *operands)
    return out[0] if part_shape is None else out


def plane_halos(first, last):
    count = lax.axis_size("slab")
    forward = [(i, i + 1) for i in range(count - 1)]
    backward = [(i + 1, i) for i in range(count - 1)]
    return lax.ppermute(last, "slab", forward), lax.ppermute(first, "slab", backward)


def edge_tile(field):
    first = lax.axis_index("tile") == 0
    planes, height, width = field.shape
    start = jnp.where(first, width - LANES, 0)
    own = lax.dynamic_slice_in_dim(field, start, LANES, axis=2)
    return lax.ppermute(own, "tile", [(0, 1), (1, 0)])


def ordered(is_far, own, other):
    near = [jnp.where(is_far, b, a) for a, b in zip(own, other)]
    far = [jnp.where(is_far, a, b) for a, b in zip(own, other)]
    return [near[0] + near[1] * far[0], near[1] * far[1]]


def take_parts(image, own, size):
    return [
        lax.dynamic_index_in_dim(image, own ^ change, 2, keepdims=False) for change in range(size)
    ]


def exchange(parts, own, shift):
    count = lax.axis_size("slab")
    merged = []
    for change, part in enumerate(parts):
        if change:
            part = lax.ppermute(part, "slab", [(i, i ^ change << shift) for i in range(count)])
        merged.append([part[:3], part[3:]])
    digit = 0
    while len(merged) > 1:
        is_far = (own >> digit & 1) == 1
        merged = [ordered(is_far, merged[k], merged[k + 1]) for k in range(0, len(merged), 2)]
        digit += 1
    return merged[0]


def reduce_image(image, parts, slab_index, block_rows):
    slab_count = lax.axis_size("slab")
    levels = slab_count.bit_length() - 1
    for shift in range(0, levels, 2):
        bits = min(2, levels - shift)
        own = (slab_index >> shift) & ((1 << bits) - 1)
        if parts is None:
            outer = slab_count >> (shift + bits)
            image = image.reshape((6, outer, 1 << bits, block_rows, image.shape[-1]))
            parts = take_parts(image, own, 1 << bits)
        colour, transmit = exchange(parts, own, shift)
        image, parts = jnp.concatenate([colour, transmit], axis=0), None
    return colour[:, 0], 1.0 - transmit[:, 0]


def per_device(field, tf_emission, tf_absorption):
    slab_count = lax.axis_size("slab")
    slab_index = lax.axis_index("slab")
    planes, height, width = field.shape
    count_breaks = tf_emission.shape[1]
    block_rows = height // slab_count
    tiles = width // LANES
    part_shape = None
    if slab_count >= 4 and block_rows % SUBLANES == 0:
        part_shape = (slab_count // 4, 4, block_rows)
    chunks = [(0, tiles // 2), (tiles // 2, tiles - tiles // 2)]
    tables = prepare_tables(tf_emission, tf_absorption, planes * slab_count)
    strips = [(first * LANES, (first + count) * LANES) for first, count in chunks]

    halos = []
    for begin, end in strips:
        first, last = field[0, :, begin:end], field[-1, :, begin:end]
        if halos:
            first, last, _ = lax.optimization_barrier((first, last, halos[-1]))
        halos.append(plane_halos(first, last))
        if len(halos) == 1:
            side = edge_tile(field)
    results = []
    for chunk, halo in zip(chunks, halos):
        if chunk[0] == 0:
            middle = march(
                "middle", chunk, tables, field, side, None, None, count_breaks, None
            )
            mode = "rim"
        else:
            middle, mode = None, "full"
        out = march(mode, chunk, tables, field, side, halo, middle, count_breaks, part_shape)
        image, parts = (out, None) if part_shape is None else (None, out)
        results.append(reduce_image(image, parts, slab_index, block_rows))
    return tuple(jnp.concatenate(pieces, axis=2) for pieces in zip(*results))


def solution(mesh):
    placed = (P("slab", None, "tile"), P(), P())
    return jax.shard_map(
        per_device,
        mesh=mesh,
        in_specs=placed,
        out_specs=(P(None, "slab", "tile"), P(None, "slab", "tile")),
        check_vma=False,
    )
```

```python
import functools

import jax
import jax.numpy as jnp
from jax import lax
from jax.experimental import pallas as pl
from jax.experimental.pallas import tpu as pltpu
from jax.sharding import PartitionSpec as P

LIGHT_DIR = (0.2672612, 0.5345225, 0.8017837)
LANES = 128
SUBLANES = 8
PAD = 8
WORD_SCALE = 2.0**31 - 2.0**17
HALF = 65536


def segment_words(tables):
    largest = jnp.maximum(jnp.max(tables), 1e-30)
    scaled = tables * (WORD_SCALE / largest)
    rise = jnp.round((scaled[:, 1:] - scaled[:, :-1]) * (1.0 / HALF))
    centre = 0.5 * (scaled[:, 1:] + scaled[:, :-1])
    rise = jnp.pad(rise, ((0, 0), (0, 1)))
    centre = jnp.concatenate([centre, scaled[:, -1:]], axis=1)
    upper = jnp.round((centre - rise) * (1.0 / HALF))
    return upper.astype(jnp.int32) * HALF + rise.astype(jnp.int32), largest / WORD_SCALE


def prepare_tables(tf_emission, tf_absorption, depth_total):
    emission, emission_unit = segment_words(tf_emission)
    absorption, absorption_unit = segment_words(tf_absorption)
    absorption_unit = absorption_unit * (4.0 / depth_total)
    words = jnp.concatenate([emission, absorption], axis=0)
    words = jnp.pad(words, ((0, 0), (0, LANES - words.shape[1])))
    words = jnp.broadcast_to(words[:, None, :], (6, SUBLANES, LANES))
    factors = jnp.stack(
        [(0.9 * part) * emission_unit for part in LIGHT_DIR]
        + [0.1 * emission_unit, absorption_unit, 0.75 * absorption_unit]
    )
    factors = jnp.broadcast_to(factors[:, None, None], (6, SUBLANES, LANES))
    return words, factors


def lookup(table, index):
    return jnp.take_along_axis(table, index, axis=1, mode="promise_in_bounds")


def march_kernel(mode, first_tile, tiles, scale, group, words, factors, *refs):
    refs = list(refs)
    field, side = refs.pop(0), refs.pop(0)
    low, high = (refs.pop(0), refs.pop(0)) if mode != "middle" else (None, None)
    middle = refs.pop(0) if mode == "rim" else None
    inner = refs.pop() if mode == "rim" else None
    cells, canvas, in_sems, out_sems = refs[-4:]
    outs = refs[:-4]
    planes, height, width = field.shape
    all_tiles = width // LANES
    body_rows = pl.ds(PAD, height)
    tile_index = lax.axis_index("tile")
    if mode == "full":
        blocks, marched = [(0, 1, planes)], range(planes)
    elif mode == "middle":
        blocks, marched = [(0, 1, planes)], range(1, planes - 1)
    else:
        blocks, marched = [(0, 1, 2), (planes - 2, 3, 2)], (0, planes - 1)
    place = {first + k: slot + k for first, slot, count in blocks for k in range(count)}
    place[-1] = 0
    place[planes] = max(place.values()) + 1

    def columns(tile):
        return pl.ds(tile * LANES, LANES)

    def incoming(slot):
        tile = first_tile + slot - 1
        copies = []
        for number, (first, where, count) in enumerate(blocks):
            if 0 <= tile < all_tiles:
                source = field.at[pl.ds(first, count), :, columns(tile)]
            else:
                source = side.at[pl.ds(first, count)]
            target = cells.at[slot, pl.ds(where, count), body_rows, :]
            copies.append(pltpu.make_async_copy(source, target, in_sems.at[slot, number]))
        if mode != "middle" and 1 <= slot <= tiles:
            here = columns(slot - 1)
            for number, (halo, plane) in enumerate(((low, -1), (high, planes))):
                target = cells.at[slot, place[plane], body_rows, :]
                copies.append(
                    pltpu.make_async_copy(halo.at[:, here], target, in_sems.at[slot, 2 + number])
                )
        if mode == "rim" and 1 <= slot <= tiles:
            copies.append(
                pltpu.make_async_copy(
                    middle.at[:, :, columns(slot - 1)], inner.at[slot - 1], in_sems.at[slot, 4]
                )
            )
        return copies

    def outgoing(tile):
        if len(outs) == 1:
            return [
                pltpu.make_async_copy(
                    canvas.at[tile], outs[0].at[:, :, columns(tile)], out_sems.at[tile, 0]
                )
            ]
        own = lax.axis_index("slab") & (group - 1)
        return [
            pltpu.make_async_copy(
                canvas.at[tile, :, :, own ^ change],
                outs[change].at[:, :, :, columns(tile)],
                out_sems.at[tile, change],
            )
            for change in range(group)
        ]

    for slot in range(tiles + 2):
        for copy in incoming(slot):
            copy.start()
    zeros = jnp.zeros((1, LANES), jnp.float32)
    for slot in range(1, tiles + 1):
        for plane in marched:
            cells[slot, place[plane], pl.ds(PAD - 1, 1), :] = zeros
            cells[slot, place[plane], pl.ds(PAD + height, 1), :] = zeros
    lane = lax.broadcasted_iota(jnp.int32, (SUBLANES, LANES), 1)
    first_lane = lane == 0
    last_lane = lane == LANES - 1
    has_left = (tile_index > 0).astype(jnp.float32)
    has_right = (tile_index < lax.axis_size("tile") - 1).astype(jnp.float32)

    def strip(slot, row):
        def rows(part, plane, offset=0):
            start = PAD + row * SUBLANES + offset
            return cells[part, place[plane], pl.ds(start, SUBLANES), :]

        colour = transmit = None
        for plane in marched:
            before, centre, after = (rows(slot, plane + k) for k in (-1, 0, 1))
            left_tile = rows(slot - 1, plane)
            right_tile = rows(slot + 1, plane)
            if first_tile + slot - 1 == 0:
                left_tile = left_tile * has_left
            if first_tile + slot == all_tiles:
                right_tile = right_tile * has_right
            left = pltpu.roll(jnp.where(last_lane, left_tile, centre), 1, 1)
            right = pltpu.roll(jnp.where(first_lane, right_tile, centre), LANES - 1, 1)
            diff_x = right - left
            diff_y = rows(slot, plane, 1) - rows(slot, plane, -1)
            diff_z = after - before
            inverse = lax.rsqrt(diff_x * diff_x + diff_y * diff_y + diff_z * diff_z + 1.0)
            facing = (factors[0] * diff_x + factors[1] * diff_y + factors[2] * diff_z) * inverse
            shading = jnp.maximum(facing, 0.0) + factors[3]
            weight = factors[4] - factors[5] * (inverse * inverse)
            middle_based = centre * scale + (scale - 0.5)
            interval = (middle_based + 0.5).astype(jnp.int32)
            offset = middle_based - interval.astype(jnp.float32)
            values = []
            for k in range(6):
                word = lookup(words[k], interval)
                rise = lax.shift_left(word, 16).astype(jnp.float32)
                values.append(word.astype(jnp.float32) + rise * offset)
            steps = [values[3 + ch] * weight for ch in range(3)]
            glows = [values[ch] * shading for ch in range(3)]
            if colour is None:
                colour = [step * glow for step, glow in zip(steps, glows)]
                transmit = [1.0 - step for step in steps]
            else:
                seen = [transmit[ch] * steps[ch] for ch in range(3)]
                colour = [colour[ch] + seen[ch] * glows[ch] for ch in range(3)]
                transmit = [transmit[ch] - seen[ch] for ch in range(3)]
            if mode == "rim" and plane == 0:
                here = pl.ds(row * SUBLANES, SUBLANES)
                held = [inner[slot - 1, k, here, :] for k in range(6)]
                colour = [colour[ch] + transmit[ch] * held[ch] for ch in range(3)]
                transmit = [transmit[ch] * held[3 + ch] for ch in range(3)]
        for k, value in enumerate(colour + transmit):
            if len(outs) == 1:
                canvas[slot - 1, k, pl.ds(row * SUBLANES, SUBLANES), :] = value
            else:
                block_rows = height // (canvas.shape[2] * group)
                block = (row * SUBLANES) // block_rows
                start = pl.multiple_of((row * SUBLANES) % block_rows, SUBLANES)
                canvas[
                    slot - 1, k, block // group, block % group, pl.ds(start, SUBLANES), :
                ] = value

    for copy in incoming(0) + incoming(1):
        copy.wait()
    for slot in range(1, tiles + 1):
        for copy in incoming(slot + 1):
            copy.wait()

        @pl.loop(0, height // SUBLANES)
        def _(row):
            strip(slot, row)

        for copy in outgoing(slot - 1):
            copy.start()
    for tile in range(tiles):
        for copy in outgoing(tile):
            copy.wait()


def march(mode, chunk, tables, field, side, halos, middle, count_breaks, part_shape):
    planes, height, width = field.shape
    first_tile, tiles = chunk
    extent = tiles * LANES
    held = 6 if mode == "rim" else planes + 2
    if part_shape is None:
        group = 1
        outs = [jax.ShapeDtypeStruct((6, height, extent), jnp.float32)]
        canvas = (tiles, 6, height, LANES)
    else:
        outer, group, rows = part_shape
        outs = [jax.ShapeDtypeStruct((6, outer, rows, extent), jnp.float32)] * group
        canvas = (tiles, 6, outer, group, rows, LANES)
    scratch = [
        pltpu.VMEM((tiles + 2, held, height + 2 * PAD, LANES), jnp.float32),
        pltpu.VMEM(canvas, jnp.float32),
        pltpu.SemaphoreType.DMA((tiles + 2, 5)),
        pltpu.SemaphoreType.DMA((tiles, group)),
    ]
    operands = [field, side]
    if mode != "middle":
        operands += list(halos)
    if mode == "rim":
        operands.append(middle)
        scratch.append(pltpu.VMEM((tiles, 6, height, LANES), jnp.float32))
    marched = {"full": planes, "middle": planes - 2, "rim": 2}[mode]
    anywhere = pl.BlockSpec(memory_space=pltpu.HBM)
    out = pl.pallas_call(
        functools.partial(
            march_kernel, mode, first_tile, tiles, 0.5 * (count_breaks - 1), group
        ),
        out_shape=outs,
        in_specs=[pl.BlockSpec(memory_space=pltpu.VMEM)] * 2 + [anywhere] * len(operands),
        out_specs=[anywhere] * len(outs),
        scratch_shapes=scratch,
        compiler_params=pltpu.CompilerParams(vmem_limit_bytes=24 * 1024 * 1024),
        cost_estimate=pl.CostEstimate(
            flops=marched * height * extent * 100,
            bytes_accessed=marched * height * extent * 6,
            transcendentals=0,
        ),
        name=f"march_{mode}_{first_tile}",
    )(*tables, *operands)
    return out[0] if part_shape is None else out


def plane_halos(first, last):
    count = lax.axis_size("slab")
    forward = [(i, i + 1) for i in range(count - 1)]
    backward = [(i + 1, i) for i in range(count - 1)]
    return lax.ppermute(last, "slab", forward), lax.ppermute(first, "slab", backward)


def edge_tile(field, earlier):
    first = lax.axis_index("tile") == 0
    planes, height, width = field.shape
    start, _ = lax.optimization_barrier((jnp.where(first, width - LANES, 0), earlier))
    own = lax.dynamic_slice_in_dim(field, start, LANES, axis=2)
    return lax.ppermute(own, "tile", [(0, 1), (1, 0)])


def ordered(is_far, own, other):
    near = [jnp.where(is_far, b, a) for a, b in zip(own, other)]
    far = [jnp.where(is_far, a, b) for a, b in zip(own, other)]
    return [near[0] + near[1] * far[0], near[1] * far[1]]


def take_parts(image, own, size):
    return [
        lax.dynamic_index_in_dim(image, own ^ change, 2, keepdims=False) for change in range(size)
    ]


def exchange(parts, own, shift):
    count = lax.axis_size("slab")
    merged = []
    for change, part in enumerate(parts):
        if change:
            part = lax.ppermute(part, "slab", [(i, i ^ change << shift) for i in range(count)])
        merged.append([part[:3], part[3:]])
    digit = 0
    while len(merged) > 1:
        is_far = (own >> digit & 1) == 1
        merged = [ordered(is_far, merged[k], merged[k + 1]) for k in range(0, len(merged), 2)]
        digit += 1
    return merged[0]


def reduce_image(image, parts, slab_index, block_rows):
    slab_count = lax.axis_size("slab")
    levels = slab_count.bit_length() - 1
    for shift in range(0, levels, 2):
        bits = min(2, levels - shift)
        own = (slab_index >> shift) & ((1 << bits) - 1)
        if parts is None:
            outer = slab_count >> (shift + bits)
            image = image.reshape((6, outer, 1 << bits, block_rows, image.shape[-1]))
            parts = take_parts(image, own, 1 << bits)
        colour, transmit = exchange(parts, own, shift)
        image, parts = jnp.concatenate([colour, transmit], axis=0), None
    return colour[:, 0], 1.0 - transmit[:, 0]


def per_device(field, tf_emission, tf_absorption):
    slab_count = lax.axis_size("slab")
    slab_index = lax.axis_index("slab")
    planes, height, width = field.shape
    count_breaks = tf_emission.shape[1]
    block_rows = height // slab_count
    tiles = width // LANES
    part_shape = None
    if slab_count >= 4 and block_rows % SUBLANES == 0:
        part_shape = (slab_count // 4, 4, block_rows)
    chunks = [(0, tiles // 2), (tiles // 2, tiles - tiles // 2)]
    tables = prepare_tables(tf_emission, tf_absorption, planes * slab_count)
    strips = [(first * LANES, (first + count) * LANES) for first, count in chunks]

    planes_out = [(field[0, :, begin:end], field[-1, :, begin:end]) for begin, end in strips]
    halos = [plane_halos(first, last) for first, last in planes_out]
    side = edge_tile(field, planes_out)
    results = []
    for chunk, halo in zip(chunks, halos):
        if results:
            halo, _ = lax.optimization_barrier((halo, out))
        if chunk[0] == 0:
            middle = march(
                "middle", chunk, tables, field, side, None, None, count_breaks, None
            )
            mode = "rim"
        else:
            middle, mode = None, "full"
        out = march(mode, chunk, tables, field, side, halo, middle, count_breaks, part_shape)
        image, parts = (out, None) if part_shape is None else (None, out)
        results.append(reduce_image(image, parts, slab_index, block_rows))
    return tuple(jnp.concatenate(pieces, axis=2) for pieces in zip(*results))


def solution(mesh):
    placed = (P("slab", None, "tile"), P(), P())
    return jax.shard_map(
        per_device,
        mesh=mesh,
        in_specs=placed,
        out_specs=(P(None, "slab", "tile"), P(None, "slab", "tile")),
        check_vma=False,
    )
```

```python
import functools

import jax
import jax.numpy as jnp
from jax import lax
from jax.experimental import pallas as pl
from jax.experimental.pallas import tpu as pltpu
from jax.sharding import PartitionSpec as P

LIGHT_DIR = (0.2672612, 0.5345225, 0.8017837)
LANES = 128
SUBLANES = 8
PAD = 8
WORD_SCALE = 2.0**31 - 2.0**17
HALF = 65536


def prepare_tables(emission, absorption, depth_total, table, words, factors):
    breaks = emission.shape[1]
    table[...] = jnp.zeros(table.shape, jnp.float32)
    table[0:3, 0:breaks] = emission[...]
    table[3:6, 0:breaks] = absorption[...]
    values = table[...]
    largest = [jnp.maximum(jnp.max(ref[...]), 1e-30) for ref in (emission, absorption)]
    row = lax.broadcasted_iota(jnp.int32, table.shape, 0)
    lane = lax.broadcasted_iota(jnp.int32, table.shape, 1)
    scaled = values * (WORD_SCALE / jnp.where(row < 3, largest[0], largest[1]))
    following = jnp.where(lane < breaks - 1, pltpu.roll(scaled, LANES - 1, 1), scaled)
    rise = jnp.floor((following - scaled) * (1.0 / HALF) + 0.5)
    upper = jnp.floor((0.5 * (following + scaled) - rise) * (1.0 / HALF) + 0.5)
    word = upper.astype(jnp.int32) * HALF + rise.astype(jnp.int32)
    units = [largest[0] / WORD_SCALE, largest[1] * (4.0 / depth_total) / WORD_SCALE]
    constants = [0.9 * part * units[0] for part in LIGHT_DIR]
    constants += [0.1 * units[0], units[1], 0.75 * units[1]]
    for k in range(6):
        words[k] = jnp.broadcast_to(word[k : k + 1, :], (SUBLANES, LANES))
        factors[k] = jnp.full((SUBLANES, LANES), constants[k], jnp.float32)


def lookup(table, index):
    return lax.gather(
        table,
        index.reshape(index.shape + (1,)),
        lax.GatherDimensionNumbers(
            offset_dims=(),
            collapsed_slice_dims=(1,),
            start_index_map=(1,),
            operand_batching_dims=(0,),
            start_indices_batching_dims=(0,),
        ),
        slice_sizes=(1, 1),
        mode=lax.GatherScatterMode.PROMISE_IN_BOUNDS,
    )


def march_kernel(mode, chunk, depth_total, group, emission, absorption, *refs):
    refs = list(refs)
    field = refs.pop(0)
    planes, height, width = field.shape
    all_tiles = width // LANES
    near = sorted({tile + k for tile in chunk for k in (-1, 0, 1)})
    side = refs.pop(0) if near[0] < 0 or near[-1] >= all_tiles else None
    low, high = (refs.pop(0), refs.pop(0)) if mode != "middle" else (None, None)
    middle = refs.pop(0) if mode == "rim" else None
    inner = refs.pop() if mode == "rim" else None
    cells, canvas, table, words, factors, in_sems, out_sems = refs[-7:]
    outs = refs[:-7]
    scale = 0.5 * (emission.shape[1] - 1)
    slot_of = {tile: slot for slot, tile in enumerate(near)}
    body_rows = pl.ds(PAD, height)
    tile_index = lax.axis_index("tile")
    if mode == "full":
        blocks, marched = [(0, 1, planes)], range(planes)
    elif mode == "middle":
        blocks, marched = [(0, 1, planes)], range(1, planes - 1)
    else:
        blocks, marched = [(0, 1, 2), (planes - 2, 3, 2)], (0, planes - 1)
    place = {first + k: slot + k for first, slot, count in blocks for k in range(count)}
    place[-1] = 0
    place[planes] = max(place.values()) + 1

    def columns(tile):
        return pl.ds(tile * LANES, LANES)

    def incoming(tile):
        slot = slot_of[tile]
        copies = []
        for number, (first, where, count) in enumerate(blocks):
            if 0 <= tile < all_tiles:
                source = field.at[pl.ds(first, count), :, columns(tile)]
            else:
                source = side.at[pl.ds(first, count)]
            target = cells.at[slot, pl.ds(where, count), body_rows, :]
            copies.append(pltpu.make_async_copy(source, target, in_sems.at[slot, number]))
        if mode != "middle" and tile in chunk:
            for number, (halo, plane) in enumerate(((low, -1), (high, planes))):
                target = cells.at[slot, place[plane], body_rows, :]
                source = halo.at[:, columns(tile)]
                copies.append(pltpu.make_async_copy(source, target, in_sems.at[slot, 2 + number]))
        if mode == "rim" and tile in chunk:
            at = chunk.index(tile)
            copies.append(
                pltpu.make_async_copy(
                    middle.at[:, :, columns(at)], inner.at[at], in_sems.at[slot, 4]
                )
            )
        return copies

    def outgoing(at):
        if len(outs) == 1:
            target = outs[0].at[:, :, columns(at)]
            return [pltpu.make_async_copy(canvas.at[at], target, out_sems.at[at, 0])]
        own = lax.axis_index("slab") & (group - 1)
        return [
            pltpu.make_async_copy(
                canvas.at[at, :, own ^ change],
                outs[change].at[:, :, :, columns(at)],
                out_sems.at[at, change],
            )
            for change in range(group)
        ]

    for tile in near:
        for copy in incoming(tile):
            copy.start()
    prepare_tables(emission, absorption, depth_total, table, words, factors)
    zeros = jnp.zeros((1, LANES), jnp.float32)
    for tile in chunk:
        for plane in marched:
            cells[slot_of[tile], place[plane], pl.ds(PAD - 1, 1), :] = zeros
            cells[slot_of[tile], place[plane], pl.ds(PAD + height, 1), :] = zeros
    lane = lax.broadcasted_iota(jnp.int32, (SUBLANES, LANES), 1)
    first_lane = lane == 0
    last_lane = lane == LANES - 1
    has_left = (tile_index > 0).astype(jnp.float32)
    has_right = (tile_index < lax.axis_size("tile") - 1).astype(jnp.float32)

    def strip(at, row):
        tile = chunk[at]

        def rows(of, plane, offset=0):
            start = PAD + row * SUBLANES + offset
            return cells[slot_of[of], place[plane], pl.ds(start, SUBLANES), :]

        colour = transmit = None
        for plane in marched:
            before, centre, after = (rows(tile, plane + k) for k in (-1, 0, 1))
            left_tile = rows(tile - 1, plane)
            right_tile = rows(tile + 1, plane)
            if tile == 0:
                left_tile = left_tile * has_left
            if tile == all_tiles - 1:
                right_tile = right_tile * has_right
            left = pltpu.roll(jnp.where(last_lane, left_tile, centre), 1, 1)
            right = pltpu.roll(jnp.where(first_lane, right_tile, centre), LANES - 1, 1)
            diff_x = right - left
            diff_y = rows(tile, plane, 1) - rows(tile, plane, -1)
            diff_z = after - before
            inverse = lax.rsqrt(diff_x * diff_x + diff_y * diff_y + diff_z * diff_z + 1.0)
            facing = (factors[0] * diff_x + factors[1] * diff_y + factors[2] * diff_z) * inverse
            shading = jnp.maximum(facing, 0.0) + factors[3]
            weight = factors[4] - factors[5] * (inverse * inverse)
            middle_based = centre * scale + (scale - 0.5)
            interval = (middle_based + 0.5).astype(jnp.int32)
            offset = middle_based - interval.astype(jnp.float32)
            values = []
            for k in range(6):
                word = lookup(words[k], interval)
                rise = lax.shift_left(word, 16).astype(jnp.float32)
                values.append(word.astype(jnp.float32) + rise * offset)
            steps = [values[3 + ch] * weight for ch in range(3)]
            glows = [values[ch] * shading for ch in range(3)]
            if colour is None:
                colour = [step * glow for step, glow in zip(steps, glows)]
                transmit = [1.0 - step for step in steps]
            else:
                seen = [transmit[ch] * steps[ch] for ch in range(3)]
                colour = [colour[ch] + seen[ch] * glows[ch] for ch in range(3)]
                transmit = [transmit[ch] - seen[ch] for ch in range(3)]
            if mode == "rim" and plane == 0:
                here = pl.ds(row * SUBLANES, SUBLANES)
                held = [inner[at, k, here, :] for k in range(6)]
                colour = [colour[ch] + transmit[ch] * held[ch] for ch in range(3)]
                transmit = [transmit[ch] * held[3 + ch] for ch in range(3)]
        for k, value in enumerate(colour + transmit):
            if len(outs) == 1:
                canvas[at, k, pl.ds(row * SUBLANES, SUBLANES), :] = value
            else:
                block_rows = canvas.shape[4]
                block = (row * SUBLANES) // block_rows
                start = pl.multiple_of((row * SUBLANES) % block_rows, SUBLANES)
                canvas[at, block // group, block % group, k, pl.ds(start, SUBLANES), :] = value

    arrived = set()
    for at, tile in enumerate(chunk):
        for other in (tile - 1, tile, tile + 1):
            if other not in arrived:
                for copy in incoming(other):
                    copy.wait()
                arrived.add(other)

        @pl.loop(0, height // SUBLANES, unroll=4 if mode == "rim" else 2)
        def _(row):
            strip(at, row)

        for copy in outgoing(at):
            copy.start()
    for at in range(len(chunk)):
        for copy in outgoing(at):
            copy.wait()


def march(mode, chunk, tables, field, side, halos, middle, depth_total, part_shape):
    planes, height, width = field.shape
    tiles = len(chunk)
    near = {tile + k for tile in chunk for k in (-1, 0, 1)}
    extent = tiles * LANES
    held = 6 if mode == "rim" else planes + 2
    if part_shape is None:
        group = 1
        outs = [jax.ShapeDtypeStruct((6, height, extent), jnp.float32)]
        canvas = (tiles, 6, height, LANES)
    else:
        outer, group, rows = part_shape
        outs = [jax.ShapeDtypeStruct((outer, 6, rows, extent), jnp.float32)] * group
        canvas = (tiles, outer, group, 6, rows, LANES)
    scratch = [
        pltpu.VMEM((len(near), held, height + 2 * PAD, LANES), jnp.float32),
        pltpu.VMEM(canvas, jnp.float32),
        pltpu.VMEM((SUBLANES, LANES), jnp.float32),
        pltpu.VMEM((6, SUBLANES, LANES), jnp.int32),
        pltpu.VMEM((6, SUBLANES, LANES), jnp.float32),
        pltpu.SemaphoreType.DMA((len(near), 5)),
        pltpu.SemaphoreType.DMA((tiles, group)),
    ]
    operands = [field]
    if min(near) < 0 or max(near) >= width // LANES:
        operands.append(side)
    if mode != "middle":
        operands += list(halos)
    if mode == "rim":
        operands.append(middle)
        scratch.append(pltpu.VMEM((tiles, 6, height, LANES), jnp.float32))
    marched = {"full": planes, "middle": planes - 2, "rim": 4}[mode]
    weight = 100 if mode == "middle" else 20000
    far = pl.BlockSpec(memory_space=pltpu.HBM)
    out = pl.pallas_call(
        functools.partial(march_kernel, mode, chunk, depth_total, group),
        out_shape=outs,
        in_specs=[pl.BlockSpec(memory_space=pltpu.VMEM)] * 2 + [far] * len(operands),
        out_specs=[far] * len(outs),
        scratch_shapes=scratch,
        compiler_params=pltpu.CompilerParams(vmem_limit_bytes=60 * 1024 * 1024),
        cost_estimate=pl.CostEstimate(
            flops=marched * height * extent * weight,
            bytes_accessed=marched * height * extent * 5,
            transcendentals=0,
        ),
        name=f"march_{mode}_{chunk[0]}",
    )(*tables, *operands)
    return out[0] if part_shape is None else out


def plane_halos(first, last):
    count = lax.axis_size("slab")
    forward = [(i, i + 1) for i in range(count - 1)]
    backward = [(i + 1, i) for i in range(count - 1)]
    return lax.ppermute(last, "slab", forward), lax.ppermute(first, "slab", backward)


def edge_tile(field, earlier):
    first = lax.axis_index("tile") == 0
    planes, height, width = field.shape
    start, _ = lax.optimization_barrier((jnp.where(first, width - LANES, 0), earlier))
    own = lax.dynamic_slice_in_dim(field, start, LANES, axis=2)
    return lax.ppermute(own, "tile", [(0, 1), (1, 0)])


def ordered(is_far, own, other):
    near = [jnp.where(is_far, b, a) for a, b in zip(own, other)]
    far = [jnp.where(is_far, a, b) for a, b in zip(own, other)]
    return [near[0] + near[1] * far[0], near[1] * far[1]]


def exchange(parts, own, shift):
    count = lax.axis_size("slab")
    merged = []
    for change, part in enumerate(parts):
        if change:
            part = lax.ppermute(part, "slab", [(i, i ^ change << shift) for i in range(count)])
        merged.append([part[:, :3], part[:, 3:]])
    digit = 0
    while len(merged) > 1:
        is_far = (own >> digit & 1) == 1
        merged = [ordered(is_far, merged[k], merged[k + 1]) for k in range(0, len(merged), 2)]
        digit += 1
    return merged[0]


def reduce_image(image, parts, slab_index, block_rows):
    slab_count = lax.axis_size("slab")
    levels = slab_count.bit_length() - 1
    if parts is None:
        image = image.reshape((6, slab_count, block_rows, image.shape[-1]))
        image = jnp.swapaxes(image, 0, 1)
    for shift in range(0, levels, 2):
        size = 1 << min(2, levels - shift)
        own = (slab_index >> shift) & (size - 1)
        if parts is None:
            image = image.reshape((-1, size) + image.shape[1:])
            parts = [
                lax.dynamic_index_in_dim(image, own ^ change, 1, keepdims=False)
                for change in range(size)
            ]
        colour, transmit = exchange(parts, own, shift)
        image, parts = jnp.concatenate([colour, transmit], axis=1), None
    return colour[0], 1.0 - transmit[0]


def per_device(field, tf_emission, tf_absorption):
    slab_count = lax.axis_size("slab")
    slab_index = lax.axis_index("slab")
    planes, height, width = field.shape
    depth_total = planes * slab_count
    block_rows = height // slab_count
    tiles = width // LANES
    part_shape = None
    if slab_count >= 4 and block_rows % SUBLANES == 0:
        part_shape = (slab_count // 4, 4, block_rows)
    chunks = [tuple(range(1, tiles - 1)), (0, tiles - 1)]
    tables = (tf_emission, tf_absorption)

    halo = plane_halos(field[0], field[-1])
    results = []
    for number, chunk in enumerate(chunks):
        if number == 0:
            middle = march(
                "middle", chunk, tables, field, None, None, None, depth_total, None
            )
            mode, side = "rim", None
        else:
            side = edge_tile(field, (halo, middle))
            halo, side, _ = lax.optimization_barrier((halo, side, out))
            middle, mode = None, "full"
        out = march(mode, chunk, tables, field, side, halo, middle, depth_total, part_shape)
        image, parts = (out, None) if part_shape is None else (None, out)
        results.append(reduce_image(image, parts, slab_index, block_rows))
    gathered = []
    for inner, outer in zip(*results):
        gathered.append(
            jnp.concatenate([outer[:, :, :LANES], inner, outer[:, :, LANES:]], axis=2)
        )
    return tuple(gathered)


def solution(mesh):
    placed = (P("slab", None, "tile"), P(), P())
    return jax.shard_map(
        per_device,
        mesh=mesh,
        in_specs=placed,
        out_specs=(P(None, "slab", "tile"), P(None, "slab", "tile")),
        check_vma=False,
    )
```

```python
import functools

import jax
import jax.numpy as jnp
from jax import lax
from jax.experimental import pallas as pl
from jax.experimental.pallas import tpu as pltpu
from jax.sharding import PartitionSpec as P

LIGHT_DIR = (0.2672612, 0.5345225, 0.8017837)
LANES = 128
SUBLANES = 8
PAD = 8
WORD_SCALE = 2.0**31 - 2.0**17
HALF = 65536


def prepare_tables(emission, absorption, depth_total, table, words, factors):
    breaks = emission.shape[1]
    table[...] = jnp.zeros(table.shape, jnp.float32)
    table[0:3, 0:breaks] = emission[...]
    table[3:6, 0:breaks] = absorption[...]
    values = table[...]
    largest = [jnp.maximum(jnp.max(ref[...]), 1e-30) for ref in (emission, absorption)]
    row = lax.broadcasted_iota(jnp.int32, table.shape, 0)
    lane = lax.broadcasted_iota(jnp.int32, table.shape, 1)
    scaled = values * (WORD_SCALE / jnp.where(row < 3, largest[0], largest[1]))
    following = jnp.where(lane < breaks - 1, pltpu.roll(scaled, LANES - 1, 1), scaled)
    rise = jnp.floor((following - scaled) * (1.0 / HALF) + 0.5)
    upper = jnp.floor((0.5 * (following + scaled) - rise) * (1.0 / HALF) + 0.5)
    word = upper.astype(jnp.int32) * HALF + rise.astype(jnp.int32)
    units = [largest[0] / WORD_SCALE, largest[1] * (4.0 / depth_total) / WORD_SCALE]
    constants = [0.9 * part * units[0] for part in LIGHT_DIR]
    constants += [0.1 * units[0], units[1], 0.75 * units[1]]
    for k in range(6):
        words[k] = jnp.broadcast_to(word[k : k + 1, :], (SUBLANES, LANES))
        factors[k] = jnp.full((SUBLANES, LANES), constants[k], jnp.float32)


def lookup(table, index):
    return lax.gather(
        table,
        index.reshape(index.shape + (1,)),
        lax.GatherDimensionNumbers(
            offset_dims=(),
            collapsed_slice_dims=(1,),
            start_index_map=(1,),
            operand_batching_dims=(0,),
            start_indices_batching_dims=(0,),
        ),
        slice_sizes=(1, 1),
        mode=lax.GatherScatterMode.PROMISE_IN_BOUNDS,
    )


def march_kernel(mode, chunk, depth_total, group, emission, absorption, *refs):
    refs = list(refs)
    field = refs.pop(0)
    planes, height, width = field.shape
    all_tiles = width // LANES
    near = sorted({tile + k for tile in chunk for k in (-1, 0, 1)})
    side = refs.pop(0) if near[0] < 0 or near[-1] >= all_tiles else None
    low, high = (refs.pop(0), refs.pop(0)) if mode != "middle" else (None, None)
    middle = refs.pop(0) if mode == "rim" else None
    inner = refs.pop() if mode == "rim" else None
    cells, shifted, canvas, table, words, factors, in_sems, out_sems = refs[-8:]
    outs = refs[:-8]
    edge = outs.pop() if mode == "middle" else None
    scale = 0.5 * (emission.shape[1] - 1)
    slot_of = {tile: slot for slot, tile in enumerate(near)}
    piece_rows = height // in_sems.shape[0]
    pieces = height // piece_rows
    tile_index = lax.axis_index("tile")
    if mode == "full":
        blocks, marched = [(0, 1, planes)], range(planes)
    elif mode == "middle":
        blocks, marched = [(0, 1, planes)], range(1, planes - 1)
    else:
        blocks, marched = [(0, 1, 2), (planes - 2, 3, 2)], (0, planes - 1)
    place = {first + k: slot + k for first, slot, count in blocks for k in range(count)}
    place[-1] = 0
    place[planes] = max(place.values()) + 1
    if mode == "rim":
        shifted_blocks = [(0, 0, 1), (planes - 1, 1, 1)]
    else:
        shifted_blocks = [(marched[0], 0, len(marched))]
    shifted_place = {plane: k for k, plane in enumerate(marched)}

    def columns(tile):
        return pl.ds(tile * LANES, LANES)

    def incoming(piece, below):
        start = pl.multiple_of(piece * piece_rows, SUBLANES)
        body = pl.ds(start, piece_rows)
        copies = []

        def copy(source, target):
            slot = len(copies) + (0 if below else 2 * len(chunk))
            copies.append(pltpu.make_async_copy(source, target, in_sems.at[piece, slot]))

        if below:
            for at, tile in enumerate(chunk):
                for first, where, count in shifted_blocks:
                    copy(
                        field.at[pl.ds(first, count), body, columns(tile)],
                        shifted.at[
                            1, at, pl.ds(where, count), pl.ds(start + PAD - 1, piece_rows), :
                        ],
                    )
            return copies
        for tile in near:
            for first, where, count in blocks:
                if 0 <= tile < all_tiles:
                    source = field.at[pl.ds(first, count), body, columns(tile)]
                else:
                    source = side.at[pl.ds(first, count), body]
                copy(source, cells.at[slot_of[tile], pl.ds(where, count), body, :])
        for at, tile in enumerate(chunk):
            for first, where, count in shifted_blocks:
                copy(
                    field.at[pl.ds(first, count), body, columns(tile)],
                    shifted.at[0, at, pl.ds(where, count), pl.ds(start + PAD + 1, piece_rows), :],
                )
            if mode != "middle":
                for halo, plane in ((low, -1), (high, planes)):
                    target = cells.at[slot_of[tile], place[plane], body, :]
                    copy(halo.at[body, columns(tile)], target)
            if mode == "rim":
                copy(middle.at[:, body, columns(at)], inner.at[at, :, body, :])
        return copies

    def outgoing(piece):
        body = pl.ds(pl.multiple_of(piece * piece_rows, SUBLANES), piece_rows)
        copies = []
        for at in range(len(chunk)):
            if len(outs) == 1:
                pairs = [(canvas.at[at, :, body, :], outs[0].at[:, body, columns(at)])]
            else:
                own = lax.axis_index("slab") & (group - 1)
                pairs = [
                    (canvas.at[at, piece, own ^ k], outs[k].at[piece, :, :, columns(at)])
                    for k in range(group)
                ]
            for k, (source, target) in enumerate(pairs):
                copies.append(pltpu.make_async_copy(source, target, out_sems.at[piece, at, k]))
        if edge is not None:
            mine = jnp.where(tile_index == 0, slot_of[all_tiles - 1], slot_of[0])
            source = cells.at[mine, pl.ds(1, planes), body, :]
            sem = out_sems.at[piece, len(chunk), 0]
            copies.append(pltpu.make_async_copy(source, edge.at[:, body, :], sem))
        return copies

    def start(piece):
        for below in (False, True):
            for copy in incoming(piece, below):
                copy.start()

    start(0)
    if pieces > 1:
        start(1)
    prepare_tables(emission, absorption, depth_total, table, words, factors)
    zeros = jnp.zeros((len(marched), 1, LANES), jnp.float32)
    for at in range(len(chunk)):
        shifted[0, at, :, pl.ds(PAD, 1), :] = zeros
    lane = lax.broadcasted_iota(jnp.int32, (SUBLANES, LANES), 1)
    first_lane = lane == 0
    last_lane = lane == LANES - 1
    has_left = (tile_index > 0).astype(jnp.float32)
    has_right = (tile_index < lax.axis_size("tile") - 1).astype(jnp.float32)

    def strip(at, piece, number):
        tile = chunk[at]
        row = pl.multiple_of(piece * piece_rows + number * SUBLANES, SUBLANES)
        here = pl.ds(row, SUBLANES)

        def rows(of, plane):
            return cells[slot_of[of], place[plane], here, :]

        def beside(which, plane):
            return shifted[which, at, shifted_place[plane], pl.ds(row + PAD, SUBLANES), :]

        colour = transmit = None
        for plane in marched:
            before, centre, after = (rows(tile, plane + k) for k in (-1, 0, 1))
            left_tile = rows(tile - 1, plane)
            right_tile = rows(tile + 1, plane)
            if tile == 0:
                left_tile = left_tile * has_left
            if tile == all_tiles - 1:
                right_tile = right_tile * has_right
            left = pltpu.roll(jnp.where(last_lane, left_tile, centre), 1, 1)
            right = pltpu.roll(jnp.where(first_lane, right_tile, centre), LANES - 1, 1)
            diff_x = right - left
            diff_y = beside(1, plane) - beside(0, plane)
            diff_z = after - before
            inverse = lax.rsqrt(diff_x * diff_x + diff_y * diff_y + diff_z * diff_z + 1.0)
            facing = (factors[0] * diff_x + factors[1] * diff_y + factors[2] * diff_z) * inverse
            shading = jnp.maximum(facing, 0.0) + factors[3]
            weight = factors[4] - factors[5] * (inverse * inverse)
            middle_based = centre * scale + (scale - 0.5)
            interval = (middle_based + 0.5).astype(jnp.int32)
            offset = middle_based - interval.astype(jnp.float32)
            values = []
            for k in range(6):
                word = lookup(words[k], interval)
                rise = lax.shift_left(word, 16).astype(jnp.float32)
                values.append(word.astype(jnp.float32) + rise * offset)
            steps = [values[3 + ch] * weight for ch in range(3)]
            glows = [values[ch] * shading for ch in range(3)]
            if colour is None:
                colour = [step * glow for step, glow in zip(steps, glows)]
                transmit = [1.0 - step for step in steps]
            else:
                seen = [transmit[ch] * steps[ch] for ch in range(3)]
                colour = [colour[ch] + seen[ch] * glows[ch] for ch in range(3)]
                transmit = [transmit[ch] - seen[ch] for ch in range(3)]
            if mode == "rim" and plane == 0:
                held = [inner[at, k, here, :] for k in range(6)]
                colour = [colour[ch] + transmit[ch] * held[ch] for ch in range(3)]
                transmit = [transmit[ch] * held[3 + ch] for ch in range(3)]
        for k, value in enumerate(colour + transmit):
            if len(outs) == 1:
                canvas[at, k, here, :] = value
            else:
                block_rows = canvas.shape[4]
                block = (number * SUBLANES) // block_rows
                first = pl.multiple_of((number * SUBLANES) % block_rows, SUBLANES)
                canvas[at, piece, block, k, pl.ds(first, SUBLANES), :] = value

    for copy in incoming(0, True):
        copy.wait()

    @pl.loop(0, pieces)
    def _(piece):
        @pl.when(piece + 2 < pieces)
        def _():
            start(piece + 2)

        for copy in incoming(piece, False):
            copy.wait()

        @pl.when(piece + 1 < pieces)
        def _():
            for copy in incoming(piece + 1, True):
                copy.wait()

        @pl.when(piece + 1 == pieces)
        def _():
            for at in range(len(chunk)):
                shifted[1, at, :, pl.ds(PAD + height - 1, 1), :] = zeros

        for at in range(len(chunk)):

            @pl.loop(0, piece_rows // SUBLANES, unroll=4 if mode == "rim" else 2)
            def _(number):
                strip(at, piece, number)

        for copy in outgoing(piece):
            copy.start()

    @pl.loop(0, pieces)
    def _(piece):
        for copy in outgoing(piece):
            copy.wait()


def march(mode, chunk, tables, field, side, halos, middle, depth_total, part_shape):
    planes, height, width = field.shape
    tiles = len(chunk)
    near = {tile + k for tile in chunk for k in (-1, 0, 1)}
    extent = tiles * LANES
    marched = {"full": planes, "middle": planes - 2, "rim": 2}[mode]
    held = 6 if mode == "rim" else planes + 2
    if part_shape is None:
        group, pieces = 1, max(1, height // 64)
        outs = [jax.ShapeDtypeStruct((6, height, extent), jnp.float32)]
        canvas = (tiles, 6, height, LANES)
    else:
        pieces, group, rows = part_shape
        outs = [jax.ShapeDtypeStruct((pieces, 6, rows, extent), jnp.float32)] * group
        canvas = (tiles, pieces, group, 6, rows, LANES)
    scratch = [
        pltpu.VMEM((len(near), held, height, LANES), jnp.float32),
        pltpu.VMEM((2, tiles, marched, height + 2 * PAD, LANES), jnp.float32),
        pltpu.VMEM(canvas, jnp.float32),
        pltpu.VMEM((SUBLANES, LANES), jnp.float32),
        pltpu.VMEM((6, SUBLANES, LANES), jnp.int32),
        pltpu.VMEM((6, SUBLANES, LANES), jnp.float32),
        pltpu.SemaphoreType.DMA((pieces, 2 * len(near) + 7 * tiles)),
        pltpu.SemaphoreType.DMA((pieces, tiles + 1, group)),
    ]
    operands = [field]
    if min(near) < 0 or max(near) >= width // LANES:
        operands.append(side)
    if mode != "middle":
        operands += list(halos)
    if mode == "rim":
        operands.append(middle)
        scratch.append(pltpu.VMEM((tiles, 6, height, LANES), jnp.float32))
    if mode == "middle":
        outs.append(jax.ShapeDtypeStruct((planes, height, LANES), jnp.float32))
    weight = 100 if mode == "middle" else 20000
    far = pl.BlockSpec(memory_space=pltpu.HBM)
    out = pl.pallas_call(
        functools.partial(march_kernel, mode, chunk, depth_total, group),
        out_shape=outs,
        in_specs=[pl.BlockSpec(memory_space=pltpu.VMEM)] * 2 + [far] * len(operands),
        out_specs=[far] * len(outs),
        scratch_shapes=scratch,
        compiler_params=pltpu.CompilerParams(vmem_limit_bytes=60 * 1024 * 1024),
        cost_estimate=pl.CostEstimate(
            flops=planes * height * extent * weight,
            bytes_accessed=planes * height * extent * 5,
            transcendentals=0,
        ),
        name=f"march_{mode}_{chunk[0]}",
    )(*tables, *operands)
    return out[0] if len(out) == 1 else out


def plane_halos(first, last):
    count = lax.axis_size("slab")
    forward = [(i, i + 1) for i in range(count - 1)]
    backward = [(i + 1, i) for i in range(count - 1)]
    return lax.ppermute(last, "slab", forward), lax.ppermute(first, "slab", backward)


def ordered(is_far, own, other):
    near = [jnp.where(is_far, b, a) for a, b in zip(own, other)]
    far = [jnp.where(is_far, a, b) for a, b in zip(own, other)]
    return [near[0] + near[1] * far[0], near[1] * far[1]]


def exchange(parts, own, shift):
    count = lax.axis_size("slab")
    merged = []
    for change, part in enumerate(parts):
        if change:
            part = lax.ppermute(part, "slab", [(i, i ^ change << shift) for i in range(count)])
        merged.append([part[:, :3], part[:, 3:]])
    digit = 0
    while len(merged) > 1:
        is_far = (own >> digit & 1) == 1
        merged = [ordered(is_far, merged[k], merged[k + 1]) for k in range(0, len(merged), 2)]
        digit += 1
    return merged[0]


def reduce_image(image, parts, slab_index, block_rows):
    slab_count = lax.axis_size("slab")
    levels = slab_count.bit_length() - 1
    if parts is None:
        image = image.reshape((6, slab_count, block_rows, image.shape[-1]))
        image = jnp.swapaxes(image, 0, 1)
    for shift in range(0, levels, 2):
        size = 1 << min(2, levels - shift)
        own = (slab_index >> shift) & (size - 1)
        if parts is None:
            image = image.reshape((-1, size) + image.shape[1:])
            parts = [
                lax.dynamic_index_in_dim(image, own ^ change, 1, keepdims=False)
                for change in range(size)
            ]
        colour, transmit = exchange(parts, own, shift)
        image, parts = jnp.concatenate([colour, transmit], axis=1), None
    return colour[0], 1.0 - transmit[0]


def per_device(field, tf_emission, tf_absorption):
    slab_count = lax.axis_size("slab")
    slab_index = lax.axis_index("slab")
    planes, height, width = field.shape
    depth_total = planes * slab_count
    block_rows = height // slab_count
    tiles = width // LANES
    part_shape = None
    if slab_count >= 4 and block_rows % SUBLANES == 0:
        part_shape = (slab_count // 4, 4, block_rows)
    chunks = [tuple(range(1, tiles - 1)), (0, tiles - 1)]
    tables = (tf_emission, tf_absorption)

    halo = plane_halos(field[0], field[-1])
    results = []
    for number, chunk in enumerate(chunks):
        if number == 0:
            middle, edge = march(
                "middle", chunk, tables, field, None, None, None, depth_total, None
            )
            side = lax.ppermute(edge, "tile", [(0, 1), (1, 0)])
            mode = "rim"
        else:
            halo, side, _ = lax.optimization_barrier((halo, side, out))
            middle, mode = None, "full"
        out = march(mode, chunk, tables, field, side, halo, middle, depth_total, part_shape)
        image, parts = (out, None) if part_shape is None else (None, out)
        results.append(reduce_image(image, parts, slab_index, block_rows))
    gathered = []
    for inner, outer in zip(*results):
        gathered.append(
            jnp.concatenate([outer[:, :, :LANES], inner, outer[:, :, LANES:]], axis=2)
        )
    return tuple(gathered)


def solution(mesh):
    placed = (P("slab", None, "tile"), P(), P())
    return jax.shard_map(
        per_device,
        mesh=mesh,
        in_specs=placed,
        out_specs=(P(None, "slab", "tile"), P(None, "slab", "tile")),
        check_vma=False,
    )
```

```python
import functools

import jax
import jax.numpy as jnp
from jax import lax
from jax.experimental import pallas as pl
from jax.experimental.pallas import tpu as pltpu
from jax.sharding import PartitionSpec as P

LIGHT_DIR = (0.2672612, 0.5345225, 0.8017837)
LANES = 128
SUBLANES = 8
PAD = 8
WORD_SCALE = 2.0**31 - 2.0**17
HALF = 65536


def prepare_tables(emission, absorption, depth_total, table, words, factors):
    breaks = emission.shape[1]
    table[...] = jnp.zeros(table.shape, jnp.float32)
    table[0:3, 0:breaks] = emission[...]
    table[3:6, 0:breaks] = absorption[...]
    values = table[...]
    largest = [jnp.maximum(jnp.max(ref[...]), 1e-30) for ref in (emission, absorption)]
    row = lax.broadcasted_iota(jnp.int32, table.shape, 0)
    lane = lax.broadcasted_iota(jnp.int32, table.shape, 1)
    scaled = values * (WORD_SCALE / jnp.where(row < 3, largest[0], largest[1]))
    following = jnp.where(lane < breaks - 1, pltpu.roll(scaled, LANES - 1, 1), scaled)
    rise = jnp.floor((following - scaled) * (1.0 / HALF) + 0.5)
    upper = jnp.floor((0.5 * (following + scaled) - rise) * (1.0 / HALF) + 0.5)
    word = upper.astype(jnp.int32) * HALF + rise.astype(jnp.int32)
    units = [largest[0] / WORD_SCALE, largest[1] * (4.0 / depth_total) / WORD_SCALE]
    constants = [0.9 * part * units[0] for part in LIGHT_DIR]
    constants += [0.1 * units[0], units[1], 0.75 * units[1]]
    for k in range(6):
        words[k] = jnp.broadcast_to(word[k : k + 1, :], (SUBLANES, LANES))
        factors[k] = jnp.full((SUBLANES, LANES), constants[k], jnp.float32)


def lookup(table, index):
    return lax.gather(
        table,
        index.reshape(index.shape + (1,)),
        lax.GatherDimensionNumbers(
            offset_dims=(),
            collapsed_slice_dims=(1,),
            start_index_map=(1,),
            operand_batching_dims=(0,),
            start_indices_batching_dims=(0,),
        ),
        slice_sizes=(1, 1),
        mode=lax.GatherScatterMode.PROMISE_IN_BOUNDS,
    )


def march_kernel(mode, depth_total, group, emission, absorption, *refs):
    refs = list(refs)
    field = refs.pop(0)
    side = refs.pop(0) if mode == "outer" else None
    low, high = (refs.pop(0), refs.pop(0)) if mode != "middle" else (None, None)
    middle = refs.pop(0) if mode == "rim" else None
    inner = refs.pop() if mode == "rim" else None
    cells, canvas, table, words, factors, in_sems, out_sems = refs[-7:]
    outs = refs[:-7]
    edge = outs.pop() if mode == "middle" else None
    planes, height, width = field.shape
    scale = 0.5 * (emission.shape[1] - 1)
    piece_rows = height // in_sems.shape[0]
    pieces = height // piece_rows
    core = lax.axis_index("tile")
    tiles = cells.shape[0] - 2
    blocks = [(0, 1, planes)] if mode != "rim" else [(0, 1, 2), (planes - 2, 3, 2)]
    marched = {
        "outer": range(planes), "middle": range(1, planes - 1), "rim": (0, planes - 1)
    }[mode]
    place = {first + k: slot + k for first, slot, count in blocks for k in range(count)}
    place[-1] = 0
    place[planes] = max(place.values()) + 1
    far = (1 - core) * (tiles + 1)
    if mode == "outer":
        first_lane_taken, first_tile, taken = (1 - core) * (width - 2 * LANES), core, 2
    else:
        first_lane_taken, first_tile, taken = 0, 1 - core, width // LANES

    def incoming(piece):
        start = pl.multiple_of(piece * piece_rows, SUBLANES)
        body = pl.ds(start, piece_rows)
        padded = pl.ds(start + PAD, piece_rows)
        pairs = []
        for k in range(taken):
            lanes = pl.ds(pl.multiple_of(first_lane_taken + k * LANES, LANES), LANES)
            held = cells.at[first_tile + k]
            for first, where, count in blocks:
                target = held.at[pl.ds(where, count), padded, :]
                pairs.append((field.at[pl.ds(first, count), body, lanes], target))
            if mode != "middle":
                for halo, plane in ((low, -1), (high, planes)):
                    pairs.append((halo.at[body, lanes], held.at[place[plane], padded, :]))
        if mode == "rim":
            pairs.append((middle.at[:, body, :], inner.at[:, body, :]))
        if mode == "outer":
            pairs.append((side.at[:, body, :], cells.at[far, pl.ds(1, planes), padded, :]))
        return [
            pltpu.make_async_copy(source, target, in_sems.at[piece, k])
            for k, (source, target) in enumerate(pairs)
        ]

    def outgoing(piece):
        start = pl.multiple_of(piece * piece_rows, SUBLANES)
        body = pl.ds(start, piece_rows)
        if len(outs) == 1:
            pairs = [(canvas.at[:, body, :], outs[0].at[:, body, :])]
        else:
            own = lax.axis_index("slab") & (group - 1)
            pairs = [(canvas.at[piece, own ^ k], outs[k].at[piece]) for k in range(group)]
        if edge is not None:
            padded = pl.ds(start + PAD, piece_rows)
            pairs.append((cells.at[far, pl.ds(1, planes), padded, :], edge.at[:, body, :]))
        return [
            pltpu.make_async_copy(source, target, out_sems.at[piece, k])
            for k, (source, target) in enumerate(pairs)
        ]

    def start(piece):
        for copy in incoming(piece):
            copy.start()

    def await_piece(piece):
        for copy in incoming(piece):
            copy.wait()

    for piece in range(min(3, pieces)):
        start(piece)
    prepare_tables(emission, absorption, depth_total, table, words, factors)
    zeros = jnp.zeros((1, LANES), jnp.float32)
    for tile in range(1, tiles + 1):
        for plane in marched:
            cells[tile, place[plane], pl.ds(PAD - 1, 1), :] = zeros
            cells[tile, place[plane], pl.ds(PAD + height, 1), :] = zeros
    if mode != "outer":
        blank = jnp.zeros((height, LANES), jnp.float32)
        for plane in marched:
            cells[core * (tiles + 1), place[plane], pl.ds(PAD, height), :] = blank

    lane = lax.broadcasted_iota(jnp.int32, (SUBLANES, LANES), 1)
    first_lane = lane == 0
    last_lane = lane == LANES - 1

    def strip(at, piece, number):
        row = pl.multiple_of(piece * piece_rows + number * SUBLANES, SUBLANES)

        def rows(tile, plane, offset=0):
            here = pl.ds(row + PAD + offset, SUBLANES)
            return cells[tile + 1, place[plane], here, :]

        colour = transmit = None
        for plane in marched:
            before, centre, after = (rows(at, plane + k) for k in (-1, 0, 1))
            left = pltpu.roll(jnp.where(last_lane, rows(at - 1, plane), centre), 1, 1)
            right = pltpu.roll(jnp.where(first_lane, rows(at + 1, plane), centre), LANES - 1, 1)
            diff_x = right - left
            diff_y = rows(at, plane, 1) - rows(at, plane, -1)
            diff_z = after - before
            inverse = lax.rsqrt(diff_x * diff_x + diff_y * diff_y + diff_z * diff_z + 1.0)
            facing = (factors[0] * diff_x + factors[1] * diff_y + factors[2] * diff_z) * inverse
            shading = jnp.maximum(facing, 0.0) + factors[3]
            weight = factors[4] - factors[5] * (inverse * inverse)
            middle_based = centre * scale + (scale - 0.5)
            interval = (middle_based + 0.5).astype(jnp.int32)
            offset = middle_based - interval.astype(jnp.float32)
            values = []
            for k in range(6):
                word = lookup(words[k], interval)
                rise = lax.shift_left(word, 16).astype(jnp.float32)
                values.append(word.astype(jnp.float32) + rise * offset)
            steps = [values[3 + ch] * weight for ch in range(3)]
            glows = [values[ch] * shading for ch in range(3)]
            if colour is None:
                colour = [step * glow for step, glow in zip(steps, glows)]
                transmit = [1.0 - step for step in steps]
            else:
                seen = [transmit[ch] * steps[ch] for ch in range(3)]
                colour = [colour[ch] + seen[ch] * glows[ch] for ch in range(3)]
                transmit = [transmit[ch] - seen[ch] for ch in range(3)]
            if mode == "rim" and plane == 0:
                held = [
                    inner[k, pl.ds(row, SUBLANES), pl.ds(at * LANES, LANES)] for k in range(6)
                ]
                colour = [colour[ch] + transmit[ch] * held[ch] for ch in range(3)]
                transmit = [transmit[ch] * held[3 + ch] for ch in range(3)]
        here = pl.ds(at * LANES, LANES)
        for k, value in enumerate(colour + transmit):
            if len(outs) == 1:
                canvas[k, pl.ds(row, SUBLANES), here] = value
            else:
                block_rows = canvas.shape[3]
                block = (number * SUBLANES) // block_rows
                first = pl.multiple_of((number * SUBLANES) % block_rows, SUBLANES)
                canvas[piece, block, k, pl.ds(first, SUBLANES), here] = value

    await_piece(0)

    @pl.loop(0, pieces)
    def _(piece):
        @pl.when(piece + 3 < pieces)
        def _():
            start(piece + 3)

        @pl.when(piece + 1 < pieces)
        def _():
            await_piece(piece + 1)

        @pl.loop(0, piece_rows // SUBLANES)
        def _(number):
            for at in range(tiles):
                strip(at, piece, number)

        for copy in outgoing(piece):
            copy.start()

    @pl.loop(0, pieces)
    def _(piece):
        for copy in outgoing(piece):
            copy.wait()


def march(mode, tables, field, side, halos, middle, depth_total, part_shape):
    planes, height, width = field.shape
    extent = LANES if mode == "outer" else width - LANES
    marched = {"outer": planes, "middle": planes - 2, "rim": 2}[mode]
    held = 6 if mode == "rim" else planes + 2
    if part_shape is None:
        group, pieces = 1, max(1, height // 64)
        outs = [jax.ShapeDtypeStruct((6, height, extent), jnp.float32)]
        canvas = (6, height, extent)
    else:
        pieces, group, rows = part_shape
        outs = [jax.ShapeDtypeStruct((pieces, 6, rows, extent), jnp.float32)] * group
        canvas = (pieces, group, 6, rows, extent)
    scratch = [
        pltpu.VMEM((extent // LANES + 2, held, height + 2 * PAD, LANES), jnp.float32),
        pltpu.VMEM(canvas, jnp.float32),
        pltpu.VMEM((SUBLANES, LANES), jnp.float32),
        pltpu.VMEM((6, SUBLANES, LANES), jnp.int32),
        pltpu.VMEM((6, SUBLANES, LANES), jnp.float32),
        pltpu.SemaphoreType.DMA((pieces, 4 * (width // LANES) + 1)),
        pltpu.SemaphoreType.DMA((pieces, group + 1)),
    ]
    operands = [field]
    if mode == "outer":
        operands.append(side)
    if mode != "middle":
        operands += list(halos)
    if mode == "rim":
        operands.append(middle)
        scratch.append(pltpu.VMEM((6, height, extent), jnp.float32))
    if mode == "middle":
        outs.append(jax.ShapeDtypeStruct((planes, height, LANES), jnp.float32))
    weight = 100 if mode == "middle" else 20000
    distant = pl.BlockSpec(memory_space=pltpu.HBM)
    out = pl.pallas_call(
        functools.partial(march_kernel, mode, depth_total, group),
        out_shape=outs,
        in_specs=[pl.BlockSpec(memory_space=pltpu.VMEM)] * 2 + [distant] * len(operands),
        out_specs=[distant] * len(outs),
        scratch_shapes=scratch,
        compiler_params=pltpu.CompilerParams(vmem_limit_bytes=60 * 1024 * 1024),
        cost_estimate=pl.CostEstimate(
            flops=planes * height * 256 * weight,
            bytes_accessed=planes * height * 256 * 5,
            transcendentals=0,
        ),
        name=f"march_{mode}",
    )(*tables, *operands)
    return out[0] if len(out) == 1 else out


def plane_halos(first, last):
    count = lax.axis_size("slab")
    forward = [(i, i + 1) for i in range(count - 1)]
    backward = [(i + 1, i) for i in range(count - 1)]
    return lax.ppermute(last, "slab", forward), lax.ppermute(first, "slab", backward)


def ordered(is_far, own, other):
    near = [jnp.where(is_far, b, a) for a, b in zip(own, other)]
    far = [jnp.where(is_far, a, b) for a, b in zip(own, other)]
    return [near[0] + near[1] * far[0], near[1] * far[1]]


def exchange(parts, own, shift):
    count = lax.axis_size("slab")
    merged = []
    for change, part in enumerate(parts):
        if change:
            part = lax.ppermute(part, "slab", [(i, i ^ change << shift) for i in range(count)])
        merged.append([part[:, :3], part[:, 3:]])
    digit = 0
    while len(merged) > 1:
        is_far = (own >> digit & 1) == 1
        merged = [ordered(is_far, merged[k], merged[k + 1]) for k in range(0, len(merged), 2)]
        digit += 1
    return merged[0]


def reduce_image(image, parts, slab_index, block_rows):
    slab_count = lax.axis_size("slab")
    levels = slab_count.bit_length() - 1
    if parts is None:
        image = image.reshape((6, slab_count, block_rows, image.shape[-1]))
        image = jnp.swapaxes(image, 0, 1)
    for shift in range(0, levels, 2):
        size = 1 << min(2, levels - shift)
        own = (slab_index >> shift) & (size - 1)
        if parts is None:
            image = image.reshape((-1, size) + image.shape[1:])
            parts = [
                lax.dynamic_index_in_dim(image, own ^ change, 1, keepdims=False)
                for change in range(size)
            ]
        colour, transmit = exchange(parts, own, shift)
        image, parts = jnp.concatenate([colour, transmit], axis=1), None
    return colour[0], 1.0 - transmit[0]


def per_device(field, tf_emission, tf_absorption):
    slab_count = lax.axis_size("slab")
    slab_index = lax.axis_index("slab")
    planes, height, width = field.shape
    depth_total = planes * slab_count
    block_rows = height // slab_count
    part_shape = None
    if slab_count >= 4 and block_rows % SUBLANES == 0:
        part_shape = (slab_count // 4, 4, block_rows)
    tables = (tf_emission, tf_absorption)

    def reduced(out):
        image, parts = (out, None) if part_shape is None else (None, out)
        return reduce_image(image, parts, slab_index, block_rows)

    halo = plane_halos(field[0], field[-1])
    middle, edge = march("middle", tables, field, None, None, None, depth_total, None)
    side = lax.ppermute(edge, "tile", [(0, 1), (1, 0)])
    rim = march("rim", tables, field, None, halo, middle, depth_total, part_shape)
    halo, side, _ = lax.optimization_barrier((halo, side, rim))
    outer = march("outer", tables, field, side, halo, None, depth_total, part_shape)
    first_core = lax.axis_index("tile") == 0
    return tuple(
        jnp.where(
            first_core,
            jnp.concatenate([wide, narrow], axis=2),
            jnp.concatenate([narrow, wide], axis=2),
        )
        for wide, narrow in zip(reduced(rim), reduced(outer))
    )


def solution(mesh):
    placed = (P("slab", None, "tile"), P(), P())
    return jax.shard_map(
        per_device,
        mesh=mesh,
        in_specs=placed,
        out_specs=(P(None, "slab", "tile"), P(None, "slab", "tile")),
        check_vma=False,
    )
```

```python
import functools

import jax
import jax.numpy as jnp
from jax import lax
from jax.experimental import pallas as pl
from jax.experimental.pallas import tpu as pltpu
from jax.sharding import PartitionSpec as P

LIGHT_DIR = (0.2672612, 0.5345225, 0.8017837)
LANES = 128
SUBLANES = 8
PAD = 8
WORD_SCALE = 2.0**31 - 2.0**17
HALF = 65536


def prepare_tables(emission, absorption, depth_total, table, words, factors):
    breaks = emission.shape[1]
    table[...] = jnp.zeros(table.shape, jnp.float32)
    table[0:3, 0:breaks] = emission[...]
    table[3:6, 0:breaks] = absorption[...]
    values = table[...]
    largest = [jnp.maximum(jnp.max(ref[...]), 1e-30) for ref in (emission, absorption)]
    row = lax.broadcasted_iota(jnp.int32, table.shape, 0)
    lane = lax.broadcasted_iota(jnp.int32, table.shape, 1)
    scaled = values * (WORD_SCALE / jnp.where(row < 3, largest[0], largest[1]))
    following = jnp.where(lane < breaks - 1, pltpu.roll(scaled, LANES - 1, 1), scaled)
    rise = jnp.floor((following - scaled) * (1.0 / HALF) + 0.5)
    upper = jnp.floor((0.5 * (following + scaled) - rise) * (1.0 / HALF) + 0.5)
    word = upper.astype(jnp.int32) * HALF + rise.astype(jnp.int32)
    units = [largest[0] / WORD_SCALE, largest[1] * (4.0 / depth_total) / WORD_SCALE]
    constants = [0.9 * part * units[0] for part in LIGHT_DIR]
    constants += [0.1 * units[0], units[1], 0.75 * units[1]]
    for k in range(6):
        words[k] = jnp.broadcast_to(word[k : k + 1, :], (SUBLANES, LANES))
        factors[k] = jnp.full((SUBLANES, LANES), constants[k], jnp.float32)


def lookup(table, index):
    return lax.gather(
        table,
        index.reshape(index.shape + (1,)),
        lax.GatherDimensionNumbers(
            offset_dims=(),
            collapsed_slice_dims=(1,),
            start_index_map=(1,),
            operand_batching_dims=(0,),
            start_indices_batching_dims=(0,),
        ),
        slice_sizes=(1, 1),
        mode=lax.GatherScatterMode.PROMISE_IN_BOUNDS,
    )


def march_kernel(mode, depth_total, group, emission, absorption, *refs):
    refs = list(refs)
    field = refs.pop(0)
    side = refs.pop(0) if mode == "outer" else None
    low, high = (refs.pop(0), refs.pop(0)) if mode != "middle" else (None, None)
    rim = mode in ("rim", "inner rim")
    middle = refs.pop(0) if rim else None
    inner = refs.pop() if rim else None
    cells, canvas, table, words, factors, in_sems, out_sems = refs[-7:]
    outs = refs[:-7]
    edge = outs.pop() if mode == "middle" else None
    planes, height, width = field.shape
    scale = 0.5 * (emission.shape[1] - 1)
    piece_rows = height // in_sems.shape[0]
    pieces = height // piece_rows
    core = lax.axis_index("tile")
    tiles = cells.shape[0] - 2
    computed = (1, tiles) if mode == "rim" else range(1, tiles + 1)
    blocks = [(0, 1, 2), (planes - 2, 3, 2)] if rim else [(0, 1, planes)]
    if rim:
        marched = (0, planes - 1)
    else:
        marched = range(1, planes - 1) if mode == "middle" else range(planes)
    place = {first + k: slot + k for first, slot, count in blocks for k in range(count)}
    place[-1] = 0
    place[planes] = max(place.values()) + 1
    far = (1 - core) * (tiles + 1)
    if mode == "outer":
        first_lane_taken, first_tile, taken = (1 - core) * (width - 2 * LANES), core, 2
    elif mode == "inner rim":
        first_lane_taken, first_tile, taken = core * LANES, 0, tiles + 2
    else:
        first_lane_taken, first_tile, taken = 0, 1 - core, width // LANES

    def incoming(piece):
        start = pl.multiple_of(piece * piece_rows, SUBLANES)
        body = pl.ds(start, piece_rows)
        padded = pl.ds(start + PAD, piece_rows)
        pairs = []
        for k in range(taken):
            lanes = pl.ds(pl.multiple_of(first_lane_taken + k * LANES, LANES), LANES)
            held = cells.at[first_tile + k]
            for first, where, count in blocks:
                target = held.at[pl.ds(where, count), padded, :]
                pairs.append((field.at[pl.ds(first, count), body, lanes], target))
            if mode != "middle":
                for halo, plane in ((low, -1), (high, planes)):
                    pairs.append((halo.at[body, lanes], held.at[place[plane], padded, :]))
        if rim:
            skipped = 1 if mode == "inner rim" else 0
            for at, tile in enumerate(computed):
                lanes = pl.ds((tile - 1 + skipped) * LANES, LANES)
                held = inner.at[:, body, pl.ds(at * LANES, LANES)]
                pairs.append((middle.at[:, body, lanes], held))
        if mode == "outer":
            pairs.append((side.at[:, body, :], cells.at[far, pl.ds(1, planes), padded, :]))
        return [
            pltpu.make_async_copy(source, target, in_sems.at[piece, k])
            for k, (source, target) in enumerate(pairs)
        ]

    def outgoing(piece):
        start = pl.multiple_of(piece * piece_rows, SUBLANES)
        body = pl.ds(start, piece_rows)
        if not group:
            pairs = [(canvas.at[:, body, :], outs[0].at[:, body, :])]
        else:
            pairs = [(canvas.at[piece], outs[0].at[:, piece])]
        if edge is not None:
            padded = pl.ds(start + PAD, piece_rows)
            pairs.append((cells.at[far, pl.ds(1, planes), padded, :], edge.at[:, body, :]))
        return [
            pltpu.make_async_copy(source, target, out_sems.at[piece, k])
            for k, (source, target) in enumerate(pairs)
        ]

    def start(piece):
        for copy in incoming(piece):
            copy.start()

    def await_piece(piece):
        for copy in incoming(piece):
            copy.wait()

    for piece in range(min(2, pieces)):
        start(piece)
    prepare_tables(emission, absorption, depth_total, table, words, factors)
    zeros = jnp.zeros((1, LANES), jnp.float32)
    for tile in computed:
        for plane in marched:
            cells[tile, place[plane], pl.ds(PAD - 1, 1), :] = zeros
            cells[tile, place[plane], pl.ds(PAD + height, 1), :] = zeros
    if mode in ("middle", "rim"):
        blank = jnp.zeros((height, LANES), jnp.float32)
        for plane in marched:
            cells[core * (tiles + 1), place[plane], pl.ds(PAD, height), :] = blank

    lane = lax.broadcasted_iota(jnp.int32, (SUBLANES, LANES), 1)
    first_lane = lane == 0
    last_lane = lane == LANES - 1

    def strip(at, tile, piece, number):
        row = pl.multiple_of(piece * piece_rows + number * SUBLANES, SUBLANES)

        def rows(tile, plane, offset=0):
            here = pl.ds(row + PAD + offset, SUBLANES)
            return cells[tile, place[plane], here, :]

        colour = transmit = None
        for plane in marched:
            before, centre, after = (rows(tile, plane + k) for k in (-1, 0, 1))
            left = pltpu.roll(jnp.where(last_lane, rows(tile - 1, plane), centre), 1, 1)
            right = pltpu.roll(jnp.where(first_lane, rows(tile + 1, plane), centre), LANES - 1, 1)
            diff_x = right - left
            diff_y = rows(tile, plane, 1) - rows(tile, plane, -1)
            diff_z = after - before
            inverse = lax.rsqrt(diff_x * diff_x + diff_y * diff_y + diff_z * diff_z + 1.0)
            facing = (factors[0] * diff_x + factors[1] * diff_y + factors[2] * diff_z) * inverse
            shading = jnp.maximum(facing, 0.0) + factors[3]
            weight = factors[4] - factors[5] * (inverse * inverse)
            middle_based = centre * scale + (scale - 0.5)
            interval = (middle_based + 0.5).astype(jnp.int32)
            offset = middle_based - interval.astype(jnp.float32)
            values = []
            for k in range(6):
                word = lookup(words[k], interval)
                rise = lax.shift_left(word, 16).astype(jnp.float32)
                values.append(word.astype(jnp.float32) + rise * offset)
            steps = [values[3 + ch] * weight for ch in range(3)]
            glows = [values[ch] * shading for ch in range(3)]
            if colour is None:
                colour = [step * glow for step, glow in zip(steps, glows)]
                transmit = [1.0 - step for step in steps]
            else:
                seen = [transmit[ch] * steps[ch] for ch in range(3)]
                colour = [colour[ch] + seen[ch] * glows[ch] for ch in range(3)]
                transmit = [transmit[ch] - seen[ch] for ch in range(3)]
            if rim and plane == 0:
                held = [
                    inner[k, pl.ds(row, SUBLANES), pl.ds(at * LANES, LANES)] for k in range(6)
                ]
                colour = [colour[ch] + transmit[ch] * held[ch] for ch in range(3)]
                transmit = [transmit[ch] * held[3 + ch] for ch in range(3)]
        here = pl.ds(at * LANES, LANES)
        for k, value in enumerate(colour + transmit):
            if not group:
                canvas[k, pl.ds(row, SUBLANES), here] = value
            else:
                block_rows = canvas.shape[3]
                block = (number * SUBLANES) // block_rows
                first = pl.multiple_of((number * SUBLANES) % block_rows, SUBLANES)
                canvas[piece, block, k, pl.ds(first, SUBLANES), here] = value

    await_piece(0)

    @pl.loop(0, pieces)
    def _(piece):
        @pl.when(piece + 2 < pieces)
        def _():
            start(piece + 2)

        @pl.loop(0, piece_rows // SUBLANES)
        def _(number):
            @pl.when((number == piece_rows // SUBLANES - 1) & (piece + 1 < pieces))
            def _():
                await_piece(piece + 1)

            for at, tile in enumerate(computed):
                strip(at, tile, piece, number)

        for copy in outgoing(piece):
            copy.start()

    @pl.loop(0, pieces)
    def _(piece):
        for copy in outgoing(piece):
            copy.wait()


def march(mode, tables, field, side, halos, middle, depth_total, part_shape):
    planes, height, width = field.shape
    rim = mode in ("rim", "inner rim")
    tiles = width // LANES - 1
    tiles_held = {"outer": 3, "inner rim": tiles}.get(mode, tiles + 2)
    extent = {"outer": 1, "rim": 2, "inner rim": tiles - 2, "middle": tiles}[mode] * LANES
    held = 6 if rim else planes + 2
    if part_shape is None:
        group, pieces = 0, max(1, height // 64)
        outs = [jax.ShapeDtypeStruct((6, height, extent), jnp.float32)]
        canvas = (6, height, extent)
    else:
        pieces, group, rows = part_shape
        outs = [jax.ShapeDtypeStruct((group, pieces, 6, rows, extent), jnp.float32)]
        canvas = (pieces, group, 6, rows, extent)
    scratch = [
        pltpu.VMEM((tiles_held, held, height + 2 * PAD, LANES), jnp.float32),
        pltpu.VMEM(canvas, jnp.float32),
        pltpu.VMEM((SUBLANES, LANES), jnp.float32),
        pltpu.VMEM((6, SUBLANES, LANES), jnp.int32),
        pltpu.VMEM((6, SUBLANES, LANES), jnp.float32),
        pltpu.SemaphoreType.DMA((pieces, 4 * tiles_held + 2)),
        pltpu.SemaphoreType.DMA((pieces, 2)),
    ]
    operands = [field]
    if mode == "outer":
        operands.append(side)
    if mode != "middle":
        operands += list(halos)
    if rim:
        operands.append(middle)
        scratch.append(pltpu.VMEM((6, height, extent), jnp.float32))
    if mode == "middle":
        outs.append(jax.ShapeDtypeStruct((planes, height, LANES), jnp.float32))
    weight = 100 if mode == "middle" else 20000
    distant = pl.BlockSpec(memory_space=pl.ANY)
    out = pl.pallas_call(
        functools.partial(march_kernel, mode, depth_total, group),
        out_shape=outs,
        in_specs=[pl.BlockSpec(memory_space=pltpu.VMEM)] * 2 + [distant] * len(operands),
        out_specs=[distant] * len(outs),
        scratch_shapes=scratch,
        compiler_params=pltpu.CompilerParams(vmem_limit_bytes=56 * 1024 * 1024),
        cost_estimate=pl.CostEstimate(
            flops=planes * height * 256 * weight,
            bytes_accessed=planes * height * 256 * 5,
            transcendentals=0,
        ),
        name="march_" + mode.replace(" ", "_"),
    )(*tables, *operands)
    return out[0] if len(out) == 1 else out


def plane_halos(first, last):
    count = lax.axis_size("slab")
    forward = [(i, i + 1) for i in range(count - 1)]
    backward = [(i + 1, i) for i in range(count - 1)]
    return lax.ppermute(last, "slab", forward), lax.ppermute(first, "slab", backward)


def composite(parts):
    total = parts[-1]
    for k in range(parts.shape[0] - 2, -1, -1):
        colour, transmit = parts[k, :, :3], parts[k, :, 3:]
        total = jnp.concatenate(
            [colour + transmit * total[:, :3], transmit * total[:, 3:]], axis=1
        )
    return total


def reduce_image(image, split, block_rows):
    slab_count = lax.axis_size("slab")
    levels = slab_count.bit_length() - 1
    if not split:
        image = image.reshape((6, slab_count, block_rows, image.shape[-1]))
        image = jnp.swapaxes(image, 0, 1)
    for shift in range(0, levels, 2):
        size = 1 << min(2, levels - shift)
        if shift or not split:
            image = image.reshape((-1, size) + image.shape[1:])
            image = jnp.moveaxis(image, 1, 0)
        groups = [
            [i + (k << shift) for k in range(size)]
            for i in range(slab_count)
            if not i >> shift & (size - 1)
        ]
        image = lax.all_to_all(image, "slab", 0, 0, axis_index_groups=groups)
        image = composite(image)
    return image[0, :3], 1.0 - image[0, 3:]


def per_device(field, tf_emission, tf_absorption):
    slab_count = lax.axis_size("slab")
    planes, height, width = field.shape
    depth_total = planes * slab_count
    block_rows = height // slab_count
    part_shape = None
    if slab_count >= 4 and block_rows % SUBLANES == 0:
        part_shape = (slab_count // 4, 4, block_rows)
    tables = (tf_emission, tf_absorption)

    halo = plane_halos(field[0], field[-1])
    middle, edge = march("middle", tables, field, None, None, None, depth_total, None)
    side = lax.ppermute(edge, "tile", [(0, 1), (1, 0)])
    results = []
    for mode in ("inner rim", "rim", "outer"):
        if results:
            halo, side, _ = lax.optimization_barrier((halo, side, out))
        out = march(mode, tables, field, side, halo, middle, depth_total, part_shape)
        results.append(reduce_image(out, part_shape is not None, block_rows))
    first_core = lax.axis_index("tile") == 0
    gathered = []
    for inner, ends, outer in zip(*results):
        wide = [ends[:, :, :LANES], inner, ends[:, :, LANES:]]
        gathered.append(
            jnp.where(
                first_core,
                jnp.concatenate(wide + [outer], axis=2),
                jnp.concatenate([outer] + wide, axis=2),
            )
        )
    return tuple(gathered)


def solution(mesh):
    placed = (P("slab", None, "tile"), P(), P())
    return jax.shard_map(
        per_device,
        mesh=mesh,
        in_specs=placed,
        out_specs=(P(None, "slab", "tile"), P(None, "slab", "tile")),
        check_vma=False,
    )
```

```python
import functools

import jax
import jax.numpy as jnp
from jax import lax
from jax.experimental import pallas as pl
from jax.experimental.pallas import tpu as pltpu
from jax.sharding import PartitionSpec as P

LIGHT_DIR = (0.2672612, 0.5345225, 0.8017837)
LANES = 128
SUBLANES = 8
PAD = 8
WORD_SCALE = 2.0**31 - 2.0**17
HALF = 65536


def prepare_tables(emission, absorption, depth_total, table, words, factors):
    breaks = emission.shape[1]
    table[...] = jnp.zeros(table.shape, jnp.float32)
    table[0:3, 0:breaks] = emission[...]
    table[3:6, 0:breaks] = absorption[...]
    values = table[...]
    largest = [jnp.maximum(jnp.max(ref[...]), 1e-30) for ref in (emission, absorption)]
    row = lax.broadcasted_iota(jnp.int32, table.shape, 0)
    lane = lax.broadcasted_iota(jnp.int32, table.shape, 1)
    scaled = values * (WORD_SCALE / jnp.where(row < 3, largest[0], largest[1]))
    following = jnp.where(lane < breaks - 1, pltpu.roll(scaled, LANES - 1, 1), scaled)
    rise = jnp.floor((following - scaled) * (1.0 / HALF) + 0.5)
    upper = jnp.floor((0.5 * (following + scaled) - rise) * (1.0 / HALF) + 0.5)
    word = upper.astype(jnp.int32) * HALF + rise.astype(jnp.int32)
    units = [largest[0] / WORD_SCALE, largest[1] * (4.0 / depth_total) / WORD_SCALE]
    constants = [0.9 * part * units[0] for part in LIGHT_DIR]
    constants += [0.1 * units[0], units[1], 0.75 * units[1]]
    for k in range(6):
        words[k] = jnp.broadcast_to(word[k : k + 1, :], (SUBLANES, LANES))
        factors[k] = jnp.full((SUBLANES, LANES), constants[k], jnp.float32)


def lookup(table, index):
    return lax.gather(
        table,
        index.reshape(index.shape + (1,)),
        lax.GatherDimensionNumbers(
            offset_dims=(),
            collapsed_slice_dims=(1,),
            start_index_map=(1,),
            operand_batching_dims=(0,),
            start_indices_batching_dims=(0,),
        ),
        slice_sizes=(1, 1),
        mode=lax.GatherScatterMode.PROMISE_IN_BOUNDS,
    )


def march_kernel(mode, depth_total, group, scale, unroll, pieces, tables_a, tables_b, *refs):
    refs = list(refs)
    field = refs.pop(0)
    side = refs.pop(0) if mode == "outer" else None
    low, high = (refs.pop(0), refs.pop(0)) if mode != "middle" else (None, None)
    rim = mode == "rim"
    middle = refs.pop(0) if rim else None
    inner = refs.pop() if rim else None
    cells, canvas, table, in_sems, out_sems = refs[-5:]
    outs = refs[:-5]
    if mode == "middle":
        edge, words, factors = outs[-3:]
        outs = outs[:-3]
    else:
        edge, words, factors = None, tables_a, tables_b
    planes, height, width = field.shape
    piece_rows = height // pieces
    in_pieces = in_sems.shape[0]
    core = lax.axis_index("tile")
    tiles = cells.shape[0] - 2
    computed = range(1, tiles + 1)
    blocks = [(0, 1, 2), (planes - 2, 3, 2)] if rim else [(0, 1, planes)]
    if rim:
        marched = (0, planes - 1)
    else:
        marched = range(1, planes - 1) if mode == "middle" else range(planes)
    place = {first + k: slot + k for first, slot, count in blocks for k in range(count)}
    place[-1] = 0
    place[planes] = max(place.values()) + 1
    far = (1 - core) * (tiles + 1)
    if mode == "outer":
        first_lane_taken, first_tile, taken = (1 - core) * (width - 2 * LANES), core, 2
    else:
        first_lane_taken, first_tile, taken = 0, 1 - core, width // LANES

    def incoming(piece):
        in_rows = height // in_pieces
        start = pl.multiple_of(piece * in_rows, SUBLANES)
        body = pl.ds(start, in_rows)
        padded = pl.ds(start + PAD, in_rows)
        pairs = []
        for k in range(taken):
            lanes = pl.ds(pl.multiple_of(first_lane_taken + k * LANES, LANES), LANES)
            held = cells.at[first_tile + k]
            for first, where, count in blocks:
                target = held.at[pl.ds(where, count), padded, :]
                pairs.append((field.at[pl.ds(first, count), body, lanes], target))
            if mode != "middle":
                for halo, plane in ((low, -1), (high, planes)):
                    pairs.append((halo.at[body, lanes], held.at[place[plane], padded, :]))
        if rim:
            pairs.append((middle.at[:, body, :], inner.at[:, body, :]))
        if mode == "outer":
            pairs.append((side.at[:, body, :], cells.at[far, pl.ds(1, planes), padded, :]))
        return [
            pltpu.make_async_copy(source, target, in_sems.at[piece, k])
            for k, (source, target) in enumerate(pairs)
        ]

    def outgoing(piece):
        start = pl.multiple_of(piece * piece_rows, SUBLANES)
        body = pl.ds(start, piece_rows)
        if len(outs) == 1:
            pairs = [(canvas.at[:, body, :], outs[0].at[:, body, :])]
        else:
            own = lax.axis_index("slab") & (group - 1)
            pairs = [(canvas.at[piece, own ^ k], outs[k].at[piece]) for k in range(group)]
        if edge is not None:
            padded = pl.ds(start + PAD, piece_rows)
            pairs.append((cells.at[far, pl.ds(1, planes), padded, :], edge.at[:, body, :]))
        return [
            pltpu.make_async_copy(source, target, out_sems.at[piece, k])
            for k, (source, target) in enumerate(pairs)
        ]

    def start(piece):
        for copy in incoming(piece):
            copy.start()

    def await_piece(piece):
        for copy in incoming(piece):
            copy.wait()

    for piece in range(min(2, in_pieces)):
        start(piece)
    if mode == "middle":
        prepare_tables(tables_a, tables_b, depth_total, table, words, factors)
    zeros = jnp.zeros((1, LANES), jnp.float32)
    for tile in computed:
        for plane in marched:
            cells[tile, place[plane], pl.ds(PAD - 1, 1), :] = zeros
            cells[tile, place[plane], pl.ds(PAD + height, 1), :] = zeros
    if mode != "outer":
        blank = jnp.zeros((height, LANES), jnp.float32)
        for plane in marched:
            cells[core * (tiles + 1), place[plane], pl.ds(PAD, height), :] = blank

    lane = lax.broadcasted_iota(jnp.int32, (SUBLANES, LANES), 1)
    first_lane = lane == 0
    last_lane = lane == LANES - 1

    def strip(at, tile, piece, number):
        row = pl.multiple_of(piece * piece_rows + number * SUBLANES, SUBLANES)

        def rows(tile, plane, offset=0):
            here = pl.ds(row + PAD + offset, SUBLANES)
            return cells[tile, place[plane], here, :]

        colour = transmit = None
        for plane in marched:
            before, centre, after = (rows(tile, plane + k) for k in (-1, 0, 1))
            left = pltpu.roll(jnp.where(last_lane, rows(tile - 1, plane), centre), 1, 1)
            right = pltpu.roll(jnp.where(first_lane, rows(tile + 1, plane), centre), LANES - 1, 1)
            diff_x = right - left
            diff_y = rows(tile, plane, 1) - rows(tile, plane, -1)
            diff_z = after - before
            inverse = lax.rsqrt(diff_x * diff_x + diff_y * diff_y + diff_z * diff_z + 1.0)
            facing = (factors[0] * diff_x + factors[1] * diff_y + factors[2] * diff_z) * inverse
            shading = jnp.maximum(facing, 0.0) + factors[3]
            weight = factors[4] - factors[5] * (inverse * inverse)
            middle_based = centre * scale + (scale - 0.5)
            interval = (middle_based + 0.5).astype(jnp.int32)
            offset = middle_based - interval.astype(jnp.float32)
            values = []
            for k in range(6):
                word = lookup(words[k], interval)
                rise = lax.shift_left(word, 16).astype(jnp.float32)
                values.append(word.astype(jnp.float32) + rise * offset)
            steps = [values[3 + ch] * weight for ch in range(3)]
            glows = [values[ch] * shading for ch in range(3)]
            if colour is None:
                colour = [step * glow for step, glow in zip(steps, glows)]
                transmit = [1.0 - step for step in steps]
            else:
                seen = [transmit[ch] * steps[ch] for ch in range(3)]
                colour = [colour[ch] + seen[ch] * glows[ch] for ch in range(3)]
                transmit = [transmit[ch] - seen[ch] for ch in range(3)]
            if rim and plane == 0:
                held = [
                    inner[k, pl.ds(row, SUBLANES), pl.ds(at * LANES, LANES)] for k in range(6)
                ]
                colour = [colour[ch] + transmit[ch] * held[ch] for ch in range(3)]
                transmit = [transmit[ch] * held[3 + ch] for ch in range(3)]
        here = pl.ds(at * LANES, LANES)
        for k, value in enumerate(colour + transmit):
            if len(outs) == 1:
                canvas[k, pl.ds(row, SUBLANES), here] = value
            else:
                block_rows = canvas.shape[3]
                block = (number * SUBLANES) // block_rows
                first = pl.multiple_of((number * SUBLANES) % block_rows, SUBLANES)
                canvas[piece, block, k, pl.ds(first, SUBLANES), here] = value

    await_piece(0)

    @pl.loop(0, pieces)
    def _(piece):
        @pl.when(piece + 2 < in_pieces)
        def _():
            start(piece + 2)

        @pl.loop(0, piece_rows // (SUBLANES * unroll))
        def _(step):
            last_step = step == piece_rows // (SUBLANES * unroll) - 1

            @pl.when(last_step & (piece + 1 < in_pieces))
            def _():
                await_piece(piece + 1)

            for k in range(unroll):
                for at, tile in enumerate(computed):
                    strip(at, tile, piece, step * unroll + k)

        for copy in outgoing(piece):
            copy.start()

    @pl.loop(0, pieces)
    def _(piece):
        for copy in outgoing(piece):
            copy.wait()


def march(mode, tables, field, side, halos, middle, depth_total, scale, part_shape):
    planes, height, width = field.shape
    rim = mode == "rim"
    tiles = width // LANES - 1
    if mode == "outer":
        tiles = 1
    tiles_held, extent = tiles + 2, tiles * LANES
    held = 6 if rim else planes + 2
    if part_shape is None:
        group, pieces = 1, max(1, height // 64)
        outs = [jax.ShapeDtypeStruct((6, height, extent), jnp.float32)]
        canvas = (6, height, extent)
    else:
        pieces, group, rows = part_shape
        outs = [jax.ShapeDtypeStruct((pieces, 6, rows, extent), jnp.float32)] * group
        canvas = (pieces, group, 6, rows, extent)
    scratch = [
        pltpu.VMEM((tiles_held, held, height + 2 * PAD, LANES), jnp.float32),
        pltpu.VMEM(canvas, jnp.float32),
        pltpu.VMEM((SUBLANES, LANES), jnp.float32),
        pltpu.SemaphoreType.DMA((1 if rim else pieces, 4 * tiles_held + 2)),
        pltpu.SemaphoreType.DMA((pieces, group + 1)),
    ]
    operands = [field]
    if mode == "outer":
        operands.append(side)
    if mode != "middle":
        operands += list(halos)
    if rim:
        operands.append(middle)
        scratch.append(pltpu.VMEM((6, height, extent), jnp.float32))
    near = pl.BlockSpec(memory_space=pltpu.VMEM)
    out_specs = [pl.BlockSpec(memory_space=pl.ANY)] * len(outs)
    if mode == "middle":
        outs.append(jax.ShapeDtypeStruct((planes, height, LANES), jnp.float32))
        outs.append(jax.ShapeDtypeStruct((6, SUBLANES, LANES), jnp.int32))
        outs.append(jax.ShapeDtypeStruct((6, SUBLANES, LANES), jnp.float32))
        out_specs += [pl.BlockSpec(memory_space=pl.ANY), near, near]
    strips = height // pieces // SUBLANES
    unroll = min(strips, {"rim": 4, "outer": 4, "middle": 2}[mode])
    weight = 100 if mode == "middle" else 20000
    distant = pl.BlockSpec(memory_space=pl.ANY)
    out = pl.pallas_call(
        functools.partial(march_kernel, mode, depth_total, group, scale, unroll, pieces),
        out_shape=outs,
        in_specs=[near] * 2 + [distant] * len(operands),
        out_specs=out_specs,
        scratch_shapes=scratch,
        compiler_params=pltpu.CompilerParams(vmem_limit_bytes=56 * 1024 * 1024),
        cost_estimate=pl.CostEstimate(
            flops=planes * height * 256 * weight,
            bytes_accessed=planes * height * 256 * 5,
            transcendentals=0,
        ),
        name=f"march_{mode}",
    )(*tables, *operands)
    return out[0] if len(out) == 1 else out


def plane_halos(first, last):
    count = lax.axis_size("slab")
    forward = [(i, i + 1) for i in range(count - 1)]
    backward = [(i + 1, i) for i in range(count - 1)]
    return lax.ppermute(last, "slab", forward), lax.ppermute(first, "slab", backward)


def ordered(is_far, own, other):
    near = [jnp.where(is_far, b, a) for a, b in zip(own, other)]
    far = [jnp.where(is_far, a, b) for a, b in zip(own, other)]
    return [near[0] + near[1] * far[0], near[1] * far[1]]


def exchange(parts, own, shift):
    count = lax.axis_size("slab")
    merged, received = [], []
    for change, part in enumerate(parts):
        if change:
            part = lax.ppermute(part, "slab", [(i, i ^ change << shift) for i in range(count)])
            received.append(part)
        merged.append([part[:, :3], part[:, 3:]])
    digit = 0
    while len(merged) > 1:
        is_far = (own >> digit & 1) == 1
        merged = [ordered(is_far, merged[k], merged[k + 1]) for k in range(0, len(merged), 2)]
        digit += 1
    return merged[0], received


def reduce_image(image, parts, slab_index, block_rows):
    slab_count = lax.axis_size("slab")
    levels = slab_count.bit_length() - 1
    if parts is None:
        image = image.reshape((6, slab_count, block_rows, image.shape[-1]))
        image = jnp.swapaxes(image, 0, 1)
    for shift in range(0, levels, 2):
        size = 1 << min(2, levels - shift)
        own = (slab_index >> shift) & (size - 1)
        if parts is None:
            image = image.reshape((-1, size) + image.shape[1:])
            parts = [
                lax.dynamic_index_in_dim(image, own ^ change, 1, keepdims=False)
                for change in range(size)
            ]
        (colour, transmit), received = exchange(parts, own, shift)
        image, parts = jnp.concatenate([colour, transmit], axis=1), None
        first = received if not shift else first
    return (colour[0], 1.0 - transmit[0]), first


def per_device(field, tf_emission, tf_absorption):
    slab_count = lax.axis_size("slab")
    slab_index = lax.axis_index("slab")
    planes, height, width = field.shape
    depth_total = planes * slab_count
    block_rows = height // slab_count
    part_shape = None
    if slab_count >= 4 and block_rows % SUBLANES == 0:
        part_shape = (slab_count // 4, 4, block_rows)
    tables = (tf_emission, tf_absorption)

    halo = plane_halos(field[0], field[-1])
    scale = 0.5 * (tf_emission.shape[1] - 1)
    middle, edge, *tables = march(
        "middle", tables, field, None, None, None, depth_total, scale, None
    )
    side = lax.ppermute(edge, "tile", [(0, 1), (1, 0)])
    arrived = None
    results = []
    for mode in ("rim", "outer"):
        if arrived is not None:
            halo, side, _ = lax.optimization_barrier((halo, side, out))
        out = march(mode, tables, field, side, halo, middle, depth_total, scale, part_shape)
        if arrived is not None:
            out, _ = lax.optimization_barrier((out, arrived))
        image, parts = (out, None) if part_shape is None else (None, out)
        result, arrived = reduce_image(image, parts, slab_index, block_rows)
        results.append(result)
    first_core = lax.axis_index("tile") == 0
    return tuple(
        jnp.where(
            first_core,
            jnp.concatenate([wide, narrow], axis=2),
            jnp.concatenate([narrow, wide], axis=2),
        )
        for wide, narrow in zip(*results)
    )


def solution(mesh):
    placed = (P("slab", None, "tile"), P(), P())
    return jax.shard_map(
        per_device,
        mesh=mesh,
        in_specs=placed,
        out_specs=(P(None, "slab", "tile"), P(None, "slab", "tile")),
        check_vma=False,
    )
```

```python
import functools

import jax
import jax.numpy as jnp
from jax import lax
from jax.experimental import pallas as pl
from jax.experimental.pallas import tpu as pltpu
from jax.sharding import PartitionSpec as P

LIGHT_DIR = (0.2672612, 0.5345225, 0.8017837)
LANES = 128
SUBLANES = 8
PAD = 8
WORD_SCALE = 2.0**31 - 2.0**17
HALF = 65536


def prepare_tables(emission, absorption, depth_total, table, words, factors):
    breaks = emission.shape[1]
    table[...] = jnp.zeros(table.shape, jnp.float32)
    table[0:3, 0:breaks] = emission[...]
    table[3:6, 0:breaks] = absorption[...]
    values = table[...]
    largest = [jnp.maximum(jnp.max(ref[...]), 1e-30) for ref in (emission, absorption)]
    row = lax.broadcasted_iota(jnp.int32, table.shape, 0)
    lane = lax.broadcasted_iota(jnp.int32, table.shape, 1)
    scaled = values * (WORD_SCALE / jnp.where(row < 3, largest[0], largest[1]))
    following = jnp.where(lane < breaks - 1, pltpu.roll(scaled, LANES - 1, 1), scaled)
    rise = jnp.floor((following - scaled) * (1.0 / HALF) + 0.5)
    upper = jnp.floor((0.5 * (following + scaled) - rise) * (1.0 / HALF) + 0.5)
    word = upper.astype(jnp.int32) * HALF + rise.astype(jnp.int32)
    units = [largest[0] / WORD_SCALE, largest[1] * (4.0 / depth_total) / WORD_SCALE]
    constants = [0.9 * part * units[0] for part in LIGHT_DIR]
    constants += [0.1 * units[0], units[1], 0.75 * units[1]]
    for k in range(6):
        words[k] = jnp.broadcast_to(word[k : k + 1, :], (SUBLANES, LANES))
        factors[k] = jnp.full((SUBLANES, LANES), constants[k], jnp.float32)


def lookup(table, index):
    return lax.gather(
        table,
        index.reshape(index.shape + (1,)),
        lax.GatherDimensionNumbers(
            offset_dims=(),
            collapsed_slice_dims=(1,),
            start_index_map=(1,),
            operand_batching_dims=(0,),
            start_indices_batching_dims=(0,),
        ),
        slice_sizes=(1, 1),
        mode=lax.GatherScatterMode.PROMISE_IN_BOUNDS,
    )


def march_kernel(mode, depth_total, group, scale, unroll, pieces, tables_a, tables_b, *refs):
    refs = list(refs)
    field = refs.pop(0)
    side = refs.pop(0) if mode == "outer" else None
    low, high = (refs.pop(0), refs.pop(0)) if mode != "middle" else (None, None)
    rim = mode == "rim"
    middle = refs.pop(0) if rim else None
    inner = refs.pop() if rim else None
    cells, canvas, table, in_sems, out_sems = refs[-5:]
    outs = refs[:-5]
    if mode == "middle":
        edge, words, factors = outs[-3:]
        outs = outs[:-3]
    else:
        edge, words, factors = None, tables_a, tables_b
    planes, height, width = field.shape
    piece_rows = height // pieces
    in_pieces = in_sems.shape[0]
    core = lax.axis_index("tile")
    tiles = cells.shape[0] - 2
    computed = range(1, tiles + 1)
    blocks = [(0, 1, 2), (planes - 2, 3, 2)] if rim else [(0, 1, planes)]
    if rim:
        marched = (0, planes - 1)
    else:
        marched = range(1, planes - 1) if mode == "middle" else range(planes)
    place = {first + k: slot + k for first, slot, count in blocks for k in range(count)}
    place[-1] = 0
    place[planes] = max(place.values()) + 1
    far = (1 - core) * (tiles + 1)
    nearer = core if mode == "outer" else 1 - core
    first_lane_taken, first_tile = (1 - nearer) * (width // 2 - LANES), nearer

    def incoming(piece):
        in_rows = height // in_pieces
        start = pl.multiple_of(piece * in_rows, SUBLANES)
        body = pl.ds(start, in_rows)
        padded = pl.ds(start + PAD, in_rows)
        pairs = []
        for k in range(tiles + 1):
            lanes = pl.ds(pl.multiple_of(first_lane_taken + k * LANES, LANES), LANES)
            held = cells.at[first_tile + k]
            for first, where, count in blocks:
                target = held.at[pl.ds(where, count), padded, :]
                pairs.append((field.at[pl.ds(first, count), body, lanes], target))
        if mode != "middle":
            for tile in computed:
                lanes = pl.ds((tile - 1) * LANES, LANES)
                for halo, plane in ((low, -1), (high, planes)):
                    target = cells.at[tile, place[plane], padded, :]
                    pairs.append((halo.at[body, lanes], target))
        if rim:
            pairs.append((middle.at[:, body, :], inner.at[:, body, :]))
        if mode == "outer":
            pairs.append((side.at[:, body, :], cells.at[far, pl.ds(1, planes), padded, :]))
        return [
            pltpu.make_async_copy(source, target, in_sems.at[piece, k])
            for k, (source, target) in enumerate(pairs)
        ]

    def outgoing(piece):
        start = pl.multiple_of(piece * piece_rows, SUBLANES)
        body = pl.ds(start, piece_rows)
        if len(outs) == 1:
            pairs = [(canvas.at[:, body, :], outs[0].at[:, body, :])]
        else:
            own = lax.axis_index("slab") & (group - 1)
            pairs = [(canvas.at[piece, own ^ k], outs[k].at[piece]) for k in range(group)]
        return [
            pltpu.make_async_copy(source, target, out_sems.at[piece, k])
            for k, (source, target) in enumerate(pairs)
        ]

    def start(piece):
        for copy in incoming(piece):
            copy.start()

    def await_piece(piece):
        for copy in incoming(piece):
            copy.wait()

    for piece in range(min(2, in_pieces)):
        start(piece)
    if mode == "middle":
        first = pl.multiple_of((1 - core) * (width - LANES), LANES)
        edge_copy = pltpu.make_async_copy(
            field.at[:, :, pl.ds(first, LANES)], edge, out_sems.at[0, group]
        )
        edge_copy.start()
        prepare_tables(tables_a, tables_b, depth_total, table, words, factors)
    zeros = jnp.zeros((1, LANES), jnp.float32)
    for tile in computed:
        for plane in marched:
            cells[tile, place[plane], pl.ds(PAD - 1, 1), :] = zeros
            cells[tile, place[plane], pl.ds(PAD + height, 1), :] = zeros
    if mode != "outer":
        blank = jnp.zeros((height, LANES), jnp.float32)
        for plane in marched:
            cells[core * (tiles + 1), place[plane], pl.ds(PAD, height), :] = blank

    lane = lax.broadcasted_iota(jnp.int32, (SUBLANES, LANES), 1)
    first_lane = lane == 0
    last_lane = lane == LANES - 1

    def strip(at, tile, piece, number):
        row = pl.multiple_of(piece * piece_rows + number * SUBLANES, SUBLANES)

        def rows(tile, plane, offset=0):
            here = pl.ds(row + PAD + offset, SUBLANES)
            return cells[tile, place[plane], here, :]

        colour = transmit = None
        for plane in marched:
            before, centre, after = (rows(tile, plane + k) for k in (-1, 0, 1))
            left = pltpu.roll(jnp.where(last_lane, rows(tile - 1, plane), centre), 1, 1)
            right = pltpu.roll(jnp.where(first_lane, rows(tile + 1, plane), centre), LANES - 1, 1)
            diff_x = right - left
            diff_y = rows(tile, plane, 1) - rows(tile, plane, -1)
            diff_z = after - before
            inverse = lax.rsqrt(diff_x * diff_x + diff_y * diff_y + diff_z * diff_z + 1.0)
            facing = (factors[0] * diff_x + factors[1] * diff_y + factors[2] * diff_z) * inverse
            shading = jnp.maximum(facing, 0.0) + factors[3]
            weight = factors[4] - factors[5] * (inverse * inverse)
            middle_based = centre * scale + (scale - 0.5)
            interval = (middle_based + 0.5).astype(jnp.int32)
            offset = middle_based - interval.astype(jnp.float32)
            values = []
            for k in range(6):
                word = lookup(words[k], interval)
                rise = lax.shift_left(word, 16).astype(jnp.float32)
                values.append(word.astype(jnp.float32) + rise * offset)
            steps = [values[3 + ch] * weight for ch in range(3)]
            glows = [values[ch] * shading for ch in range(3)]
            if colour is None:
                colour = [step * glow for step, glow in zip(steps, glows)]
                transmit = [1.0 - step for step in steps]
            else:
                seen = [transmit[ch] * steps[ch] for ch in range(3)]
                colour = [colour[ch] + seen[ch] * glows[ch] for ch in range(3)]
                transmit = [transmit[ch] - seen[ch] for ch in range(3)]
            if rim and plane == 0:
                held = [
                    inner[k, pl.ds(row, SUBLANES), pl.ds(at * LANES, LANES)] for k in range(6)
                ]
                colour = [colour[ch] + transmit[ch] * held[ch] for ch in range(3)]
                transmit = [transmit[ch] * held[3 + ch] for ch in range(3)]
        here = pl.ds(at * LANES, LANES)
        for k, value in enumerate(colour + transmit):
            if len(outs) == 1:
                canvas[k, pl.ds(row, SUBLANES), here] = value
            else:
                block_rows = canvas.shape[3]
                block = (number * SUBLANES) // block_rows
                first = pl.multiple_of((number * SUBLANES) % block_rows, SUBLANES)
                canvas[piece, block, k, pl.ds(first, SUBLANES), here] = value

    await_piece(0)

    @pl.loop(0, pieces)
    def _(piece):
        @pl.when(piece + 2 < in_pieces)
        def _():
            start(piece + 2)

        @pl.loop(0, piece_rows // (SUBLANES * unroll))
        def _(step):
            last_step = step == piece_rows // (SUBLANES * unroll) - 1

            @pl.when(last_step & (piece + 1 < in_pieces))
            def _():
                await_piece(piece + 1)

            for k in range(unroll):
                for at, tile in enumerate(computed):
                    strip(at, tile, piece, step * unroll + k)

        for copy in outgoing(piece):
            copy.start()

    @pl.loop(0, pieces)
    def _(piece):
        for copy in outgoing(piece):
            copy.wait()

    if mode == "middle":
        edge_copy.wait()


def march(mode, tables, field, side, halos, middle, depth_total, scale, part_shape):
    planes, height, width = field.shape
    rim = mode == "rim"
    tiles = width // LANES // 2
    tiles_held, extent = tiles + 2, tiles * LANES
    held = 6 if rim else planes + 2
    if part_shape is None:
        group, pieces = 1, max(1, height // (32 if mode == "middle" else 64))
        outs = [jax.ShapeDtypeStruct((6, height, extent), jnp.float32)]
        canvas = (6, height, extent)
    else:
        pieces, group, rows = part_shape
        outs = [jax.ShapeDtypeStruct((pieces, 6, rows, extent), jnp.float32)] * group
        canvas = (pieces, group, 6, rows, extent)
    scratch = [
        pltpu.VMEM((tiles_held, held, height + 2 * PAD, LANES), jnp.float32),
        pltpu.VMEM(canvas, jnp.float32),
        pltpu.VMEM((SUBLANES, LANES), jnp.float32),
        pltpu.SemaphoreType.DMA((1 if rim else pieces, 4 * tiles_held + 2)),
        pltpu.SemaphoreType.DMA((pieces, group + 1)),
    ]
    operands = [field]
    if mode == "outer":
        operands.append(side)
    if mode != "middle":
        operands += list(halos)
    if rim:
        operands.append(middle)
        scratch.append(pltpu.VMEM((6, height, extent), jnp.float32))
    near = pl.BlockSpec(memory_space=pltpu.VMEM)
    out_specs = [pl.BlockSpec(memory_space=pl.ANY)] * len(outs)
    if mode == "middle":
        outs.append(jax.ShapeDtypeStruct((planes, height, LANES), jnp.float32))
        outs.append(jax.ShapeDtypeStruct((6, SUBLANES, LANES), jnp.int32))
        outs.append(jax.ShapeDtypeStruct((6, SUBLANES, LANES), jnp.float32))
        out_specs += [pl.BlockSpec(memory_space=pl.ANY), near, near]
    strips = height // pieces // SUBLANES
    unroll = min(strips, {"rim": 4, "outer": 4, "middle": 2}[mode])
    weight = 20000 if mode == "outer" else 100
    distant = pl.BlockSpec(memory_space=pl.ANY)
    out = pl.pallas_call(
        functools.partial(march_kernel, mode, depth_total, group, scale, unroll, pieces),
        out_shape=outs,
        in_specs=[near] * 2 + [distant] * len(operands),
        out_specs=out_specs,
        scratch_shapes=scratch,
        compiler_params=pltpu.CompilerParams(vmem_limit_bytes=56 * 1024 * 1024),
        cost_estimate=pl.CostEstimate(
            flops=planes * height * 256 * weight,
            bytes_accessed=planes * height * 256 * 5,
            transcendentals=0,
        ),
        name=f"march_{mode}",
    )(*tables, *operands)
    return out[0] if len(out) == 1 else out


def plane_halos(first, last):
    count = lax.axis_size("slab")
    forward = [(i, i + 1) for i in range(count - 1)]
    backward = [(i + 1, i) for i in range(count - 1)]
    return lax.ppermute(last, "slab", forward), lax.ppermute(first, "slab", backward)


def ordered(is_far, own, other):
    near = [jnp.where(is_far, b, a) for a, b in zip(own, other)]
    far = [jnp.where(is_far, a, b) for a, b in zip(own, other)]
    return [near[0] + near[1] * far[0], near[1] * far[1]]


def exchange(parts, own, shift):
    count = lax.axis_size("slab")
    merged, received = [], []
    for change, part in enumerate(parts):
        if change:
            part = lax.ppermute(part, "slab", [(i, i ^ change << shift) for i in range(count)])
            received.append(part)
        merged.append([part[:, :3], part[:, 3:]])
    digit = 0
    while len(merged) > 1:
        is_far = (own >> digit & 1) == 1
        merged = [ordered(is_far, merged[k], merged[k + 1]) for k in range(0, len(merged), 2)]
        digit += 1
    return merged[0], received


def reduce_image(image, parts, slab_index, block_rows):
    slab_count = lax.axis_size("slab")
    levels = slab_count.bit_length() - 1
    if parts is None:
        image = image.reshape((6, slab_count, block_rows, image.shape[-1]))
        image = jnp.swapaxes(image, 0, 1)
    for shift in range(0, levels, 2):
        size = 1 << min(2, levels - shift)
        own = (slab_index >> shift) & (size - 1)
        if parts is None:
            image = image.reshape((-1, size) + image.shape[1:])
            parts = [
                lax.dynamic_index_in_dim(image, own ^ change, 1, keepdims=False)
                for change in range(size)
            ]
        (colour, transmit), received = exchange(parts, own, shift)
        image, parts = jnp.concatenate([colour, transmit], axis=1), None
        first = received if not shift else first
    return (colour[0], 1.0 - transmit[0]), first


def per_device(field, tf_emission, tf_absorption):
    slab_count = lax.axis_size("slab")
    slab_index = lax.axis_index("slab")
    planes, height, width = field.shape
    depth_total = planes * slab_count
    block_rows = height // slab_count
    part_shape = None
    if slab_count >= 4 and block_rows % SUBLANES == 0:
        part_shape = (slab_count // 4, 4, block_rows)
    tables = (tf_emission, tf_absorption)

    core = lax.axis_index("tile")
    half = width // 2
    halos = []
    for start in (core * half, (1 - core) * half):
        first, last = (
            lax.dynamic_slice_in_dim(field[plane], start, half, axis=1) for plane in (0, -1)
        )
        halos.append(plane_halos(first, last))
    scale = 0.5 * (tf_emission.shape[1] - 1)
    middle, edge, *tables = march(
        "middle", tables, field, None, None, None, depth_total, scale, None
    )
    edge, _ = lax.optimization_barrier((edge, halos[0]))
    side = lax.ppermute(edge, "tile", [(0, 1), (1, 0)])
    arrived = None
    results = []
    for mode, halo in zip(("rim", "outer"), halos):
        if arrived is not None:
            halo, side, _ = lax.optimization_barrier((halo, side, out))
        out = march(mode, tables, field, side, halo, middle, depth_total, scale, part_shape)
        out, _ = lax.optimization_barrier((out, halos[1] if arrived is None else arrived))
        image, parts = (out, None) if part_shape is None else (None, out)
        result, arrived = reduce_image(image, parts, slab_index, block_rows)
        results.append(result)
    first_core = core == 0
    return tuple(
        jnp.where(
            first_core,
            jnp.concatenate([wide, narrow], axis=2),
            jnp.concatenate([narrow, wide], axis=2),
        )
        for wide, narrow in zip(*results)
    )


def solution(mesh):
    placed = (P("slab", None, "tile"), P(), P())
    return jax.shard_map(
        per_device,
        mesh=mesh,
        in_specs=placed,
        out_specs=(P(None, "slab", "tile"), P(None, "slab", "tile")),
        check_vma=False,
    )
```

```python
import functools

import jax
import jax.numpy as jnp
from jax import lax
from jax.experimental import pallas as pl
from jax.experimental.pallas import tpu as pltpu
from jax.sharding import PartitionSpec as P

LIGHT_DIR = (0.2672612, 0.5345225, 0.8017837)
LANES = 128
SUBLANES = 8
PAD = 8
WORD_SCALE = 2.0**31 - 2.0**17
HALF = 65536


def prepare_tables(emission, absorption, depth_total, table, words, factors):
    breaks = emission.shape[1]
    table[...] = jnp.zeros(table.shape, jnp.float32)
    table[0:3, 0:breaks] = emission[...]
    table[3:6, 0:breaks] = absorption[...]
    values = table[...]
    largest = [jnp.maximum(jnp.max(ref[...]), 1e-30) for ref in (emission, absorption)]
    row = lax.broadcasted_iota(jnp.int32, table.shape, 0)
    lane = lax.broadcasted_iota(jnp.int32, table.shape, 1)
    scaled = values * (WORD_SCALE / jnp.where(row < 3, largest[0], largest[1]))
    following = jnp.where(lane < breaks - 1, pltpu.roll(scaled, LANES - 1, 1), scaled)
    rise = jnp.floor((following - scaled) * (1.0 / HALF) + 0.5)
    upper = jnp.floor((0.5 * (following + scaled) - rise) * (1.0 / HALF) + 0.5)
    word = upper.astype(jnp.int32) * HALF + rise.astype(jnp.int32)
    units = [largest[0] / WORD_SCALE, largest[1] * (4.0 / depth_total) / WORD_SCALE]
    constants = [0.9 * part * units[0] for part in LIGHT_DIR]
    constants += [0.1 * units[0], units[1], 0.75 * units[1]]
    for k in range(6):
        words[k] = jnp.broadcast_to(word[k : k + 1, :], (SUBLANES, LANES))
        factors[k] = jnp.full((SUBLANES, LANES), constants[k], jnp.float32)


def lookup(table, index):
    return lax.gather(
        table,
        index.reshape(index.shape + (1,)),
        lax.GatherDimensionNumbers(
            offset_dims=(),
            collapsed_slice_dims=(1,),
            start_index_map=(1,),
            operand_batching_dims=(0,),
            start_indices_batching_dims=(0,),
        ),
        slice_sizes=(1, 1),
        mode=lax.GatherScatterMode.PROMISE_IN_BOUNDS,
    )


def march_kernel(mode, depth_total, group, scale, unroll, pieces, tables_a, tables_b, *refs):
    refs = list(refs)
    field = refs.pop(0)
    side = refs.pop(0) if mode == "outer" else None
    low, high = (refs.pop(0), refs.pop(0)) if mode != "middle" else (None, None)
    rim = mode == "rim"
    middle = refs.pop(0) if rim else None
    inner = refs.pop() if mode != "outer" else None
    cells, canvas, table, in_sems, out_sems = refs[-5:]
    outs = refs[:-5]
    if mode == "middle":
        edge, words, factors = outs[-3:]
        outs = outs[:-3]
    else:
        edge, words, factors = None, tables_a, tables_b
    planes, height, width = field.shape
    piece_rows = height // pieces
    in_pieces = in_sems.shape[0]
    core = lax.axis_index("tile")
    tiles = cells.shape[0] - 2
    computed = range(1, tiles + 1)
    blocks = [(0, 1, 2), (planes - 2, 3, 2)] if rim else [(0, 1, planes)]
    if rim:
        marched = (0, planes - 1)
    else:
        marched = range(1, planes - 1) if mode == "middle" else range(planes)
    place = {first + k: slot + k for first, slot, count in blocks for k in range(count)}
    place[-1] = 0
    place[planes] = max(place.values()) + 1
    far = (1 - core) * (tiles + 1)
    nearer = core if mode == "outer" else 1 - core
    first_lane_taken, first_tile = (1 - nearer) * (width // 2 - LANES), nearer

    def incoming(piece):
        in_rows = height // in_pieces
        start = pl.multiple_of(piece * in_rows, SUBLANES)
        body = pl.ds(start, in_rows)
        padded = pl.ds(start + PAD, in_rows)
        pairs = []
        for k in range(tiles + 1):
            lanes = pl.ds(pl.multiple_of(first_lane_taken + k * LANES, LANES), LANES)
            held = cells.at[first_tile + k]
            for first, where, count in blocks:
                target = held.at[pl.ds(where, count), padded, :]
                pairs.append((field.at[pl.ds(first, count), body, lanes], target))
        if mode != "middle":
            for tile in computed:
                lane = (1 - nearer) * (width // 2) + (tile - 1) * LANES
                lanes = pl.ds(pl.multiple_of(lane, LANES), LANES)
                for halo, plane in ((low, -1), (high, planes)):
                    target = cells.at[tile, place[plane], padded, :]
                    pairs.append((halo.at[body, lanes], target))
        if rim:
            pairs.append((middle.at[:, body, :], inner.at[:, body, :]))
        if mode == "outer":
            pairs.append((side.at[:, body, :], cells.at[far, pl.ds(1, planes), padded, :]))
        return [
            pltpu.make_async_copy(source, target, in_sems.at[piece, k])
            for k, (source, target) in enumerate(pairs)
        ]

    def outgoing(piece):
        start = pl.multiple_of(piece * piece_rows, SUBLANES)
        body = pl.ds(start, piece_rows)
        if len(outs) == 1:
            pairs = [(canvas.at[:, body, :], outs[0].at[:, body, :])]
        else:
            own = lax.axis_index("slab") & (group - 1)
            pairs = [(canvas.at[piece, own ^ k], outs[k].at[piece]) for k in range(group)]
        return [
            pltpu.make_async_copy(source, target, out_sems.at[piece, k])
            for k, (source, target) in enumerate(pairs)
        ]

    def start(piece):
        for copy in incoming(piece):
            copy.start()

    def await_piece(piece):
        for copy in incoming(piece):
            copy.wait()

    for piece in range(min(2, in_pieces)):
        start(piece)
    if mode == "middle":
        first = pl.multiple_of((1 - core) * (width - LANES), LANES)
        edge_in = pltpu.make_async_copy(
            field.at[:, :, pl.ds(first, LANES)], inner, out_sems.at[0, group]
        )
        edge_out = pltpu.make_async_copy(inner, edge, out_sems.at[1, group])
        edge_in.start()
        prepare_tables(tables_a, tables_b, depth_total, table, words, factors)
    zeros = jnp.zeros((1, LANES), jnp.float32)
    for tile in computed:
        for plane in marched:
            cells[tile, place[plane], pl.ds(PAD - 1, 1), :] = zeros
            cells[tile, place[plane], pl.ds(PAD + height, 1), :] = zeros
    if mode != "outer":
        blank = jnp.zeros((height, LANES), jnp.float32)
        for plane in marched:
            cells[core * (tiles + 1), place[plane], pl.ds(PAD, height), :] = blank

    lane = lax.broadcasted_iota(jnp.int32, (SUBLANES, LANES), 1)
    first_lane = lane == 0
    last_lane = lane == LANES - 1

    def strip(at, tile, piece, number):
        row = pl.multiple_of(piece * piece_rows + number * SUBLANES, SUBLANES)

        def rows(tile, plane, offset=0):
            here = pl.ds(row + PAD + offset, SUBLANES)
            return cells[tile, place[plane], here, :]

        colour = transmit = None
        for plane in marched:
            before, centre, after = (rows(tile, plane + k) for k in (-1, 0, 1))
            left = pltpu.roll(jnp.where(last_lane, rows(tile - 1, plane), centre), 1, 1)
            right = pltpu.roll(jnp.where(first_lane, rows(tile + 1, plane), centre), LANES - 1, 1)
            diff_x = right - left
            diff_y = rows(tile, plane, 1) - rows(tile, plane, -1)
            diff_z = after - before
            inverse = lax.rsqrt(diff_x * diff_x + diff_y * diff_y + diff_z * diff_z + 1.0)
            facing = (factors[0] * diff_x + factors[1] * diff_y + factors[2] * diff_z) * inverse
            shading = jnp.maximum(facing, 0.0) + factors[3]
            weight = factors[4] - factors[5] * (inverse * inverse)
            middle_based = centre * scale + (scale - 0.5)
            interval = (middle_based + 0.5).astype(jnp.int32)
            offset = middle_based - interval.astype(jnp.float32)
            values = []
            for k in range(6):
                word = lookup(words[k], interval)
                rise = lax.shift_left(word, 16).astype(jnp.float32)
                values.append(word.astype(jnp.float32) + rise * offset)
            steps = [values[3 + ch] * weight for ch in range(3)]
            glows = [values[ch] * shading for ch in range(3)]
            if colour is None:
                colour = [step * glow for step, glow in zip(steps, glows)]
                transmit = [1.0 - step for step in steps]
            else:
                seen = [transmit[ch] * steps[ch] for ch in range(3)]
                colour = [colour[ch] + seen[ch] * glows[ch] for ch in range(3)]
                transmit = [transmit[ch] - seen[ch] for ch in range(3)]
            if rim and plane == 0:
                held = [
                    inner[k, pl.ds(row, SUBLANES), pl.ds(at * LANES, LANES)] for k in range(6)
                ]
                colour = [colour[ch] + transmit[ch] * held[ch] for ch in range(3)]
                transmit = [transmit[ch] * held[3 + ch] for ch in range(3)]
        here = pl.ds(at * LANES, LANES)
        for k, value in enumerate(colour + transmit):
            if len(outs) == 1:
                canvas[k, pl.ds(row, SUBLANES), here] = value
            else:
                block_rows = canvas.shape[3]
                block = (number * SUBLANES) // block_rows
                first = pl.multiple_of((number * SUBLANES) % block_rows, SUBLANES)
                canvas[piece, block, k, pl.ds(first, SUBLANES), here] = value

    await_piece(0)

    @pl.loop(0, pieces)
    def _(piece):
        @pl.when(piece + 2 < in_pieces)
        def _():
            start(piece + 2)

        @pl.loop(0, piece_rows // (SUBLANES * unroll))
        def _(step):
            last_step = step == piece_rows // (SUBLANES * unroll) - 1

            @pl.when(last_step & (piece + 1 < in_pieces))
            def _():
                await_piece(piece + 1)

            for k in range(unroll):
                for at, tile in enumerate(computed):
                    strip(at, tile, piece, step * unroll + k)

        for copy in outgoing(piece):
            copy.start()
        if mode == "middle":

            @pl.when(piece == pieces // 2)
            def _():
                edge_in.wait()
                edge_out.start()

    @pl.loop(0, pieces)
    def _(piece):
        for copy in outgoing(piece):
            copy.wait()

    if mode == "middle":
        edge_out.wait()


def march(mode, tables, field, side, halos, middle, depth_total, scale, part_shape):
    planes, height, width = field.shape
    rim = mode == "rim"
    tiles = width // LANES // 2
    tiles_held, extent = tiles + 2, tiles * LANES
    held = 6 if rim else planes + 2
    if part_shape is None:
        group, pieces = 1, max(1, height // (32 if mode == "middle" else 64))
        outs = [jax.ShapeDtypeStruct((6, height, extent), jnp.float32)]
        canvas = (6, height, extent)
    else:
        pieces, group, rows = part_shape
        outs = [jax.ShapeDtypeStruct((pieces, 6, rows, extent), jnp.float32)] * group
        canvas = (pieces, group, 6, rows, extent)
    scratch = [
        pltpu.VMEM((tiles_held, held, height + 2 * PAD, LANES), jnp.float32),
        pltpu.VMEM(canvas, jnp.float32),
        pltpu.VMEM((SUBLANES, LANES), jnp.float32),
        pltpu.SemaphoreType.DMA((1 if rim else pieces, 4 * tiles_held + 2)),
        pltpu.SemaphoreType.DMA((pieces, group + 1)),
    ]
    operands = [field]
    if mode == "outer":
        operands.append(side)
    if mode != "middle":
        operands += list(halos)
    if rim:
        operands.append(middle)
        scratch.append(pltpu.VMEM((6, height, extent), jnp.float32))
    if mode == "middle":
        scratch.append(pltpu.VMEM((planes, height, LANES), jnp.float32))
    near = pl.BlockSpec(memory_space=pltpu.VMEM)
    out_specs = [pl.BlockSpec(memory_space=pl.ANY)] * len(outs)
    if mode == "middle":
        outs.append(jax.ShapeDtypeStruct((planes, height, LANES), jnp.float32))
        outs.append(jax.ShapeDtypeStruct((6, SUBLANES, LANES), jnp.int32))
        outs.append(jax.ShapeDtypeStruct((6, SUBLANES, LANES), jnp.float32))
        out_specs += [pl.BlockSpec(memory_space=pl.ANY), near, near]
    strips = height // pieces // SUBLANES
    unroll = min(strips, {"rim": 4, "outer": 4, "middle": 2}[mode])
    weight = 20000 if mode == "outer" else 0
    distant = pl.BlockSpec(memory_space=pl.ANY)
    out = pl.pallas_call(
        functools.partial(march_kernel, mode, depth_total, group, scale, unroll, pieces),
        out_shape=outs,
        in_specs=[near] * 2 + [distant] * len(operands),
        out_specs=out_specs,
        scratch_shapes=scratch,
        compiler_params=pltpu.CompilerParams(vmem_limit_bytes=56 * 1024 * 1024),
        cost_estimate=pl.CostEstimate(
            flops=planes * height * 256 * weight,
            bytes_accessed=planes * height * 4 * weight,
            transcendentals=0,
        ),
        name=f"march_{mode}",
    )(*tables, *operands)
    return out[0] if len(out) == 1 else out


def plane_halos(first, last):
    count = lax.axis_size("slab")
    forward = [(i, i + 1) for i in range(count - 1)]
    backward = [(i + 1, i) for i in range(count - 1)]
    return lax.ppermute(last, "slab", forward), lax.ppermute(first, "slab", backward)


def ordered(is_far, own, other):
    near = [jnp.where(is_far, b, a) for a, b in zip(own, other)]
    far = [jnp.where(is_far, a, b) for a, b in zip(own, other)]
    return [near[0] + near[1] * far[0], near[1] * far[1]]


def exchange(parts, own, shift):
    count = lax.axis_size("slab")
    merged, received = [], []
    for change, part in enumerate(parts):
        if change:
            part = lax.ppermute(part, "slab", [(i, i ^ change << shift) for i in range(count)])
            received.append(part)
        merged.append([part[:, :3], part[:, 3:]])
    digit = 0
    while len(merged) > 1:
        is_far = (own >> digit & 1) == 1
        merged = [ordered(is_far, merged[k], merged[k + 1]) for k in range(0, len(merged), 2)]
        digit += 1
    return merged[0], received


def reduce_image(image, parts, slab_index, block_rows):
    slab_count = lax.axis_size("slab")
    levels = slab_count.bit_length() - 1
    if parts is None:
        image = image.reshape((6, slab_count, block_rows, image.shape[-1]))
        image = jnp.swapaxes(image, 0, 1)
    for shift in range(0, levels, 2):
        size = 1 << min(2, levels - shift)
        own = (slab_index >> shift) & (size - 1)
        if parts is None:
            image = image.reshape((-1, size) + image.shape[1:])
            parts = [
                lax.dynamic_index_in_dim(image, own ^ change, 1, keepdims=False)
                for change in range(size)
            ]
        (colour, transmit), received = exchange(parts, own, shift)
        image, parts = jnp.concatenate([colour, transmit], axis=1), None
        first = received if not shift else first
    return (colour[0], 1.0 - transmit[0]), first


def per_device(field, tf_emission, tf_absorption):
    slab_count = lax.axis_size("slab")
    slab_index = lax.axis_index("slab")
    planes, height, width = field.shape
    depth_total = planes * slab_count
    block_rows = height // slab_count
    part_shape = None
    if slab_count >= 4 and block_rows % SUBLANES == 0:
        part_shape = (slab_count // 4, 4, block_rows)
    tables = (tf_emission, tf_absorption)

    core = lax.axis_index("tile")
    halo = plane_halos(field[0], field[-1])
    scale = 0.5 * (tf_emission.shape[1] - 1)
    middle, edge, *tables = march(
        "middle", tables, field, None, None, None, depth_total, scale, None
    )
    edge, _ = lax.optimization_barrier((edge, halo))
    side = lax.ppermute(edge, "tile", [(0, 1), (1, 0)])
    arrived = None
    results = []
    for mode in ("rim", "outer"):
        if arrived is not None:
            halo, side, _ = lax.optimization_barrier((halo, side, out))
        out = march(mode, tables, field, side, halo, middle, depth_total, scale, part_shape)
        if arrived is not None:
            out, _ = lax.optimization_barrier((out, arrived))
        image, parts = (out, None) if part_shape is None else (None, out)
        result, arrived = reduce_image(image, parts, slab_index, block_rows)
        results.append(result)
    first_core = core == 0
    return tuple(
        jnp.where(
            first_core,
            jnp.concatenate([wide, narrow], axis=2),
            jnp.concatenate([narrow, wide], axis=2),
        )
        for wide, narrow in zip(*results)
    )


def solution(mesh):
    placed = (P("slab", None, "tile"), P(), P())
    return jax.shard_map(
        per_device,
        mesh=mesh,
        in_specs=placed,
        out_specs=(P(None, "slab", "tile"), P(None, "slab", "tile")),
        check_vma=False,
    )
```

```python
import functools

import jax
import jax.numpy as jnp
from jax import lax
from jax.experimental import pallas as pl
from jax.experimental.pallas import tpu as pltpu
from jax.sharding import PartitionSpec as P

LIGHT_DIR = (0.2672612, 0.5345225, 0.8017837)
LANES = 128
SUBLANES = 8
PAD = 8
WORD_SCALE = 2.0**31 - 2.0**17
HALF = 65536


def prepare_tables(emission, absorption, depth_total, table, words, factors):
    breaks = emission.shape[1]
    table[...] = jnp.zeros(table.shape, jnp.float32)
    table[0:3, 0:breaks] = emission[...]
    table[3:6, 0:breaks] = absorption[...]
    values = table[...]
    largest = [jnp.maximum(jnp.max(ref[...]), 1e-30) for ref in (emission, absorption)]
    row = lax.broadcasted_iota(jnp.int32, table.shape, 0)
    lane = lax.broadcasted_iota(jnp.int32, table.shape, 1)
    scaled = values * (WORD_SCALE / jnp.where(row < 3, largest[0], largest[1]))
    following = jnp.where(lane < breaks - 1, pltpu.roll(scaled, LANES - 1, 1), scaled)
    rise = jnp.floor((following - scaled) * (1.0 / HALF) + 0.5)
    upper = jnp.floor((0.5 * (following + scaled) - rise) * (1.0 / HALF) + 0.5)
    word = upper.astype(jnp.int32) * HALF + rise.astype(jnp.int32)
    units = [largest[0] / WORD_SCALE, largest[1] * (4.0 / depth_total) / WORD_SCALE]
    constants = [0.9 * part * units[0] for part in LIGHT_DIR]
    constants += [0.1 * units[0], units[1], 0.75 * units[1]]
    for k in range(6):
        words[k] = jnp.broadcast_to(word[k : k + 1, :], (SUBLANES, LANES))
        factors[k] = jnp.full((SUBLANES, LANES), constants[k], jnp.float32)


def lookup(table, index):
    return lax.gather(
        table,
        index.reshape(index.shape + (1,)),
        lax.GatherDimensionNumbers(
            offset_dims=(),
            collapsed_slice_dims=(1,),
            start_index_map=(1,),
            operand_batching_dims=(0,),
            start_indices_batching_dims=(0,),
        ),
        slice_sizes=(1, 1),
        mode=lax.GatherScatterMode.PROMISE_IN_BOUNDS,
    )


def march_kernel(mode, depth_total, group, scale, unroll, pieces, tables_a, tables_b, *refs):
    refs = list(refs)
    field = refs.pop(0)
    side = refs.pop(0) if mode == "outer" else None
    low, high = (refs.pop(0), refs.pop(0)) if mode != "middle" else (None, None)
    rim = mode == "rim"
    middle = refs.pop(0) if rim else None
    inner = refs.pop() if mode != "outer" else None
    cells, canvas, table, in_sems, out_sems = refs[-5:]
    outs = refs[:-5]
    if mode == "middle":
        edge, words, factors = outs[-3:]
        outs = outs[:-3]
    else:
        edge, words, factors = None, tables_a, tables_b
    planes, height, width = field.shape
    piece_rows = height // pieces
    in_pieces = in_sems.shape[0]
    core = lax.axis_index("tile")
    tiles = cells.shape[0] - 2
    computed = range(1, tiles + 1)
    blocks = [(0, 1, 2), (planes - 2, 3, 2)] if rim else [(0, 1, planes)]
    if rim:
        marched = (0, planes - 1)
    else:
        marched = range(1, planes - 1) if mode == "middle" else range(planes)
    place = {first + k: slot + k for first, slot, count in blocks for k in range(count)}
    place[-1] = 0
    place[planes] = max(place.values()) + 1
    far = (1 - core) * (tiles + 1)
    nearer = core if mode == "outer" else 1 - core
    first_lane_taken, first_tile = (1 - nearer) * (width // 2 - LANES), nearer

    def incoming(piece):
        in_rows = height // in_pieces
        start = pl.multiple_of(piece * in_rows, SUBLANES)
        body = pl.ds(start, in_rows)
        padded = pl.ds(start + PAD, in_rows)
        pairs = []
        for k in range(tiles + 1):
            lanes = pl.ds(pl.multiple_of(first_lane_taken + k * LANES, LANES), LANES)
            held = cells.at[first_tile + k]
            for first, where, count in blocks:
                target = held.at[pl.ds(where, count), padded, :]
                pairs.append((field.at[pl.ds(first, count), body, lanes], target))
        if mode != "middle":
            for tile in computed:
                lane = (1 - nearer) * (width // 2) + (tile - 1) * LANES
                lanes = pl.ds(pl.multiple_of(lane, LANES), LANES)
                for halo, plane in ((low, -1), (high, planes)):
                    target = cells.at[tile, place[plane], padded, :]
                    pairs.append((halo.at[body, lanes], target))
        if rim:
            pairs.append((middle.at[:, body, :], inner.at[:, body, :]))
        if mode == "outer":
            pairs.append((side.at[:, body, :], cells.at[far, pl.ds(1, planes), padded, :]))
        return [
            pltpu.make_async_copy(source, target, in_sems.at[piece, k])
            for k, (source, target) in enumerate(pairs)
        ]

    def outgoing(piece):
        start = pl.multiple_of(piece * piece_rows, SUBLANES)
        body = pl.ds(start, piece_rows)
        if len(outs) == 1:
            pairs = [(canvas.at[:, body, :], outs[0].at[:, body, :])]
        else:
            own = lax.axis_index("slab") & (group - 1)
            pairs = [(canvas.at[piece, own ^ k], outs[k].at[piece]) for k in range(group)]
        return [
            pltpu.make_async_copy(source, target, out_sems.at[piece, k])
            for k, (source, target) in enumerate(pairs)
        ]

    def start(piece):
        for copy in incoming(piece):
            copy.start()

    def await_piece(piece):
        for copy in incoming(piece):
            copy.wait()

    for piece in range(min(2, in_pieces)):
        start(piece)
    if mode == "middle":
        first = pl.multiple_of((1 - core) * (width - LANES), LANES)
        edge_in = pltpu.make_async_copy(
            field.at[:, :, pl.ds(first, LANES)], inner, out_sems.at[0, group]
        )
        edge_out = pltpu.make_async_copy(inner, edge, out_sems.at[1, group])
        edge_in.start()
        prepare_tables(tables_a, tables_b, depth_total, table, words, factors)
    zeros = jnp.zeros((1, LANES), jnp.float32)
    for tile in computed:
        for plane in marched:
            cells[tile, place[plane], pl.ds(PAD - 1, 1), :] = zeros
            cells[tile, place[plane], pl.ds(PAD + height, 1), :] = zeros
    if mode != "outer":
        blank = jnp.zeros((height, LANES), jnp.float32)
        for plane in marched:
            cells[core * (tiles + 1), place[plane], pl.ds(PAD, height), :] = blank

    lane = lax.broadcasted_iota(jnp.int32, (SUBLANES, LANES), 1)
    first_lane = lane == 0
    last_lane = lane == LANES - 1

    def strip(at, tile, piece, number):
        row = pl.multiple_of(piece * piece_rows + number * SUBLANES, SUBLANES)

        def rows(tile, plane, offset=0):
            here = pl.ds(row + PAD + offset, SUBLANES)
            return cells[tile, place[plane], here, :]

        colour = transmit = None
        for plane in marched:
            before, centre, after = (rows(tile, plane + k) for k in (-1, 0, 1))
            left = pltpu.roll(jnp.where(last_lane, rows(tile - 1, plane), centre), 1, 1)
            right = pltpu.roll(jnp.where(first_lane, rows(tile + 1, plane), centre), LANES - 1, 1)
            diff_x = right - left
            diff_y = rows(tile, plane, 1) - rows(tile, plane, -1)
            diff_z = after - before
            inverse = lax.rsqrt(diff_x * diff_x + diff_y * diff_y + diff_z * diff_z + 1.0)
            facing = (factors[0] * diff_x + factors[1] * diff_y + factors[2] * diff_z) * inverse
            shading = jnp.maximum(facing, 0.0) + factors[3]
            weight = factors[4] - factors[5] * (inverse * inverse)
            middle_based = centre * scale + (scale - 0.5)
            interval = (middle_based + 0.5).astype(jnp.int32)
            offset = middle_based - interval.astype(jnp.float32)
            values = []
            for k in range(6):
                word = lookup(words[k], interval)
                rise = lax.shift_left(word, 16).astype(jnp.float32)
                values.append(word.astype(jnp.float32) + rise * offset)
            steps = [values[3 + ch] * weight for ch in range(3)]
            glows = [values[ch] * shading for ch in range(3)]
            if colour is None:
                colour = [step * glow for step, glow in zip(steps, glows)]
                transmit = [1.0 - step for step in steps]
            else:
                seen = [transmit[ch] * steps[ch] for ch in range(3)]
                colour = [colour[ch] + seen[ch] * glows[ch] for ch in range(3)]
                transmit = [transmit[ch] - seen[ch] for ch in range(3)]
            if rim and plane == 0:
                held = [
                    inner[k, pl.ds(row, SUBLANES), pl.ds(at * LANES, LANES)] for k in range(6)
                ]
                colour = [colour[ch] + transmit[ch] * held[ch] for ch in range(3)]
                transmit = [transmit[ch] * held[3 + ch] for ch in range(3)]
        here = pl.ds(at * LANES, LANES)
        for k, value in enumerate(colour + transmit):
            if len(outs) == 1:
                canvas[k, pl.ds(row, SUBLANES), here] = value
            else:
                block_rows = canvas.shape[3]
                block = (number * SUBLANES) // block_rows
                first = pl.multiple_of((number * SUBLANES) % block_rows, SUBLANES)
                canvas[piece, block, k, pl.ds(first, SUBLANES), here] = value

    await_piece(0)

    @pl.loop(0, pieces)
    def _(piece):
        @pl.when(piece + 2 < in_pieces)
        def _():
            start(piece + 2)

        @pl.loop(0, piece_rows // (SUBLANES * unroll))
        def _(step):
            last_step = step == piece_rows // (SUBLANES * unroll) - 1

            @pl.when(last_step & (piece + 1 < in_pieces))
            def _():
                await_piece(piece + 1)

            for k in range(unroll):
                for at, tile in enumerate(computed):
                    strip(at, tile, piece, step * unroll + k)

        for copy in outgoing(piece):
            copy.start()
        if mode == "middle":

            @pl.when(piece == pieces // 2)
            def _():
                edge_in.wait()
                edge_out.start()

    @pl.loop(0, pieces)
    def _(piece):
        for copy in outgoing(piece):
            copy.wait()

    if mode == "middle":
        edge_out.wait()


def march(mode, tables, field, side, halos, middle, depth_total, scale, part_shape):
    planes, height, width = field.shape
    rim = mode == "rim"
    tiles = width // LANES // 2
    tiles_held, extent = tiles + 2, tiles * LANES
    held = 6 if rim else planes + 2
    if part_shape is None:
        group, pieces = 1, max(1, height // (32 if mode == "middle" else 64))
        outs = [jax.ShapeDtypeStruct((6, height, extent), jnp.float32)]
        canvas = (6, height, extent)
    else:
        pieces, group, rows = part_shape
        outs = [jax.ShapeDtypeStruct((pieces, 6, rows, extent), jnp.float32)] * group
        canvas = (pieces, group, 6, rows, extent)
    scratch = [
        pltpu.VMEM((tiles_held, held, height + 2 * PAD, LANES), jnp.float32),
        pltpu.VMEM(canvas, jnp.float32),
        pltpu.VMEM((SUBLANES, LANES), jnp.float32),
        pltpu.SemaphoreType.DMA((1 if rim else pieces, 4 * tiles_held + 2)),
        pltpu.SemaphoreType.DMA((pieces, group + 1)),
    ]
    operands = [field]
    if mode == "outer":
        operands.append(side)
    if mode != "middle":
        operands += list(halos)
    if rim:
        operands.append(middle)
        scratch.append(pltpu.VMEM((6, height, extent), jnp.float32))
    if mode == "middle":
        scratch.append(pltpu.VMEM((planes, height, LANES), jnp.float32))
    near = pl.BlockSpec(memory_space=pltpu.VMEM)
    out_specs = [pl.BlockSpec(memory_space=pl.ANY)] * len(outs)
    if mode == "middle":
        outs.append(jax.ShapeDtypeStruct((planes, height, LANES), jnp.float32))
        outs.append(jax.ShapeDtypeStruct((6, SUBLANES, LANES), jnp.int32))
        outs.append(jax.ShapeDtypeStruct((6, SUBLANES, LANES), jnp.float32))
        out_specs += [pl.BlockSpec(memory_space=pl.ANY), near, near]
    strips = height // pieces // SUBLANES
    unroll = min(strips, {"rim": 8, "outer": 4, "middle": 2}[mode])
    weight = 20000 if mode == "outer" else 0
    distant = pl.BlockSpec(memory_space=pl.ANY)
    out = pl.pallas_call(
        functools.partial(march_kernel, mode, depth_total, group, scale, unroll, pieces),
        out_shape=outs,
        in_specs=[near] * 2 + [distant] * len(operands),
        out_specs=out_specs,
        scratch_shapes=scratch,
        compiler_params=pltpu.CompilerParams(vmem_limit_bytes=44 * 1024 * 1024),
        cost_estimate=pl.CostEstimate(
            flops=planes * height * 256 * weight,
            bytes_accessed=planes * height * 4 * weight,
            transcendentals=0,
        ),
        name=f"march_{mode}",
    )(*tables, *operands)
    return out[0] if len(out) == 1 else out


def plane_halos(first, last):
    count = lax.axis_size("slab")
    forward = [(i, i + 1) for i in range(count - 1)]
    backward = [(i + 1, i) for i in range(count - 1)]
    return lax.ppermute(last, "slab", forward), lax.ppermute(first, "slab", backward)


def ordered(is_far, own, other):
    near = [jnp.where(is_far, b, a) for a, b in zip(own, other)]
    far = [jnp.where(is_far, a, b) for a, b in zip(own, other)]
    return [near[0] + near[1] * far[0], near[1] * far[1]]


def exchange(parts, own, shift):
    count = lax.axis_size("slab")
    merged, received = [], []
    for change, part in enumerate(parts):
        if change:
            part = lax.ppermute(part, "slab", [(i, i ^ change << shift) for i in range(count)])
            received.append(part)
        merged.append([part[:, :3], part[:, 3:]])
    digit = 0
    while len(merged) > 1:
        is_far = (own >> digit & 1) == 1
        merged = [ordered(is_far, merged[k], merged[k + 1]) for k in range(0, len(merged), 2)]
        digit += 1
    return merged[0], received


def reduce_image(image, parts, slab_index, block_rows):
    slab_count = lax.axis_size("slab")
    levels = slab_count.bit_length() - 1
    if parts is None:
        image = image.reshape((6, slab_count, block_rows, image.shape[-1]))
        image = jnp.swapaxes(image, 0, 1)
    for shift in range(0, levels, 2):
        size = 1 << min(2, levels - shift)
        own = (slab_index >> shift) & (size - 1)
        if parts is None:
            image = image.reshape((-1, size) + image.shape[1:])
            parts = [
                lax.dynamic_index_in_dim(image, own ^ change, 1, keepdims=False)
                for change in range(size)
            ]
        (colour, transmit), received = exchange(parts, own, shift)
        image, parts = jnp.concatenate([colour, transmit], axis=1), None
        first = received if not shift else first
    return (colour[0], 1.0 - transmit[0]), first


def per_device(field, tf_emission, tf_absorption):
    slab_count = lax.axis_size("slab")
    slab_index = lax.axis_index("slab")
    planes, height, width = field.shape
    depth_total = planes * slab_count
    block_rows = height // slab_count
    part_shape = None
    if slab_count >= 4 and block_rows % SUBLANES == 0:
        part_shape = (slab_count // 4, 4, block_rows)
    tables = (tf_emission, tf_absorption)

    core = lax.axis_index("tile")
    halo = plane_halos(field[0], field[-1])
    scale = 0.5 * (tf_emission.shape[1] - 1)
    middle, edge, *tables = march(
        "middle", tables, field, None, None, None, depth_total, scale, None
    )
    edge, _ = lax.optimization_barrier((edge, halo))
    side = lax.ppermute(edge, "tile", [(0, 1), (1, 0)])
    arrived = None
    results = []
    for mode in ("rim", "outer"):
        if arrived is not None:
            halo, side, _ = lax.optimization_barrier((halo, side, out))
        out = march(mode, tables, field, side, halo, middle, depth_total, scale, part_shape)
        if arrived is not None:
            out, _ = lax.optimization_barrier((out, arrived))
        image, parts = (out, None) if part_shape is None else (None, out)
        result, arrived = reduce_image(image, parts, slab_index, block_rows)
        results.append(result)
    first_core = core == 0
    return tuple(
        jnp.where(
            first_core,
            jnp.concatenate([wide, narrow], axis=2),
            jnp.concatenate([narrow, wide], axis=2),
        )
        for wide, narrow in zip(*results)
    )


def solution(mesh):
    placed = (P("slab", None, "tile"), P(), P())
    return jax.shard_map(
        per_device,
        mesh=mesh,
        in_specs=placed,
        out_specs=(P(None, "slab", "tile"), P(None, "slab", "tile")),
        check_vma=False,
    )
```

```python
import functools

import jax
import jax.numpy as jnp
from jax import lax
from jax.experimental import pallas as pl
from jax.experimental.pallas import tpu as pltpu
from jax.sharding import PartitionSpec as P

LIGHT_DIR = (0.2672612, 0.5345225, 0.8017837)
LANES = 128
SUBLANES = 8
PAD = 8
WORD_SCALE = 2.0**31 - 2.0**17
HALF = 65536


def prepare_tables(emission, absorption, depth_total, table, words, factors):
    breaks = emission.shape[1]
    table[...] = jnp.zeros(table.shape, jnp.float32)
    table[0:3, 0:breaks] = emission[...]
    table[3:6, 0:breaks] = absorption[...]
    values = table[...]
    largest = [jnp.maximum(jnp.max(ref[...]), 1e-30) for ref in (emission, absorption)]
    row = lax.broadcasted_iota(jnp.int32, table.shape, 0)
    lane = lax.broadcasted_iota(jnp.int32, table.shape, 1)
    scaled = values * (WORD_SCALE / jnp.where(row < 3, largest[0], largest[1]))
    following = jnp.where(lane < breaks - 1, pltpu.roll(scaled, LANES - 1, 1), scaled)
    rise = jnp.floor((following - scaled) * (1.0 / HALF) + 0.5)
    upper = jnp.floor((0.5 * (following + scaled) - rise) * (1.0 / HALF) + 0.5)
    word = upper.astype(jnp.int32) * HALF + rise.astype(jnp.int32)
    units = [largest[0] / WORD_SCALE, largest[1] * (4.0 / depth_total) / WORD_SCALE]
    constants = [0.9 * part * units[0] for part in LIGHT_DIR]
    constants += [0.1 * units[0], units[1], 0.75 * units[1]]
    for k in range(6):
        words[k] = jnp.broadcast_to(word[k : k + 1, :], (SUBLANES, LANES))
        factors[k] = jnp.full((SUBLANES, LANES), constants[k], jnp.float32)


def lookup(table, index):
    return lax.gather(
        table,
        index.reshape(index.shape + (1,)),
        lax.GatherDimensionNumbers(
            offset_dims=(),
            collapsed_slice_dims=(1,),
            start_index_map=(1,),
            operand_batching_dims=(0,),
            start_indices_batching_dims=(0,),
        ),
        slice_sizes=(1, 1),
        mode=lax.GatherScatterMode.PROMISE_IN_BOUNDS,
    )


def march_kernel(mode, depth_total, group, scale, unroll, pieces, tables_a, tables_b, *refs):
    refs = list(refs)
    field = refs.pop(0)
    side = refs.pop(0) if mode == "outer" else None
    low, high = (refs.pop(0), refs.pop(0)) if mode != "middle" else (None, None)
    rim = mode == "rim"
    middle = refs.pop(0) if rim else None
    inner = refs.pop() if mode != "outer" else None
    cells, canvas, table, in_sems, out_sems = refs[-5:]
    outs = refs[:-5]
    if mode == "middle":
        edge, words, factors = outs[-3:]
        outs = outs[:-3]
    else:
        edge, words, factors = None, tables_a, tables_b
    planes, height, width = field.shape
    piece_rows = height // pieces
    in_pieces = in_sems.shape[0]
    core = lax.axis_index("tile")
    tiles = cells.shape[0] - 2
    computed = range(1, tiles + 1)
    blocks = [(0, 1, 2), (planes - 2, 3, 2)] if rim else [(0, 1, planes)]
    if rim:
        marched = (0, planes - 1)
    else:
        marched = range(1, planes - 1) if mode == "middle" else range(planes)
    place = {first + k: slot + k for first, slot, count in blocks for k in range(count)}
    place[-1] = 0
    place[planes] = max(place.values()) + 1
    far = (1 - core) * (tiles + 1)
    nearer = core if mode == "outer" else 1 - core
    first_lane_taken, first_tile = (1 - nearer) * (width // 2 - LANES), nearer

    def incoming(piece):
        in_rows = height // in_pieces
        start = pl.multiple_of(piece * in_rows, SUBLANES)
        body = pl.ds(start, in_rows)
        padded = pl.ds(start + PAD, in_rows)
        pairs = []
        for k in range(tiles + 1):
            lanes = pl.ds(pl.multiple_of(first_lane_taken + k * LANES, LANES), LANES)
            held = cells.at[first_tile + k]
            for first, where, count in blocks:
                target = held.at[pl.ds(where, count), padded, :]
                pairs.append((field.at[pl.ds(first, count), body, lanes], target))
        if mode != "middle":
            for tile in computed:
                lane = (1 - nearer) * (width // 2) + (tile - 1) * LANES
                lanes = pl.ds(pl.multiple_of(lane, LANES), LANES)
                for halo, plane in ((low, -1), (high, planes)):
                    target = cells.at[tile, place[plane], padded, :]
                    pairs.append((halo.at[body, lanes], target))
        if rim:
            pairs.append((middle.at[:, body, :], inner.at[:, body, :]))
        if mode == "outer":
            pairs.append((side.at[:, body, :], cells.at[far, pl.ds(1, planes), padded, :]))
        return [
            pltpu.make_async_copy(source, target, in_sems.at[piece, k])
            for k, (source, target) in enumerate(pairs)
        ]

    def outgoing(piece):
        start = pl.multiple_of(piece * piece_rows, SUBLANES)
        body = pl.ds(start, piece_rows)
        if len(outs) == 1:
            pairs = [(canvas.at[:, body, :], outs[0].at[:, body, :])]
        else:
            own = lax.axis_index("slab") & (group - 1)
            pairs = [(canvas.at[piece, own ^ k], outs[k].at[piece]) for k in range(group)]
        return [
            pltpu.make_async_copy(source, target, out_sems.at[piece, k])
            for k, (source, target) in enumerate(pairs)
        ]

    def start(piece):
        for copy in incoming(piece):
            copy.start()

    def await_piece(piece):
        for copy in incoming(piece):
            copy.wait()

    start(0)
    if mode == "middle":
        first = pl.multiple_of((1 - core) * (width - LANES), LANES)
        edge_in = pltpu.make_async_copy(
            field.at[:, :, pl.ds(first, LANES)], inner, out_sems.at[0, group]
        )
        edge_out = pltpu.make_async_copy(inner, edge, out_sems.at[1, group])
        edge_in.start()
        prepare_tables(tables_a, tables_b, depth_total, table, words, factors)
    zeros = jnp.zeros((1, LANES), jnp.float32)
    for tile in computed:
        for plane in marched:
            cells[tile, place[plane], pl.ds(PAD - 1, 1), :] = zeros
            cells[tile, place[plane], pl.ds(PAD + height, 1), :] = zeros
    if mode != "outer":
        blank = jnp.zeros((height, LANES), jnp.float32)
        for plane in marched:
            cells[core * (tiles + 1), place[plane], pl.ds(PAD, height), :] = blank

    lane = lax.broadcasted_iota(jnp.int32, (SUBLANES, LANES), 1)
    first_lane = lane == 0
    last_lane = lane == LANES - 1

    def strip(at, tile, piece, number):
        row = pl.multiple_of(piece * piece_rows + number * SUBLANES, SUBLANES)

        def rows(tile, plane, offset=0):
            here = pl.ds(row + PAD + offset, SUBLANES)
            return cells[tile, place[plane], here, :]

        colour = transmit = None
        for plane in marched:
            before, centre, after = (rows(tile, plane + k) for k in (-1, 0, 1))
            left = pltpu.roll(jnp.where(last_lane, rows(tile - 1, plane), centre), 1, 1)
            right = pltpu.roll(jnp.where(first_lane, rows(tile + 1, plane), centre), LANES - 1, 1)
            diff_x = right - left
            diff_y = rows(tile, plane, 1) - rows(tile, plane, -1)
            diff_z = after - before
            inverse = lax.rsqrt(diff_x * diff_x + diff_y * diff_y + diff_z * diff_z + 1.0)
            facing = (factors[0] * diff_x + factors[1] * diff_y + factors[2] * diff_z) * inverse
            shading = jnp.maximum(facing, 0.0) + factors[3]
            weight = factors[4] - factors[5] * (inverse * inverse)
            middle_based = centre * scale + (scale - 0.5)
            interval = (middle_based + 0.5).astype(jnp.int32)
            offset = middle_based - interval.astype(jnp.float32)
            values = []
            for k in range(6):
                word = lookup(words[k], interval)
                rise = lax.shift_left(word, 16).astype(jnp.float32)
                values.append(word.astype(jnp.float32) + rise * offset)
            steps = [values[3 + ch] * weight for ch in range(3)]
            glows = [values[ch] * shading for ch in range(3)]
            if colour is None:
                colour = [step * glow for step, glow in zip(steps, glows)]
                transmit = [1.0 - step for step in steps]
            else:
                seen = [transmit[ch] * steps[ch] for ch in range(3)]
                colour = [colour[ch] + seen[ch] * glows[ch] for ch in range(3)]
                transmit = [transmit[ch] - seen[ch] for ch in range(3)]
            if rim and plane == 0:
                held = [
                    inner[k, pl.ds(row, SUBLANES), pl.ds(at * LANES, LANES)] for k in range(6)
                ]
                colour = [colour[ch] + transmit[ch] * held[ch] for ch in range(3)]
                transmit = [transmit[ch] * held[3 + ch] for ch in range(3)]
        here = pl.ds(at * LANES, LANES)
        for k, value in enumerate(colour + transmit):
            if len(outs) == 1:
                canvas[k, pl.ds(row, SUBLANES), here] = value
            else:
                block_rows = canvas.shape[3]
                block = (number * SUBLANES) // block_rows
                first = pl.multiple_of((number * SUBLANES) % block_rows, SUBLANES)
                canvas[piece, block, k, pl.ds(first, SUBLANES), here] = value

    await_piece(0)

    @pl.loop(0, pieces)
    def _(piece):
        @pl.when(piece + 1 < in_pieces)
        def _():
            start(piece + 1)

        @pl.loop(0, piece_rows // (SUBLANES * unroll))
        def _(step):
            last_step = step == piece_rows // (SUBLANES * unroll) - 1

            @pl.when(last_step & (piece + 1 < in_pieces))
            def _():
                await_piece(piece + 1)

            for k in range(unroll):
                for at, tile in enumerate(computed):
                    strip(at, tile, piece, step * unroll + k)

        for copy in outgoing(piece):
            copy.start()
        if mode == "middle":

            @pl.when(piece == pieces // 2)
            def _():
                edge_in.wait()
                edge_out.start()

    @pl.loop(0, pieces)
    def _(piece):
        for copy in outgoing(piece):
            copy.wait()

    if mode == "middle":
        edge_out.wait()


def march(mode, tables, field, side, halos, middle, depth_total, scale, part_shape):
    planes, height, width = field.shape
    rim = mode == "rim"
    tiles = width // LANES // 2
    tiles_held, extent = tiles + 2, tiles * LANES
    held = 6 if rim else planes + 2
    if part_shape is None:
        group, pieces = 1, max(1, height // (32 if mode == "middle" else 64))
        outs = [jax.ShapeDtypeStruct((6, height, extent), jnp.float32)]
        canvas = (6, height, extent)
    else:
        pieces, group, rows = part_shape
        outs = [jax.ShapeDtypeStruct((pieces, 6, rows, extent), jnp.float32)] * group
        canvas = (pieces, group, 6, rows, extent)
    scratch = [
        pltpu.VMEM((tiles_held, held, height + 2 * PAD, LANES), jnp.float32),
        pltpu.VMEM(canvas, jnp.float32),
        pltpu.VMEM((SUBLANES, LANES), jnp.float32),
        pltpu.SemaphoreType.DMA((1 if rim else pieces, 4 * tiles_held + 2)),
        pltpu.SemaphoreType.DMA((pieces, group + 1)),
    ]
    operands = [field]
    if mode == "outer":
        operands.append(side)
    if mode != "middle":
        operands += list(halos)
    if rim:
        operands.append(middle)
        scratch.append(pltpu.VMEM((6, height, extent), jnp.float32))
    if mode == "middle":
        scratch.append(pltpu.VMEM((planes, height, LANES), jnp.float32))
    near = pl.BlockSpec(memory_space=pltpu.VMEM)
    out_specs = [pl.BlockSpec(memory_space=pl.ANY)] * len(outs)
    if mode == "middle":
        outs.append(jax.ShapeDtypeStruct((planes, height, LANES), jnp.float32))
        outs.append(jax.ShapeDtypeStruct((6, SUBLANES, LANES), jnp.int32))
        outs.append(jax.ShapeDtypeStruct((6, SUBLANES, LANES), jnp.float32))
        out_specs += [pl.BlockSpec(memory_space=pl.ANY), near, near]
    strips = height // pieces // SUBLANES
    unroll = min(strips, {"rim": 8, "outer": 8, "middle": 2}[mode])
    weight = 20000 if mode == "outer" else 0
    distant = pl.BlockSpec(memory_space=pl.ANY)
    out = pl.pallas_call(
        functools.partial(march_kernel, mode, depth_total, group, scale, unroll, pieces),
        out_shape=outs,
        in_specs=[near] * 2 + [distant] * len(operands),
        out_specs=out_specs,
        scratch_shapes=scratch,
        compiler_params=pltpu.CompilerParams(vmem_limit_bytes=44 * 1024 * 1024),
        cost_estimate=pl.CostEstimate(
            flops=planes * height * 256 * weight,
            bytes_accessed=planes * height * 4 * weight,
            transcendentals=0,
        ),
        name=f"march_{mode}",
    )(*tables, *operands)
    return out[0] if len(out) == 1 else out


def plane_halos(first, last):
    count = lax.axis_size("slab")
    forward = [(i, i + 1) for i in range(count - 1)]
    backward = [(i + 1, i) for i in range(count - 1)]
    return lax.ppermute(last, "slab", forward), lax.ppermute(first, "slab", backward)


def ordered(is_far, own, other):
    near = [jnp.where(is_far, b, a) for a, b in zip(own, other)]
    far = [jnp.where(is_far, a, b) for a, b in zip(own, other)]
    return [near[0] + near[1] * far[0], near[1] * far[1]]


def exchange(parts, own, shift):
    count = lax.axis_size("slab")
    merged, received = [], []
    for change, part in enumerate(parts):
        if change:
            part = lax.ppermute(part, "slab", [(i, i ^ change << shift) for i in range(count)])
            received.append(part)
        merged.append([part[:, :3], part[:, 3:]])
    digit = 0
    while len(merged) > 1:
        is_far = (own >> digit & 1) == 1
        merged = [ordered(is_far, merged[k], merged[k + 1]) for k in range(0, len(merged), 2)]
        digit += 1
    return merged[0], received


def reduce_image(image, parts, slab_index, block_rows):
    slab_count = lax.axis_size("slab")
    levels = slab_count.bit_length() - 1
    if parts is None:
        image = image.reshape((6, slab_count, block_rows, image.shape[-1]))
        image = jnp.swapaxes(image, 0, 1)
    for shift in range(0, levels, 2):
        size = 1 << min(2, levels - shift)
        own = (slab_index >> shift) & (size - 1)
        if parts is None:
            image = image.reshape((-1, size) + image.shape[1:])
            parts = [
                lax.dynamic_index_in_dim(image, own ^ change, 1, keepdims=False)
                for change in range(size)
            ]
        (colour, transmit), received = exchange(parts, own, shift)
        image, parts = jnp.concatenate([colour, transmit], axis=1), None
        first = received if not shift else first
    return (colour[0], 1.0 - transmit[0]), first


def per_device(field, tf_emission, tf_absorption):
    slab_count = lax.axis_size("slab")
    slab_index = lax.axis_index("slab")
    planes, height, width = field.shape
    depth_total = planes * slab_count
    block_rows = height // slab_count
    part_shape = None
    if slab_count >= 4 and block_rows % SUBLANES == 0:
        part_shape = (slab_count // 4, 4, block_rows)
    tables = (tf_emission, tf_absorption)

    core = lax.axis_index("tile")
    halo = plane_halos(field[0], field[-1])
    scale = 0.5 * (tf_emission.shape[1] - 1)
    middle, edge, *tables = march(
        "middle", tables, field, None, None, None, depth_total, scale, None
    )
    edge, _ = lax.optimization_barrier((edge, halo))
    side = lax.ppermute(edge, "tile", [(0, 1), (1, 0)])
    arrived = None
    results = []
    for mode in ("rim", "outer"):
        if arrived is not None:
            halo, side, _ = lax.optimization_barrier((halo, side, out))
        out = march(mode, tables, field, side, halo, middle, depth_total, scale, part_shape)
        if arrived is not None:
            out, _ = lax.optimization_barrier((out, arrived))
        image, parts = (out, None) if part_shape is None else (None, out)
        result, arrived = reduce_image(image, parts, slab_index, block_rows)
        results.append(result)
    first_core = core == 0
    return tuple(
        jnp.where(
            first_core,
            jnp.concatenate([wide, narrow], axis=2),
            jnp.concatenate([narrow, wide], axis=2),
        )
        for wide, narrow in zip(*results)
    )


def solution(mesh):
    placed = (P("slab", None, "tile"), P(), P())
    return jax.shard_map(
        per_device,
        mesh=mesh,
        in_specs=placed,
        out_specs=(P(None, "slab", "tile"), P(None, "slab", "tile")),
        check_vma=False,
    )
```

```python
import functools

import jax
import jax.numpy as jnp
from jax import lax
from jax.experimental import pallas as pl
from jax.experimental.pallas import tpu as pltpu
from jax.sharding import PartitionSpec as P

LIGHT_DIR = (0.2672612, 0.5345225, 0.8017837)
LANES = 128
SUBLANES = 8
PAD = 8
WORD_SCALE = 2.0**31 - 2.0**17
HALF = 65536


def prepare_tables(emission, absorption, depth_total, table, words, factors):
    breaks = emission.shape[1]
    table[...] = jnp.zeros(table.shape, jnp.float32)
    table[0:3, 0:breaks] = emission[...]
    table[3:6, 0:breaks] = absorption[...]
    values = table[...]
    largest = [jnp.maximum(jnp.max(ref[...]), 1e-30) for ref in (emission, absorption)]
    row = lax.broadcasted_iota(jnp.int32, table.shape, 0)
    lane = lax.broadcasted_iota(jnp.int32, table.shape, 1)
    scaled = values * (WORD_SCALE / jnp.where(row < 3, largest[0], largest[1]))
    following = jnp.where(lane < breaks - 1, pltpu.roll(scaled, LANES - 1, 1), scaled)
    rise = jnp.floor((following - scaled) * (1.0 / HALF) + 0.5)
    upper = jnp.floor((0.5 * (following + scaled) - rise) * (1.0 / HALF) + 0.5)
    word = upper.astype(jnp.int32) * HALF + rise.astype(jnp.int32)
    units = [largest[0] / WORD_SCALE, largest[1] * (4.0 / depth_total) / WORD_SCALE]
    constants = [0.9 * part * units[0] for part in LIGHT_DIR]
    constants += [0.1 * units[0], units[1], 0.75 * units[1]]
    for k in range(6):
        words[k] = jnp.broadcast_to(word[k : k + 1, :], (SUBLANES, LANES))
        factors[k] = jnp.full((SUBLANES, LANES), constants[k], jnp.float32)


def lookup(table, index):
    return lax.gather(
        table,
        index.reshape(index.shape + (1,)),
        lax.GatherDimensionNumbers(
            offset_dims=(),
            collapsed_slice_dims=(1,),
            start_index_map=(1,),
            operand_batching_dims=(0,),
            start_indices_batching_dims=(0,),
        ),
        slice_sizes=(1, 1),
        mode=lax.GatherScatterMode.PROMISE_IN_BOUNDS,
    )


def march_kernel(mode, depth_total, group, scale, unroll, pieces, tables_a, tables_b, *refs):
    refs = list(refs)
    field = refs.pop(0)
    side = refs.pop(0) if mode == "outer" else None
    low, high = (refs.pop(0), refs.pop(0)) if mode != "middle" else (None, None)
    rim = mode == "rim"
    middle = refs.pop(0) if rim else None
    inner = refs.pop() if mode != "outer" else None
    cells, canvas, table, in_sems, out_sems = refs[-5:]
    outs = refs[:-5]
    if mode == "middle":
        edge, words, factors = outs[-3:]
        outs = outs[:-3]
    else:
        edge, words, factors = None, tables_a, tables_b
    planes, height, width = field.shape
    piece_rows = height // pieces
    in_pieces = in_sems.shape[0]
    core = lax.axis_index("tile")
    tiles = cells.shape[0] - 2
    computed = range(1, tiles + 1)
    blocks = [(0, 1, 2), (planes - 2, 3, 2)] if rim else [(0, 1, planes)]
    if rim:
        marched = (0, planes - 1)
    else:
        marched = range(1, planes - 1) if mode == "middle" else range(planes)
    place = {first + k: slot + k for first, slot, count in blocks for k in range(count)}
    place[-1] = 0
    place[planes] = max(place.values()) + 1
    far = (1 - core) * (tiles + 1)
    nearer = core if mode == "outer" else 1 - core
    first_lane_taken, first_tile = (1 - nearer) * (width // 2 - LANES), nearer

    def incoming(piece):
        in_rows = height // in_pieces
        start = pl.multiple_of(piece * in_rows, SUBLANES)
        body = pl.ds(start, in_rows)
        padded = pl.ds(start + PAD, in_rows)
        pairs = []
        for k in range(tiles + 1):
            lanes = pl.ds(pl.multiple_of(first_lane_taken + k * LANES, LANES), LANES)
            held = cells.at[first_tile + k]
            for first, where, count in blocks:
                target = held.at[pl.ds(where, count), padded, :]
                pairs.append((field.at[pl.ds(first, count), body, lanes], target))
        if mode != "middle":
            for tile in computed:
                lane = (1 - nearer) * (width // 2) + (tile - 1) * LANES
                lanes = pl.ds(pl.multiple_of(lane, LANES), LANES)
                for halo, plane in ((low, -1), (high, planes)):
                    target = cells.at[tile, place[plane], padded, :]
                    pairs.append((halo.at[body, lanes], target))
        if rim:
            pairs.append((middle.at[:, body, :], inner.at[:, body, :]))
        if mode == "outer":
            pairs.append((side.at[:, body, :], cells.at[far, pl.ds(1, planes), padded, :]))
        return [
            pltpu.make_async_copy(source, target, in_sems.at[piece, k])
            for k, (source, target) in enumerate(pairs)
        ]

    def outgoing(piece):
        start = pl.multiple_of(piece * piece_rows, SUBLANES)
        body = pl.ds(start, piece_rows)
        if len(outs) == 1:
            pairs = [(canvas.at[:, body, :], outs[0].at[:, body, :])]
        else:
            own = lax.axis_index("slab") & (group - 1)
            pairs = [(canvas.at[piece, own ^ k], outs[k].at[piece]) for k in range(group)]
        return [
            pltpu.make_async_copy(source, target, out_sems.at[piece, k])
            for k, (source, target) in enumerate(pairs)
        ]

    def start(piece):
        for copy in incoming(piece):
            copy.start()

    def await_piece(piece):
        for copy in incoming(piece):
            copy.wait()

    for piece in range(in_pieces):
        start(piece)
    if mode == "middle":
        first = pl.multiple_of((1 - core) * (width - LANES), LANES)
        edge_in = pltpu.make_async_copy(
            field.at[:, :, pl.ds(first, LANES)], inner, out_sems.at[0, group]
        )
        edge_out = pltpu.make_async_copy(inner, edge, out_sems.at[1, group])
        edge_in.start()
        prepare_tables(tables_a, tables_b, depth_total, table, words, factors)
    zeros = jnp.zeros((1, LANES), jnp.float32)
    for tile in computed:
        for plane in marched:
            cells[tile, place[plane], pl.ds(PAD - 1, 1), :] = zeros
            cells[tile, place[plane], pl.ds(PAD + height, 1), :] = zeros
    if mode != "outer":
        blank = jnp.zeros((height, LANES), jnp.float32)
        for plane in marched:
            cells[core * (tiles + 1), place[plane], pl.ds(PAD, height), :] = blank

    lane = lax.broadcasted_iota(jnp.int32, (SUBLANES, LANES), 1)
    first_lane = lane == 0
    last_lane = lane == LANES - 1

    def strip(at, tile, piece, number):
        row = pl.multiple_of(piece * piece_rows + number * SUBLANES, SUBLANES)

        def rows(tile, plane, offset=0):
            here = pl.ds(row + PAD + offset, SUBLANES)
            return cells[tile, place[plane], here, :]

        colour = transmit = None
        for plane in marched:
            before, centre, after = (rows(tile, plane + k) for k in (-1, 0, 1))
            left = pltpu.roll(jnp.where(last_lane, rows(tile - 1, plane), centre), 1, 1)
            right = pltpu.roll(jnp.where(first_lane, rows(tile + 1, plane), centre), LANES - 1, 1)
            diff_x = right - left
            diff_y = rows(tile, plane, 1) - rows(tile, plane, -1)
            diff_z = after - before
            inverse = lax.rsqrt(diff_x * diff_x + diff_y * diff_y + diff_z * diff_z + 1.0)
            facing = (factors[0] * diff_x + factors[1] * diff_y + factors[2] * diff_z) * inverse
            shading = jnp.maximum(facing, 0.0) + factors[3]
            weight = factors[4] - factors[5] * (inverse * inverse)
            middle_based = centre * scale + (scale - 0.5)
            interval = (middle_based + 0.5).astype(jnp.int32)
            offset = middle_based - interval.astype(jnp.float32)
            values = []
            for k in range(6):
                word = lookup(words[k], interval)
                rise = lax.shift_left(word, 16).astype(jnp.float32)
                values.append(word.astype(jnp.float32) + rise * offset)
            steps = [values[3 + ch] * weight for ch in range(3)]
            glows = [values[ch] * shading for ch in range(3)]
            if colour is None:
                colour = [step * glow for step, glow in zip(steps, glows)]
                transmit = [1.0 - step for step in steps]
            else:
                seen = [transmit[ch] * steps[ch] for ch in range(3)]
                colour = [colour[ch] + seen[ch] * glows[ch] for ch in range(3)]
                transmit = [transmit[ch] - seen[ch] for ch in range(3)]
            if rim and plane == 0:
                held = [
                    inner[k, pl.ds(row, SUBLANES), pl.ds(at * LANES, LANES)] for k in range(6)
                ]
                colour = [colour[ch] + transmit[ch] * held[ch] for ch in range(3)]
                transmit = [transmit[ch] * held[3 + ch] for ch in range(3)]
        here = pl.ds(at * LANES, LANES)
        for k, value in enumerate(colour + transmit):
            if len(outs) == 1:
                canvas[k, pl.ds(row, SUBLANES), here] = value
            else:
                block_rows = canvas.shape[3]
                block = (number * SUBLANES) // block_rows
                first = pl.multiple_of((number * SUBLANES) % block_rows, SUBLANES)
                canvas[piece, block, k, pl.ds(first, SUBLANES), here] = value

    await_piece(0)

    @pl.loop(0, pieces)
    def _(piece):
        @pl.loop(0, piece_rows // (SUBLANES * unroll))
        def _(step):
            last_step = step == piece_rows // (SUBLANES * unroll) - 1

            @pl.when(last_step & (piece + 1 < in_pieces))
            def _():
                await_piece(piece + 1)

            for k in range(unroll):
                for at, tile in enumerate(computed):
                    strip(at, tile, piece, step * unroll + k)

        for copy in outgoing(piece):
            copy.start()
        if mode == "middle":

            @pl.when(piece == pieces // 2)
            def _():
                edge_in.wait()
                edge_out.start()

    @pl.loop(0, pieces)
    def _(piece):
        for copy in outgoing(piece):
            copy.wait()

    if mode == "middle":
        edge_out.wait()


def march(mode, tables, field, side, halos, middle, depth_total, scale, part_shape):
    planes, height, width = field.shape
    rim = mode == "rim"
    tiles = width // LANES // 2
    tiles_held, extent = tiles + 2, tiles * LANES
    held = 6 if rim else planes + 2
    if part_shape is None:
        group, pieces = 1, max(1, height // (32 if mode == "middle" else 64))
        outs = [jax.ShapeDtypeStruct((6, height, extent), jnp.float32)]
        canvas = (6, height, extent)
    else:
        pieces, group, rows = part_shape
        outs = [jax.ShapeDtypeStruct((pieces, 6, rows, extent), jnp.float32)] * group
        canvas = (pieces, group, 6, rows, extent)
    scratch = [
        pltpu.VMEM((tiles_held, held, height + 2 * PAD, LANES), jnp.float32),
        pltpu.VMEM(canvas, jnp.float32),
        pltpu.VMEM((SUBLANES, LANES), jnp.float32),
        pltpu.SemaphoreType.DMA((1 if rim else pieces, 4 * tiles_held + 2)),
        pltpu.SemaphoreType.DMA((pieces, group + 1)),
    ]
    operands = [field]
    if mode == "outer":
        operands.append(side)
    if mode != "middle":
        operands += list(halos)
    if rim:
        operands.append(middle)
        scratch.append(pltpu.VMEM((6, height, extent), jnp.float32))
    if mode == "middle":
        scratch.append(pltpu.VMEM((planes, height, LANES), jnp.float32))
    near = pl.BlockSpec(memory_space=pltpu.VMEM)
    out_specs = [pl.BlockSpec(memory_space=pl.ANY)] * len(outs)
    if mode == "middle":
        outs.append(jax.ShapeDtypeStruct((planes, height, LANES), jnp.float32))
        outs.append(jax.ShapeDtypeStruct((6, SUBLANES, LANES), jnp.int32))
        outs.append(jax.ShapeDtypeStruct((6, SUBLANES, LANES), jnp.float32))
        out_specs += [pl.BlockSpec(memory_space=pl.ANY), near, near]
    strips = height // pieces // SUBLANES
    unroll = min(strips, {"rim": 8, "outer": 4, "middle": 2}[mode])
    weight = 20000 if mode == "outer" else 0
    distant = pl.BlockSpec(memory_space=pl.ANY)
    out = pl.pallas_call(
        functools.partial(march_kernel, mode, depth_total, group, scale, unroll, pieces),
        out_shape=outs,
        in_specs=[near] * 2 + [distant] * len(operands),
        out_specs=out_specs,
        scratch_shapes=scratch,
        compiler_params=pltpu.CompilerParams(vmem_limit_bytes=44 * 1024 * 1024),
        cost_estimate=pl.CostEstimate(
            flops=planes * height * 256 * weight,
            bytes_accessed=planes * height * 4 * weight,
            transcendentals=0,
        ),
        name=f"march_{mode}",
    )(*tables, *operands)
    return out[0] if len(out) == 1 else out


def plane_halos(first, last):
    count = lax.axis_size("slab")
    forward = [(i, i + 1) for i in range(count - 1)]
    backward = [(i + 1, i) for i in range(count - 1)]
    return lax.ppermute(last, "slab", forward), lax.ppermute(first, "slab", backward)


def ordered(is_far, own, other):
    near = [jnp.where(is_far, b, a) for a, b in zip(own, other)]
    far = [jnp.where(is_far, a, b) for a, b in zip(own, other)]
    return [near[0] + near[1] * far[0], near[1] * far[1]]


def exchange(parts, own, shift):
    count = lax.axis_size("slab")
    merged, received = [], []
    for change, part in enumerate(parts):
        if change:
            part = lax.ppermute(part, "slab", [(i, i ^ change << shift) for i in range(count)])
            received.append(part)
        merged.append([part[:, :3], part[:, 3:]])
    digit = 0
    while len(merged) > 1:
        is_far = (own >> digit & 1) == 1
        merged = [ordered(is_far, merged[k], merged[k + 1]) for k in range(0, len(merged), 2)]
        digit += 1
    return merged[0], received


def reduce_image(image, parts, slab_index, block_rows):
    slab_count = lax.axis_size("slab")
    levels = slab_count.bit_length() - 1
    if parts is None:
        image = image.reshape((6, slab_count, block_rows, image.shape[-1]))
        image = jnp.swapaxes(image, 0, 1)
    for shift in range(0, levels, 2):
        size = 1 << min(2, levels - shift)
        own = (slab_index >> shift) & (size - 1)
        if parts is None:
            image = image.reshape((-1, size) + image.shape[1:])
            parts = [
                lax.dynamic_index_in_dim(image, own ^ change, 1, keepdims=False)
                for change in range(size)
            ]
        (colour, transmit), received = exchange(parts, own, shift)
        image, parts = jnp.concatenate([colour, transmit], axis=1), None
        first = received if not shift else first
    return (colour[0], 1.0 - transmit[0]), first


def per_device(field, tf_emission, tf_absorption):
    slab_count = lax.axis_size("slab")
    slab_index = lax.axis_index("slab")
    planes, height, width = field.shape
    depth_total = planes * slab_count
    block_rows = height // slab_count
    part_shape = None
    if slab_count >= 4 and block_rows % SUBLANES == 0:
        part_shape = (slab_count // 4, 4, block_rows)
    tables = (tf_emission, tf_absorption)

    core = lax.axis_index("tile")
    halo = plane_halos(field[0], field[-1])
    scale = 0.5 * (tf_emission.shape[1] - 1)
    middle, edge, *tables = march(
        "middle", tables, field, None, None, None, depth_total, scale, None
    )
    edge, _ = lax.optimization_barrier((edge, halo))
    side = lax.ppermute(edge, "tile", [(0, 1), (1, 0)])
    arrived = None
    results = []
    for mode in ("rim", "outer"):
        if arrived is not None:
            halo, side, _ = lax.optimization_barrier((halo, side, out))
        out = march(mode, tables, field, side, halo, middle, depth_total, scale, part_shape)
        if arrived is not None:
            out, _ = lax.optimization_barrier((out, arrived))
        image, parts = (out, None) if part_shape is None else (None, out)
        result, arrived = reduce_image(image, parts, slab_index, block_rows)
        results.append(result)
    first_core = core == 0
    return tuple(
        jnp.where(
            first_core,
            jnp.concatenate([wide, narrow], axis=2),
            jnp.concatenate([narrow, wide], axis=2),
        )
        for wide, narrow in zip(*results)
    )


def solution(mesh):
    placed = (P("slab", None, "tile"), P(), P())
    return jax.shard_map(
        per_device,
        mesh=mesh,
        in_specs=placed,
        out_specs=(P(None, "slab", "tile"), P(None, "slab", "tile")),
        check_vma=False,
    )
```
